32 devices in a mesh: fsdp: 4 (over z), seq: 8 (over y, x, core).
Axes of the slice: x: 2, y: 2, z: 4, core: 2. Of those that a mesh axis runs over, the one named last changes fastest.
Arguments:
- tokens: bfloat16 [12288, 1024], P(('fsdp', 'seq')), may hold values from -6 to 6
- cotangent: bfloat16 [12288, 1024], P(('fsdp', 'seq')), may hold values from -6 to 6
- doc_starts: int32 [4, 4], P('fsdp'), may hold values from 0 to 3071, as said below
- gain_one: bfloat16 [1024], P(('fsdp', 'seq')), may hold values from 0.5 to 1.5
- w_query: bfloat16 [1024, 1024], P(('fsdp', 'seq')), may hold values from -1 to 1
- w_key: bfloat16 [1024, 1024], P(('fsdp', 'seq')), may hold values from -1 to 1
- w_value: bfloat16 [1024, 1024], P(('fsdp', 'seq')), may hold values from -0.1875 to 0.1875
- w_swish: bfloat16 [1024, 1024], P(('fsdp', 'seq')), may hold values from -0.1875 to 0.1875
- w_rank_in: bfloat16 [1024, 16], P(('fsdp', 'seq')), may hold values from -0.1875 to 0.1875
- w_rank_out: bfloat16 [16, 1024], P(None, ('fsdp', 'seq')), may hold values from -1.5 to 1.5
- gate_bias: bfloat16 [1024], P(('fsdp', 'seq')), may hold values from -1 to 9
- head_gain: bfloat16 [256], P(('fsdp', 'seq')), may hold values from 0.5 to 1.5
- w_output: bfloat16 [1024, 1024], P(('fsdp', 'seq')), may hold values from -0.375 to 0.375
- gain_two: bfloat16 [1024], P(('fsdp', 'seq')), may hold values from 0.5 to 1.5
- w_gate: bfloat16 [1024, 2816], P(('fsdp', 'seq')), may hold values from -0.1875 to 0.1875
- w_up: bfloat16 [1024, 2816], P(('fsdp', 'seq')), may hold values from -0.1875 to 0.1875
- w_down: bfloat16 [2816, 1024], P(('fsdp', 'seq')), may hold values from -0.21875 to 0.21875
Outputs:
- output: bfloat16 [12288, 1024], P(('fsdp', 'seq'))
- input_grad: float32 [12288, 1024], P(('fsdp', 'seq'))
- grad_gain_one: float32 [1024], P(('fsdp', 'seq'))
- grad_w_query: float32 [1024, 1024], P(('fsdp', 'seq'))
- grad_w_key: float32 [1024, 1024], P(('fsdp', 'seq'))
- grad_w_value: float32 [1024, 1024], P(('fsdp', 'seq'))
- grad_w_swish: float32 [1024, 1024], P(('fsdp', 'seq'))
- grad_w_rank_in: float32 [1024, 16], P(('fsdp', 'seq'))
- grad_w_rank_out: float32 [16, 1024], P(None, ('fsdp', 'seq'))
- grad_gate_bias: float32 [1024], P(('fsdp', 'seq'))
- grad_head_gain: float32 [256], P(('fsdp', 'seq'))
- grad_w_output: float32 [1024, 1024], P(('fsdp', 'seq'))
- grad_gain_two: float32 [1024], P(('fsdp', 'seq'))
- grad_w_gate: float32 [1024, 2816], P(('fsdp', 'seq'))
- grad_w_up: float32 [1024, 2816], P(('fsdp', 'seq'))
- grad_w_down: float32 [2816, 1024], P(('fsdp', 'seq'))
The draws below stay inside these ranges and needn't reach their ends.
Inputs may be any that keep to these rules, and one draw needn't show every extreme that they name: `doc_starts`: each row holds 4 increasing positions: the first is 0, the second lies among the first 384 positions, the third and fourth among the last 384 positions of the sequence; in some row the fourth is the sequence's last position.
All inputs are finite; a program needn't handle non-finite values.
Results may differ from the reference program's by a relative error of at most 0.029.
Values may be sent and summed in bfloat16 or wider, within the bound.
No kernel may reach another device: no remote copies, remote signals or barrier semaphores. Data moves between devices by JAX's collectives and lax.ppermute only.
A program may use at most 256 MiB of HBM per device.

```python
import jax
import jax.numpy as jnp
from jax import lax

D = 1024
HEADS = 4
HEAD_K = 256
HEAD_V = 256
RANK = 16
FF = 2816
GROUP = 64
TOK_DEV = 384
LENGTH = 3072
SEQS = 4
TOKENS = 12288


def shared_projection(key):
    return jax.random.normal(key, (D, HEADS * HEAD_K), jnp.float32) * D ** (-0.5)


def draw_w_query(key, part):
    common = shared_projection(key)
    key = jax.random.fold_in(key, 21)
    own_part = jax.random.normal(key, (D, HEADS * HEAD_K), jnp.float32) * D ** (-0.5)
    return (0.8 * common + 0.6 * own_part).astype(jnp.bfloat16)


def draw_w_key(key, part):
    common = shared_projection(key)
    key = jax.random.fold_in(key, 22)
    own_part = jax.random.normal(key, (D, HEADS * HEAD_K), jnp.float32) * D ** (-0.5)
    return (0.8 * common + 0.6 * own_part).astype(jnp.bfloat16)


def draw_doc_starts(key, part):
    key = jax.random.fold_in(key, 11)
    subkeys = jax.random.split(key, 4)
    second_start = jax.random.randint(subkeys[0], (SEQS,), 1, TOK_DEV)
    third_start = jax.random.randint(subkeys[1], (SEQS,), LENGTH - TOK_DEV + 1, LENGTH - 1)
    offset = jax.random.randint(subkeys[2], (SEQS,), 0, 1 << 20)
    fourth_start = third_start + 1 + offset % (LENGTH - 1 - third_start)
    chosen_row = jax.random.randint(subkeys[3], (), 0, SEQS)
    row_ids = jnp.arange(SEQS, dtype=jnp.int32)
    fourth_start = jnp.where(row_ids == chosen_row, LENGTH - 1, fourth_start)
    zero_start = jnp.zeros((SEQS,), jnp.int32)
    return jnp.stack([zero_start, second_start, third_start, fourth_start], axis=1).astype(jnp.int32)


def steps_of(rng, dims, cuts, low, top_value):
    level, own = 1.0, jax.random.fold_in(rng, 6)
    for position, shards_of in cuts:
        steps = jnp.exp(jax.random.uniform(jax.random.fold_in(own, position), (shards_of,), jnp.float32, low / len(cuts), top_value / len(cuts)))
        level = level * jnp.repeat(steps, dims[position] // shards_of).reshape([-1 if axis == position else 1 for axis in range(len(dims))])
    return level


def bell_draw(rng, shape, width, limit, cuts=(), kind=jnp.bfloat16):
    values = width * jax.random.normal(rng, shape, jnp.float32)
    if cuts:
        values = values * steps_of(rng, shape, cuts, -0.22, 0.18)
    return jnp.clip(values, -limit, limit).astype(kind)


def setup_inputs(seed: int = 0) -> dict:
    streams_of = jax.random.split(jax.random.key(seed), 18)
    tokens = bell_draw(streams_of[0], (TOKENS, D), 1.0, 6.0, ((0, 32),))
    cotangent = bell_draw(streams_of[1], (TOKENS, D), 1.0, 6.0, ((0, 32),))
    doc_starts = draw_doc_starts(jax.random.fold_in(streams_of[17], 71), 0)
    gain_one = jnp.clip(1.0 + 0.1 * jax.random.normal(streams_of[3], (D,), jnp.float32), 0.5, 1.5).astype(jnp.bfloat16)
    w_query = draw_w_query(jax.random.fold_in(streams_of[17], 71), 0)
    w_key = draw_w_key(jax.random.fold_in(streams_of[17], 71), 0)
    w_value = bell_draw(streams_of[6], (D, HEADS * HEAD_V), D ** -0.5, 0.1875, ((0, 32),))
    w_swish = bell_draw(streams_of[7], (D, HEADS * HEAD_V), D ** -0.5, 0.1875, ((0, 32),))
    w_rank_in = bell_draw(streams_of[8], (D, RANK), D ** -0.5, 0.1875, ((0, 32),))
    w_rank_out = bell_draw(streams_of[9], (RANK, HEADS * HEAD_K), RANK ** -0.5, 1.5, ((1, 32),))
    gate_bias = jnp.clip(-1.0 + 10.0 * jax.random.uniform(streams_of[10], (HEADS * HEAD_K,), jnp.float32) ** steps_of(streams_of[10], (HEADS * HEAD_K,), ((0, 32),), -0.2, 0.2), -1.0, 9.0).astype(jnp.bfloat16)
    head_gain = jnp.clip(1.0 + 0.1 * jax.random.normal(streams_of[11], (HEAD_V,), jnp.float32), 0.5, 1.5).astype(jnp.bfloat16)
    w_output = bell_draw(streams_of[12], (HEADS * HEAD_V, D), (HEADS * HEAD_V // 4) ** -0.5, 0.375, ((0, 32),))
    gain_two = jnp.clip(1.0 + 0.1 * jax.random.normal(streams_of[13], (D,), jnp.float32), 0.5, 1.5).astype(jnp.bfloat16)
    w_gate = bell_draw(streams_of[14], (D, FF), D ** -0.5, 0.1875, ((0, 32),))
    w_up = bell_draw(streams_of[15], (D, FF), D ** -0.5, 0.1875, ((0, 32),))
    w_down = bell_draw(streams_of[16], (FF, D), (FF // 4) ** -0.5, 0.21875, ((0, 32),))
    return {"tokens": tokens, "cotangent": cotangent, "doc_starts": doc_starts, "gain_one": gain_one, "w_query": w_query, "w_key": w_key, "w_value": w_value, "w_swish": w_swish, "w_rank_in": w_rank_in, "w_rank_out": w_rank_out, "gate_bias": gate_bias, "head_gain": head_gain, "w_output": w_output, "gain_two": gain_two, "w_gate": w_gate, "w_up": w_up, "w_down": w_down}


MAXIMUM_ACCURACY = lax.Precision.HIGHEST

@jax.custom_vjp
def low(v):
    return lax.optimization_barrier(v.astype(jnp.bfloat16)).astype(jnp.float32)

@jax.custom_vjp
def low_back(v):
    return v

def low_keep(v):
    return (low(v), None)

def low_pass(kept, grad):
    return (grad,)

def back_keep(v):
    return (v, None)

def back_low(kept, grad):
    return (low(grad),)
low.defvjp(low_keep, low_pass)
low_back.defvjp(back_keep, back_low)

def norm_rows(values, scales, epsilon):
    return values * lax.rsqrt(lax.optimization_barrier(jnp.mean(values * values, axis=-1, keepdims=True)) + epsilon) * scales

def heads_of(tensor, head_width):
    return tensor.reshape(tensor.shape[0], -1, head_width)

def document_of(positions, starts):
    return lax.optimization_barrier(jnp.sum((starts[None, :] <= positions[:, None]).astype(jnp.int32), axis=1)) - 1

def group_step(passed_state, pieces):
    queries, key_rows, value_matrix, decays, doc_ids, prev_doc = pieces
    running_total = jnp.cumsum(decays, axis=0)
    query_entering = queries * jnp.exp(running_total)
    key_in = key_rows * jnp.exp(-running_total)
    scores = jnp.einsum('thk,shk->hts', query_entering, key_in, precision=MAXIMUM_ACCURACY)
    indices = jnp.arange(doc_ids.shape[0], dtype=jnp.int32)
    allowed = (doc_ids[:, None] == doc_ids[None, :]) & (indices[:, None] >= indices[None, :])
    scores = jnp.where(allowed[None], scores, 0.0)
    within = jnp.einsum('hts,shv->thv', scores, value_matrix, precision=MAXIMUM_ACCURACY)
    entering = (doc_ids == prev_doc).astype(queries.dtype)
    carried_over = jnp.einsum('wiu,iug->wig', query_entering, passed_state, precision=MAXIMUM_ACCURACY)
    outputs = within + entering[:, None, None] * carried_over
    closing_sum = running_total[-1]
    tail_rows = (doc_ids == doc_ids[-1]).astype(queries.dtype)
    key_finish = key_rows * jnp.exp(closing_sum[None] - running_total) * tail_rows[:, None, None]
    retained_state = (doc_ids[-1] == prev_doc).astype(queries.dtype)
    updated_state = retained_state * jnp.exp(closing_sum)[:, :, None] * passed_state + jnp.einsum('yaq,yap->aqp', key_finish, value_matrix, precision=MAXIMUM_ACCURACY)
    return (updated_state, outputs)

def mix_sequence(queries, key_rows, value_matrix, decays, starts):
    positions = jnp.arange(LENGTH, dtype=jnp.int32)
    doc_ids = document_of(positions, starts)
    prev_ids = document_of(positions - 1, starts)
    blocks = LENGTH // GROUP

    def split_blocks(tensor):
        return tensor.reshape((blocks, GROUP) + tensor.shape[1:])
    start_state = jnp.zeros((HEADS, HEAD_K, HEAD_V), queries.dtype)
    _, outputs = lax.scan(jax.checkpoint(group_step), start_state, (split_blocks(queries), split_blocks(key_rows), split_blocks(value_matrix), split_blocks(decays), split_blocks(doc_ids), split_blocks(prev_ids)[:, 0]))
    return outputs.reshape(LENGTH, HEADS, HEAD_V)

def block_layer(inputs, starts, weights):
    gain_one, w_query, w_key, w_value, w_swish, w_rank_in, w_rank_out, gate_bias, head_gain, w_output, gain_two, w_gate, w_up, w_down = weights
    normed = low(norm_rows(inputs, gain_one, 1e-06))
    queries = low_back(low(jnp.dot(normed, w_query, precision=MAXIMUM_ACCURACY)))
    key_rows = low_back(low(jnp.dot(normed, w_key, precision=MAXIMUM_ACCURACY)))
    value_matrix = low_back(low(jnp.dot(normed, w_value, precision=MAXIMUM_ACCURACY)))
    low_rank = low_back(low(jnp.dot(normed, w_rank_in, precision=MAXIMUM_ACCURACY)))
    gate_pre = low_back(jnp.dot(low_rank, w_rank_out, precision=MAXIMUM_ACCURACY) + gate_bias)
    decays = jax.nn.log_sigmoid(gate_pre) / 16.0
    swish_pre = low_back(jnp.dot(normed, w_swish, precision=MAXIMUM_ACCURACY))
    mixed_heads = mix_sequence(heads_of(queries, HEAD_K) * HEAD_K ** (-0.5), heads_of(key_rows, HEAD_K), heads_of(value_matrix, HEAD_V), heads_of(decays, HEAD_K), starts)
    headed = norm_rows(mixed_heads, head_gain, 1e-05) * jax.nn.silu(heads_of(swish_pre, HEAD_V))
    gated_rows = low(headed.reshape(LENGTH, HEADS * HEAD_V))
    branch = low_back(jnp.dot(gated_rows, w_output, precision=MAXIMUM_ACCURACY))
    hidden_state = inputs + branch
    normed_two = low(norm_rows(hidden_state, gain_two, 1e-06))
    gate_proj = low_back(jnp.dot(normed_two, w_gate, precision=MAXIMUM_ACCURACY))
    up_proj = low_back(jnp.dot(normed_two, w_up, precision=MAXIMUM_ACCURACY))
    inner_rows = low(jax.nn.silu(gate_proj) * up_proj)
    return hidden_state + low_back(jnp.dot(inner_rows, w_down, precision=MAXIMUM_ACCURACY))

def reference(tokens, cotangent, doc_starts, gain_one, w_query, w_key, w_value, w_swish, w_rank_in, w_rank_out, gate_bias, head_gain, w_output, gain_two, w_gate, w_up, w_down):
    weights = tuple((weight.astype(jnp.float32) for weight in (gain_one, w_query, w_key, w_value, w_swish, w_rank_in, w_rank_out, gate_bias, head_gain, w_output, gain_two, w_gate, w_up, w_down)))
    inputs = tokens.astype(jnp.float32).reshape(SEQS, LENGTH, D)
    upstream = cotangent.astype(jnp.float32).reshape(SEQS, LENGTH, D)

    def per_sequence(totals, pieces):
        inputs_one, upstream_one, starts = pieces

        def forward(inputs_arg, *weight_args):
            return block_layer(inputs_arg, starts, weight_args)
        result, pullback = jax.vjp(forward, inputs_one, *weights)
        gradients = pullback(upstream_one)
        totals = tuple((running + fresh_grads for running, fresh_grads in zip(totals, gradients[1:])))
        return (totals, (result, gradients[0]))
    zero_grads = tuple((jnp.zeros_like(weight) for weight in weights))
    totals, (results, input_grads) = lax.scan(per_sequence, zero_grads, (inputs, upstream, doc_starts))
    return (results.reshape(TOKENS, D).astype(jnp.bfloat16), input_grads.reshape(TOKENS, D), totals[0], totals[1], totals[2], totals[3], totals[4], totals[5], totals[6], totals[7], totals[8], totals[9], totals[10], totals[11], totals[12], totals[13])
```

```python
from functools import partial

import jax
import jax.numpy as jnp
from jax import lax
from jax.experimental import pallas as pl
from jax.experimental.pallas import tpu as pltpu
from jax.sharding import Mesh
from jax.sharding import PartitionSpec as P

HEAD_K = 256
HEAD_V = 256
GROUP = 64
AXES = ("z", "y", "x", "c")
VMEM = 56 * 1024 * 1024
F32 = jnp.float32
BF16 = jnp.bfloat16


def shift(value, axis, step):
    size = lax.axis_size(axis)
    return lax.ppermute(value, axis, [(i, (i + step) % size) for i in range(size)])


def flip(value, axis):
    return shift(value, axis, 1)


def place():
    return tuple(lax.axis_index(a) for a in AXES)


def spread(shard):
    depth, height = lax.axis_size("z"), lax.axis_size("y")
    half = depth // 2
    own = jnp.stack([shard] + [shift(shard, "z", k) for k in range(1, depth)])
    across = flip(own, "x")
    pieces = [(own, 0, 0, 0, depth), (across, 0, 1, 0, depth)]
    for j in range(1, height):
        along = shift(own, "y", j)
        pieces.append((along, j, 0, 0, depth))
        pieces.append((shift(across[:half], "y", j), j, 1, 0, half))
        pieces.append((flip(along[half:], "x"), j, 1, half, depth))
    return pieces


def gathered(shard):
    pieces = spread(shard)
    return [(a, j, i, 0, f, l) for a, j, i, f, l in pieces] + [
        (flip(a, "c"), j, i, 1, f, l) for a, j, i, f, l in pieces
    ]


def sources(pieces):
    z, y, x, c = place()
    depth, height = lax.axis_size("z"), lax.axis_size("y")
    chips, cores = [], []
    for _, j, i, other, first, last in pieces:
        for k in range(first, last):
            chip = (((z - k) % depth) * height + (y - j) % height) * 2 + (x + i) % 2
            chips.append(chip)
            cores.append((c + other) % 2)
    return jnp.stack(chips + cores).astype(jnp.int32)


def assemble(shard, parts):
    pieces = gathered(shard)
    where = sources(pieces)
    arrays = [p[0] for p in pieces]
    blocks = [(n, k) for n, p in enumerate(pieces) for k in range(p[5] - p[4])]
    total = len(blocks)

    if any(rows % 16 for _, rows, _, _ in parts):
        chips, cores = where[:total], where[total:]
        back = jnp.zeros((total,), jnp.int32).at[chips * 2 + cores].set(jnp.arange(total, dtype=jnp.int32))
        ordered = jnp.take(jnp.concatenate(arrays), back, axis=0)
        whole = []
        for first, rows, by_columns, shape in parts:
            part = lax.optimization_barrier(ordered[:, first : first + rows])
            if by_columns:
                part = part.reshape(total // 2, 2, rows, -1).transpose(0, 2, 1, 3)
            whole.append(lax.optimization_barrier(part.reshape(shape)))
        return whole

    def body(where_ref, *refs):
        ins, outs, sems = refs[: len(arrays)], refs[len(arrays) : -1], refs[-1]
        for at, (n, k) in enumerate(blocks):
            chip, core = where_ref[at], where_ref[total + at]
            for w, (first, rows, by_columns, shape) in enumerate(parts):
                source = ins[n].at[k, pl.ds(first, rows), :]
                if by_columns:
                    width = shape[1] // 2
                    goal = outs[w].at[
                        pl.ds(pl.multiple_of(chip * rows, rows), rows),
                        pl.ds(pl.multiple_of(core * width, width), width),
                    ]
                else:
                    device = chip * 2 + core
                    goal = outs[w].at[pl.ds(pl.multiple_of(device * rows, rows), rows), :]
                pltpu.make_async_copy(source, goal, sems.at[w]).start()
        for w in range(len(parts)):
            pltpu.make_async_copy(outs[w], outs[w], sems.at[w]).wait()

    hbm = pl.BlockSpec(memory_space=pl.ANY)
    return pl.pallas_call(
        body,
        grid_spec=pltpu.PrefetchScalarGridSpec(
            num_scalar_prefetch=1,
            grid=(1,),
            in_specs=[hbm] * len(arrays),
            out_specs=[pl.BlockSpec(p[3], lambda n, s: (0, 0)) for p in parts],
            scratch_shapes=[pltpu.SemaphoreType.DMA((len(parts),))],
        ),
        out_shape=[jax.ShapeDtypeStruct(p[3], shard.dtype) for p in parts],
        compiler_params=pltpu.CompilerParams(vmem_limit_bytes=VMEM),
    )(where, *arrays)


def routes():
    depth, height = lax.axis_size("z"), lax.axis_size("y")
    half = depth // 2
    order = []
    for j in range(1, height):
        order += [(j, 1, 0, half), (j, 1, half, depth)]
    for j in range(1, height):
        order.append((j, 0, 0, depth))
    return order + [(0, 1, 0, depth), (0, 0, 0, depth)]


def targets():
    z, y, x, _ = place()
    depth, height = lax.axis_size("z"), lax.axis_size("y")
    chips = []
    for j, i, first, last in routes():
        for k in range(first, last):
            chips.append((((z + k) % depth) * height + (y + j) % height) * 2 + (x + i) % 2)
    return jnp.stack(chips).astype(jnp.int32)


def collect(blocks):
    depth, height = lax.axis_size("z"), lax.axis_size("y")
    half = depth // 2
    held = dict(zip(routes(), blocks))

    def wide(a):
        return a.astype(F32)

    by_x = [flip(held[j, 1, 0, half], "x") for j in range(1, height)]
    by_y = [shift(held[j, 1, half, depth], "y", j) for j in range(1, height)]
    straight = held[0, 0, 0, depth]
    across = held[0, 1, 0, depth]
    across_late = wide(across[half:])
    for a in by_y:
        across_late = across_late + wide(a)
    across = jnp.concatenate([across[:half], across_late.astype(BF16)])
    arrived = [flip(across, "x")]
    for j in range(1, height):
        along = held[j, 0, 0, depth]
        early = (wide(along[:half]) + wide(by_x[j - 1])).astype(BF16)
        arrived.append(shift(jnp.concatenate([early, along[half:]]), "y", j))
    sums = []
    for k in range(depth):
        total = wide(straight[k])
        for a in arrived:
            total = total + wide(a[k])
        sums.append(total)
    result = sums[0]
    for k in range(1, depth):
        result = result + wide(shift(sums[k].astype(BF16), "z", k))
    return result


def weight_grads(left, right, tile, halves=False):
    order = routes()
    _, _, _, c = place()
    chips = targets()
    count = chips.shape[0]
    tokens, height = left[0].shape
    width = right[0].shape[1] // (2 if halves else 1)
    rows = height // (count if halves else 2 * count)
    starts = chips * rows if halves else (chips * 2 + c) * rows

    if rows % 16:
        full = jnp.concatenate(left)
        product = matmul_t(full, jnp.concatenate(right)).astype(BF16)
        if halves:
            product = lax.dynamic_slice_in_dim(product, c * width, width, 1).reshape(count, rows, width)
        else:
            product = lax.dynamic_index_in_dim(product.reshape(count, 2, rows, width), c, 1, False)
        product = jnp.take(product, chips, axis=0)
        blocks, at = [], 0
        for _, _, first, last in order:
            blocks.append(product[at : at + last - first])
            at += last - first
        return blocks

    first_tile = c * (width // tile) if halves else jnp.int32(0)
    numbers = jnp.concatenate([starts, first_tile[None]]).astype(jnp.int32)

    def body(numbers_ref, lo_ref, ls_ref, ro_ref, rs_ref, *refs):
        outs, (turned, chosen) = refs[:-2], refs[-2:]

        @pl.when(pl.program_id(0) == 0)
        def _():
            turned[:, :tokens] = lo_ref[...].T
            turned[:, tokens:] = ls_ref[...].T
            for at in range(count):
                start = pl.multiple_of(numbers_ref[at], 16)
                chosen[at * rows : (at + 1) * rows, :] = turned[pl.ds(start, rows), :]

        both = jnp.concatenate([ro_ref[...], rs_ref[...]], axis=0)
        product = jnp.dot(chosen[...], both, preferred_element_type=F32).astype(BF16)
        at = 0
        for out, (_, _, first, last) in zip(outs, order):
            span = (last - first) * rows
            out[...] = product[at : at + span].reshape(last - first, rows, tile)
            at += span

    whole = pl.BlockSpec((tokens, height), lambda n, s: (0, 0))
    strip = pl.BlockSpec((tokens, tile), lambda n, s: (0, n + s[count]))
    outs = [(last - first, rows, width) for _, _, first, last in order]
    return pl.pallas_call(
        body,
        grid_spec=pltpu.PrefetchScalarGridSpec(
            num_scalar_prefetch=1,
            grid=(width // tile,),
            in_specs=[whole, whole, strip, strip],
            out_specs=[pl.BlockSpec((n, rows, tile), lambda n, s: (0, 0, n)) for n, _, _ in outs],
            scratch_shapes=[
                pltpu.VMEM((height, 2 * tokens), BF16),
                pltpu.VMEM((count * rows, 2 * tokens), BF16),
            ],
        ),
        out_shape=[jax.ShapeDtypeStruct(o, BF16) for o in outs],
        compiler_params=pltpu.CompilerParams(vmem_limit_bytes=VMEM),
        cost_estimate=pl.CostEstimate(
            flops=4 * tokens * count * rows * width,
            bytes_accessed=2 * (count * rows * width + 2 * tokens * (height + width)),
            transcendentals=0,
        ),
    )(numbers, left[0], left[1], right[0], right[1])


MAXIMUM_ACCURACY = lax.Precision.HIGHEST


def prefix(value, axis, combine, identity):
    length, place = (lax.axis_size(axis), lax.axis_index(axis))
    everything = jax.tree.map(
        lambda part, kind: lax.all_gather(part.astype(kind), axis),
        value,
        (jnp.bfloat16, jnp.bfloat16),
    )
    start = jax.tree.map(
        lambda part, zero: jnp.broadcast_to(jnp.asarray(zero, part.dtype), part.shape),
        value,
        identity,
    )

    def prefix_lap(k, before):
        reached = k < place
        new = combine(
            before, jax.tree.map(lambda part, own: part[k].astype(own.dtype), everything, value)
        )
        return jax.tree.map(lambda a, b: jnp.where(reached, a, b), new, before)

    return lax.fori_loop(0, length, prefix_lap, start)


def entering_2(value, axis, combine, identity):
    length, place = (lax.axis_size(axis), lax.axis_index(axis))
    everything = jax.tree.map(
        lambda part, kind: lax.all_gather(part.astype(kind), axis),
        value,
        jax.tree.map(lambda a: jnp.bfloat16 if a.dtype == jnp.float32 else a.dtype, value),
    )
    start = jax.tree.map(
        lambda part, zero: jnp.broadcast_to(jnp.asarray(zero, part.dtype), part.shape),
        value,
        identity,
    )

    def entering_lap(k, before):
        at = length - 1 - k
        reached = at > place
        new = combine(
            before, jax.tree.map(lambda part, own: part[at].astype(own.dtype), everything, value)
        )
        return jax.tree.map(lambda a, b: jnp.where(reached, a, b), new, before)

    return lax.fori_loop(0, length, entering_lap, start)


def matmul(left, right):
    return jnp.dot(left, right, preferred_element_type=jnp.float32)


def matmul_t(left, right):
    return lax.dot_general(
        left, right, (((0,), (0,)), ((), ())), preferred_element_type=jnp.float32
    )


def matmul_nt(left, right):
    return lax.dot_general(
        left, right, (((1,), (1,)), ((), ())), preferred_element_type=jnp.float32
    )


def norm_rows(values, scales, epsilon):
    return values * lax.rsqrt(jnp.mean(values * values, axis=-1, keepdims=True) + epsilon) * scales


def norm_model(values, scales):
    return norm_rows(values, scales, 1e-06)


def heads_of(tensor, head_width):
    return tensor.reshape(tensor.shape[0], -1, head_width)


def head_gate(mixed_heads, scales, swish_pre):
    headed = norm_rows(mixed_heads, scales, 1e-05) * jax.nn.silu(heads_of(swish_pre, HEAD_V))
    return headed.reshape(headed.shape[0], -1)


def decay_of(gate_pre):
    return heads_of(jax.nn.log_sigmoid(gate_pre) / 16.0, HEAD_K)


def swiglu(gate_proj, up_proj):
    return jax.nn.silu(gate_proj) * up_proj


def document_of(positions, starts):
    return jnp.sum((starts[None, :] <= positions[:, None]).astype(jnp.int32), axis=1) - 1


def combine_states(earlier_part, later_part):
    return (
        earlier_part[0] * later_part[0],
        later_part[0][:, :, None] * earlier_part[1] + later_part[1],
    )


def group_step(passed_state, pieces):
    queries, key_rows, value_matrix, decays, doc_ids, prev_doc = pieces
    running_total = jnp.cumsum(decays, axis=0)
    query_entering = queries * jnp.exp(running_total)
    key_in = key_rows * jnp.exp(-running_total)
    scores = jnp.einsum("thk,shk->hts", query_entering, key_in, precision=MAXIMUM_ACCURACY)
    indices = jnp.arange(doc_ids.shape[0], dtype=jnp.int32)
    allowed = (doc_ids[:, None] == doc_ids[None, :]) & (indices[:, None] >= indices[None, :])
    scores = jnp.where(allowed[None], scores, 0.0)
    within = jnp.einsum("hts,shv->thv", scores, value_matrix, precision=MAXIMUM_ACCURACY)
    entering = (doc_ids == prev_doc).astype(queries.dtype)
    carried_over = jnp.einsum(
        "wiu,iug->wig", query_entering, passed_state, precision=MAXIMUM_ACCURACY
    )
    outputs = within + entering[:, None, None] * carried_over
    closing_sum = running_total[-1]
    tail_rows = (doc_ids == doc_ids[-1]).astype(queries.dtype)
    key_finish = key_rows * jnp.exp(closing_sum[None] - running_total) * tail_rows[:, None, None]
    retained_state = (doc_ids[-1] == prev_doc).astype(queries.dtype)
    updated_state = retained_state * jnp.exp(closing_sum)[:, :, None] * passed_state + jnp.einsum(
        "yaq,yap->aqp", key_finish, value_matrix, precision=MAXIMUM_ACCURACY
    )
    return (updated_state, outputs)


def local_mixer(queries, key_rows, value_matrix, decays, doc_ids, prev_ids, device_keep):
    blocks = queries.shape[0] // GROUP
    rescaled_rows = queries * queries.shape[-1] ** (-0.5)

    def split_blocks(tensor):
        return tensor.reshape((blocks, GROUP) + tensor.shape[1:])

    start_state = jnp.zeros(
        (queries.shape[1], queries.shape[2], value_matrix.shape[2]), jnp.float32
    )
    final_state, outputs = lax.scan(
        group_step,
        start_state,
        (
            split_blocks(rescaled_rows),
            split_blocks(key_rows),
            split_blocks(value_matrix),
            split_blocks(decays),
            split_blocks(doc_ids),
            split_blocks(prev_ids)[:, 0],
        ),
    )
    transfer_scale = device_keep * jnp.exp(jnp.sum(decays, axis=0))
    return (outputs.reshape(value_matrix.shape), final_state, transfer_scale)


def incoming(queries, decays, incoming_state, entry_rows):
    rescaled_rows = queries * queries.shape[-1] ** (-0.5)
    running_total = jnp.cumsum(decays, axis=0)
    return entry_rows[:, None, None] * jnp.einsum(
        "wiu,iug->wig",
        rescaled_rows * jnp.exp(running_total),
        incoming_state,
        precision=MAXIMUM_ACCURACY,
    )


def forward(inputs, attention, feedforward, context):
    doc_ids, prev_ids, entry_rows, device_keep = context
    (
        gain_one,
        w_query,
        w_key,
        w_value,
        w_swish,
        w_rank_in,
        w_rank_out,
        gate_bias,
        head_gain,
        w_output,
    ) = attention
    gain_two, w_gate, w_up, w_down = feedforward
    normed = norm_model(inputs, gain_one.astype(jnp.float32)).astype(jnp.bfloat16)
    queries = matmul(normed, w_query).astype(jnp.bfloat16)
    key_rows = matmul(normed, w_key).astype(jnp.bfloat16)
    value_matrix = matmul(normed, w_value).astype(jnp.bfloat16)
    low_rank = matmul(normed, w_rank_in).astype(jnp.bfloat16)
    gate_pre = matmul(low_rank, w_rank_out) + gate_bias.astype(jnp.float32)
    swish_pre = matmul(normed, w_swish)
    decays = decay_of(gate_pre)
    query_heads = heads_of(queries.astype(jnp.float32), HEAD_K)
    mixed_zero, final_state, transfer_scale = local_mixer(
        query_heads,
        heads_of(key_rows.astype(jnp.float32), HEAD_K),
        heads_of(value_matrix.astype(jnp.float32), HEAD_V),
        decays,
        doc_ids,
        prev_ids,
        device_keep,
    )
    identity = (jnp.ones_like(transfer_scale), jnp.zeros_like(final_state))
    prefix_scale, incoming_state = prefix(
        (transfer_scale, final_state), ("y", "x", "c"), combine_states, identity
    )
    mixed_heads = mixed_zero + incoming(query_heads, decays, incoming_state, entry_rows)
    gated_rows = head_gate(mixed_heads, head_gain.astype(jnp.float32), swish_pre).astype(
        jnp.bfloat16
    )
    hidden_state = inputs + matmul(gated_rows, w_output)
    normed_two = norm_model(hidden_state, gain_two.astype(jnp.float32)).astype(jnp.bfloat16)
    gate_proj = matmul(normed_two, w_gate)
    up_proj = matmul(normed_two, w_up)
    inner_rows = swiglu(gate_proj, up_proj).astype(jnp.bfloat16)
    result = hidden_state + matmul(inner_rows, w_down)
    return (
        result,
        normed,
        queries,
        key_rows,
        value_matrix,
        low_rank,
        gate_pre,
        swish_pre,
        mixed_heads,
        incoming_state,
        transfer_scale,
        gated_rows,
        hidden_state,
        normed_two,
        gate_proj,
        up_proj,
        inner_rows,
    )


def backward(upstream, inputs, attention, feedforward, kept_values, context):
    doc_ids, prev_ids, entry_rows, device_keep = context
    (
        gain_one,
        w_query,
        w_key,
        w_value,
        w_swish,
        w_rank_in,
        w_rank_out,
        gate_bias,
        head_gain,
        w_output,
    ) = attention
    gain_two, w_gate, w_up, w_down = feedforward
    (
        result,
        normed,
        queries,
        key_rows,
        value_matrix,
        low_rank,
        gate_pre,
        swish_pre,
        mixed_heads,
        incoming_state,
        transfer_scale,
        gated_rows,
        hidden_state,
        normed_two,
        gate_proj,
        up_proj,
        inner_rows,
    ) = kept_values
    down_grad = upstream.astype(jnp.bfloat16)
    grad_inner = matmul_nt(down_grad, w_down)
    _, pull_mlp = jax.vjp(swiglu, gate_proj, up_proj)
    grad_gate, grad_up = pull_mlp(grad_inner)
    grad_gate = grad_gate.astype(jnp.bfloat16)
    grad_up = grad_up.astype(jnp.bfloat16)
    grad_normed_two = matmul_nt(grad_gate, w_gate) + matmul_nt(grad_up, w_up)
    _, pull_second = jax.vjp(norm_model, hidden_state, gain_two.astype(jnp.float32))
    hidden_extra, grad_gain_two = pull_second(grad_normed_two)
    grad_hidden = upstream + hidden_extra
    branch_grad = grad_hidden.astype(jnp.bfloat16)
    grad_gated = matmul_nt(branch_grad, w_output)
    _, pull_head = jax.vjp(head_gate, mixed_heads, head_gain.astype(jnp.float32), swish_pre)
    grad_mixed, grad_head_gain, grad_swish = pull_head(grad_gated)
    query_heads = heads_of(queries.astype(jnp.float32), HEAD_K)
    key_heads = heads_of(key_rows.astype(jnp.float32), HEAD_K)
    value_heads = heads_of(value_matrix.astype(jnp.float32), HEAD_V)
    decays, pull_decay = jax.vjp(decay_of, gate_pre)
    _, pull_enter = jax.vjp(
        partial(incoming, entry_rows=entry_rows), query_heads, decays, incoming_state
    )
    grad_q_enter, grad_decay_enter, grad_entry = pull_enter(grad_mixed)
    identity = (jnp.ones_like(transfer_scale), jnp.zeros_like(grad_entry))
    suffix_scale, exit_grad = entering_2(
        (transfer_scale, grad_entry), ("y", "x", "c"), combine_states, identity
    )
    grad_scale = jnp.sum(exit_grad * incoming_state, axis=2)
    _, pull_local = jax.vjp(
        partial(local_mixer, doc_ids=doc_ids, prev_ids=prev_ids, device_keep=device_keep),
        query_heads,
        key_heads,
        value_heads,
        decays,
    )
    grad_q_local, grad_key, grad_value, grad_decay_local = pull_local(
        (grad_mixed, exit_grad, grad_scale)
    )
    (grad_gate_pre,) = pull_decay(grad_decay_local + grad_decay_enter)
    gate_grad_low = grad_gate_pre.astype(jnp.bfloat16)
    grad_gate_bias = jnp.sum(gate_grad_low.astype(jnp.float32), axis=0)
    grad_low_rank = matmul_nt(gate_grad_low, w_rank_out).astype(jnp.bfloat16)
    row_count = normed.shape[0]
    swish_grad_low = grad_swish.astype(jnp.bfloat16)
    query_grad_low = (grad_q_local + grad_q_enter).reshape(row_count, -1).astype(jnp.bfloat16)
    key_grad_low = grad_key.reshape(row_count, -1).astype(jnp.bfloat16)
    value_grad_low = grad_value.reshape(row_count, -1).astype(jnp.bfloat16)
    grad_normed = (
        matmul_nt(query_grad_low, w_query)
        + matmul_nt(key_grad_low, w_key)
        + matmul_nt(value_grad_low, w_value)
        + matmul_nt(swish_grad_low, w_swish)
        + matmul_nt(grad_low_rank, w_rank_in)
    )
    _, pull_first = jax.vjp(norm_model, inputs, gain_one.astype(jnp.float32))
    input_extra, grad_gain_one = pull_first(grad_normed)
    input_grad = grad_hidden + input_extra
    return (
        input_grad,
        (grad_gain_one, grad_gate_bias, grad_head_gain, grad_gain_two),
        (gate_grad_low, low_rank, grad_low_rank, normed),
        jnp.concatenate([query_grad_low, key_grad_low, value_grad_low], axis=1),
        (gated_rows, branch_grad, swish_grad_low),
        (normed_two, jnp.concatenate([grad_gate, grad_up], axis=1)),
        (inner_rows, down_grad),
    )


def pair(value):
    return (value, flip(value, "c"))


def gather_weights(
    gain_one, w_query, w_key, w_value, w_swish, w_rank_in, w_rank_out, gate_bias, head_gain, w_output, gain_two,
    w_gate, w_up, w_down,
):
    c = lax.axis_index("c")
    rows, wide = w_query.shape
    rank = w_rank_in.shape[1]
    devices = wide // rows
    piece = jnp.zeros((rank, wide), BF16)
    piece = piece.at[:, :rows].set(w_rank_out)
    piece = piece.at[:, rows : 2 * rows].set(w_rank_in.T)
    piece = piece.at[0, 2 * rows : 3 * rows].set(gain_one)
    piece = piece.at[1, 2 * rows : 3 * rows].set(gate_bias)
    piece = piece.at[2, 2 * rows : 3 * rows].set(gain_two)
    piece = piece.at[3, 2 * rows : 2 * rows + head_gain.shape[0]].set(head_gain)
    square = (wide, wide)
    query, key, value, small = assemble(
        jnp.concatenate([w_query, w_key, w_value, piece]),
        [(n * rows, rows, False, square) for n in range(3)] + [(3 * rows, rank, False, (devices * rank, wide))],
    )
    swish, output = assemble(
        jnp.concatenate([w_swish, w_output]), [(n * rows, rows, False, square) for n in range(2)]
    )
    ff = w_gate.shape[1]
    gate, up = assemble(
        jnp.concatenate([w_gate, w_up]), [(n * rows, rows, False, (wide, ff)) for n in range(2)]
    )
    half = wide // 2
    keep = lax.dynamic_slice_in_dim(w_down, c * half, half, 1)
    other = flip(lax.dynamic_slice_in_dim(w_down, (1 - c) * half, half, 1), "c")
    both = jnp.where(c == 0, jnp.concatenate([keep, other]), jnp.concatenate([other, keep]))
    (down,) = assemble(both, [(0, both.shape[0], True, (ff, wide))])
    small = small.reshape(devices, rank, wide)
    rank_out = small[:, :, :rows].transpose(1, 0, 2).reshape(rank, wide)
    rank_in = small[:, :, rows : 2 * rows].transpose(0, 2, 1).reshape(wide, rank)
    vectors = small[:, :4, 2 * rows : 3 * rows]
    attention = (
        vectors[:, 0].reshape(-1), query, key, value, swish, rank_in, rank_out, vectors[:, 1].reshape(-1),
        vectors[:, 3, : head_gain.shape[0]].reshape(-1), output,
    )
    return attention, (vectors[:, 2].reshape(-1), gate, up, down)


def small_grads(vectors, factors):
    gain_one, gate_bias, head_gain, gain_two = vectors
    gate_grad, low_rank, low_grad, normed = factors
    c = lax.axis_index("c")
    wide = gain_one.shape[0]
    devices = lax.axis_size("z") * lax.axis_size("y") * 4
    rows = wide // devices
    heads = jnp.zeros((devices, rows), F32).at[:, : head_gain.shape[0] // devices].set(head_gain.reshape(devices, -1))
    table = jnp.concatenate(
        [matmul_t(normed, low_grad), matmul_t(gate_grad, low_rank)]
        + [v.reshape(wide, 1) for v in (gain_one, gate_bias, gain_two, heads)],
        axis=1,
    )
    table = jnp.pad(table, ((0, 0), (0, 128 - table.shape[1])))
    table = table.reshape(devices // 2, 2, rows, 128)
    mine = lax.dynamic_index_in_dim(table, c, 1, False)
    theirs = flip(lax.dynamic_index_in_dim(table, 1 - c, 1, False), "c")
    table = jnp.take((mine + theirs).astype(BF16), targets(), axis=0)
    blocks, at = [], 0
    for _, _, first, last in routes():
        blocks.append(table[at : at + last - first])
        at += last - first
    return blocks


def shards(tokens, cotangent, doc_starts, *weights):
    row_count = tokens.shape[0]
    z, y, x, c = place()
    first_row = ((y * 2 + x) * 2 + c) * row_count
    positions = first_row + jnp.arange(row_count, dtype=jnp.int32)
    starts = doc_starts[0]
    doc_ids = document_of(positions, starts)
    prev_ids = document_of(positions - 1, starts)
    entry_rows = (doc_ids == prev_ids[0]).astype(jnp.float32)
    device_keep = entry_rows[-1]
    context = (doc_ids, prev_ids, entry_rows, device_keep)
    inputs = tokens.astype(jnp.float32)
    attention, feedforward = gather_weights(*weights)
    kept_values = forward(inputs, attention, feedforward, context)
    output = kept_values[0].astype(jnp.bfloat16)
    upstream = cotangent.astype(jnp.float32)
    input_grad, vectors, factors, qkv_grad, middle, first, second = backward(
        upstream, inputs, attention, feedforward, kept_values, context
    )
    gates = collect(weight_grads(pair(first[0]), pair(first[1]), 512))
    down = collect(weight_grads(pair(second[0]), pair(second[1]), 256, True))
    gated_rows, branch_grad, swish_grad = middle
    normed = pair(factors[3])
    grad_output = collect(weight_grads(pair(gated_rows), pair(branch_grad), 512))
    grad_swish = collect(weight_grads(normed, pair(swish_grad), 512))
    qkv = collect(weight_grads(normed, pair(qkv_grad), 512))
    small = collect(small_grads(vectors, factors))
    rows, wide = weights[1].shape
    ff = weights[11].shape[1]
    own_rows = weights[13].shape[0]
    keep = lax.dynamic_slice_in_dim(down, c * own_rows, own_rows, 0)
    other = flip(lax.dynamic_slice_in_dim(down, (1 - c) * own_rows, own_rows, 0), "c")
    down = jnp.where(c == 0, jnp.concatenate([keep, other], 1), jnp.concatenate([other, keep], 1))
    rank = weights[5].shape[1]
    return (
        output,
        input_grad,
        small[:, 2 * rank],
        qkv[:, :wide],
        qkv[:, wide : 2 * wide],
        qkv[:, 2 * wide :],
        grad_swish,
        small[:, :rank],
        small[:, rank : 2 * rank].T,
        small[:, 2 * rank + 1],
        small[: weights[8].shape[0], 2 * rank + 3],
        grad_output,
        small[:, 2 * rank + 2],
        gates[:, :ff],
        gates[:, ff:],
        down,
    )


def solution(mesh):
    fsdp, seq = mesh.shape["fsdp"], mesh.shape["seq"]
    inner = Mesh(mesh.devices.reshape(fsdp, seq // 4, 2, 2), AXES)
    rows, vector, columns = P(AXES, None), P(AXES), P(None, AXES)
    in_specs = (rows, rows, P("z", None), vector, rows, rows, rows, rows, rows, columns, vector, vector, rows, vector) + (rows,) * 3
    out_specs = (rows, rows, vector) + (rows,) * 5 + (columns, vector, vector, rows, vector) + (rows,) * 3
    return jax.shard_map(shards, mesh=inner, in_specs=in_specs, out_specs=out_specs, check_vma=False)
```

```python
from functools import partial

import jax
import jax.numpy as jnp
from jax import lax
from jax.experimental import pallas as pl
from jax.experimental.pallas import tpu as pltpu
from jax.sharding import Mesh
from jax.sharding import PartitionSpec as P

HEAD_K = 256
HEAD_V = 256
GROUP = 64
LANES = 128
AXES = ("z", "y", "x", "c")
VMEM = 56 * 1024 * 1024
QUICK = pl.CostEstimate(flops=0, bytes_accessed=0, transcendentals=0)
F32 = jnp.float32
BF16 = jnp.bfloat16


def shift(value, axis, step):
    size = lax.axis_size(axis)
    return lax.ppermute(value, axis, [(i, (i + step) % size) for i in range(size)])


def flip(value, axis):
    return shift(value, axis, 1)


def place():
    return tuple(lax.axis_index(a) for a in AXES)


def after(done, *values):
    out = lax.optimization_barrier((values, done))[0]
    return out[0] if len(values) == 1 else out


def square_plane():
    return lax.axis_size("y") == 2


def cross(value, late):
    perm = [(i, i ^ (2 if (i % 2 == 0) != late else 4)) for i in range(8)]
    return lax.ppermute(value, ("y", "x", "c"), perm)


def neighbour(early, late, core):
    _, y, x, _ = place()
    by_x = jnp.where(core == 0, early, late)
    by_y = jnp.where(core == 0, late, early)
    return (y + by_y) % 2, (x + by_x) % 2


def gathered(own, early, late, corner):
    pieces = [(own, 0, 0, 0), (early, 1, 0, 0), (late, 0, 1, 0), (corner, 1, 1, 0)]
    return pieces + [(flip(a, "c"), i, j, 1) for a, i, j, _ in pieces]


def sources(pieces):
    z, _, _, c = place()
    depth = lax.axis_size("z")
    chips, cores = [], []
    for _, early, late, other in pieces:
        core = (c + other) % 2
        y, x = neighbour(early, late, core)
        for k in range(depth):
            chips.append((((z - k) % depth) * 2 + y) * 2 + x)
            cores.append(core)
    return jnp.stack(chips + cores).astype(jnp.int32)


def assemble(pieces, rows, shape, by_columns=False):
    where = sources(pieces)
    arrays = [p[0] for p in pieces]
    depth = arrays[0].shape[0]
    blocks = [(n, k) for n in range(len(pieces)) for k in range(depth)]
    total = len(blocks)

    def body(where_ref, *refs):
        ins, out, sem = refs[: len(arrays)], refs[-2], refs[-1]
        for at, (n, k) in enumerate(blocks):
            chip, core = where_ref[at], where_ref[total + at]
            if by_columns:
                width = shape[1] // 2
                goal = out.at[
                    pl.ds(pl.multiple_of(chip * rows, rows), rows),
                    pl.ds(pl.multiple_of(core * width, width), width),
                ]
            else:
                goal = out.at[pl.ds(pl.multiple_of((chip * 2 + core) * rows, rows), rows), :]
            pltpu.make_async_copy(ins[n].at[k], goal, sem).start()
        pltpu.make_async_copy(out, out, sem).wait()

    return pl.pallas_call(
        body,
        grid_spec=pltpu.PrefetchScalarGridSpec(
            num_scalar_prefetch=1,
            grid=(1,),
            in_specs=[pl.BlockSpec(memory_space=pl.ANY)] * len(arrays),
            out_specs=pl.BlockSpec(shape, lambda n, s: (0, 0)),
            scratch_shapes=[pltpu.SemaphoreType.DMA],
        ),
        out_shape=jax.ShapeDtypeStruct(shape, BF16),
        compiler_params=pltpu.CompilerParams(vmem_limit_bytes=VMEM),
        cost_estimate=QUICK,
    )(where, *arrays)


def layout():
    _, _, _, c = place()
    depth, height = lax.axis_size("z"), lax.axis_size("y")
    if not square_plane():
        return [jnp.arange(depth * height * 2, dtype=jnp.int32)]

    def column(early, late):
        y, x = neighbour(early, late, c)
        return (jnp.arange(depth, dtype=jnp.int32) * 2 + y) * 2 + x

    return [jnp.concatenate([column(1, 0), column(1, 1)]), column(0, 1), column(0, 0)]


def wide(a):
    return a.astype(F32)


class Sum:
    def __init__(self, blocks):
        self.blocks = blocks

    def first(self, done=()):
        self.arrived = cross(after(done, self.blocks[0]), False) if square_plane() else ()
        return self.arrived

    def second(self, done=()):
        if not square_plane():
            self.through = ()
            return ()
        depth = lax.axis_size("z")
        arrived, kept = after(done, self.arrived, self.blocks[1])
        self.through = cross((wide(kept) + wide(arrived[depth:])).astype(BF16), True)
        return self.through

    def third(self, done=()):
        width = self.blocks[-1].shape[-1]
        if not square_plane():
            total = self.blocks[0].reshape(-1, width)
            return wide(lax.psum_scatter(total, ("z", "y", "x"), scatter_dimension=0, tiled=True))
        depth = lax.axis_size("z")
        arrived, through = after(done, self.arrived, self.through)
        total = wide(self.blocks[2]) + wide(arrived[:depth]) + wide(through)
        total = total.astype(BF16).reshape(-1, width)
        return wide(lax.psum_scatter(total, "z", scatter_dimension=0, tiled=True))


def weight_grads(groups, tile, halves=False, table=None):
    _, _, _, c = place()
    chips = layout()
    spans = [a.shape[0] for a in chips]
    chips = jnp.concatenate(chips)
    count = chips.shape[0]
    lefts = [left for left, _ in groups]
    rights = [right for _, group in groups for right in group]
    owner = [n for n, (_, group) in enumerate(groups) for _ in group]
    tokens, height = lefts[0][0].shape
    each = rights[0][0].shape[1] // (2 if halves else 1)
    width = each * len(rights)
    rows = height // (count if halves else 2 * count)
    starts = chips * rows if halves else (chips * 2 + c) * rows

    if rows % 16:
        products = []
        for n, right in zip(owner, rights):
            product = tn(jnp.concatenate(lefts[n]), jnp.concatenate(right)).astype(BF16)
            if halves:
                product = lax.dynamic_slice_in_dim(product, c * each, each, 1).reshape(count, rows, each)
            else:
                product = lax.dynamic_index_in_dim(product.reshape(count, 2, rows, each), c, 1, False)
            products.append(product)
        if table is not None:
            product = wide(table[1])
            for left, right in table[0]:
                product = product + tn(jnp.concatenate(left), jnp.concatenate(right))
            product = product.astype(BF16).reshape(count, 2, rows, LANES)
            products.append(lax.dynamic_index_in_dim(product, c, 1, False))
        product = jnp.take(jnp.concatenate(products, axis=2), chips, axis=0)
        blocks, at = [], 0
        for span in spans:
            blocks.append(product[at : at + span])
            at += span
        return Sum(blocks)

    strips = each // tile
    first_tile = c * strips if halves else jnp.int32(0)
    numbers = jnp.concatenate([starts, first_tile[None]]).astype(jnp.int32)

    steps = width // tile
    terms, base = table if table is not None else ((), None)
    flat = [a for left in lefts for a in left] + [a for right in rights for a in right]
    narrow = [a for left, right in terms for a in (*left, *right)]
    if table is not None:
        narrow.append(base)

    def body(numbers_ref, *refs):
        left_refs, right_refs = refs[: 2 * len(lefts)], refs[2 * len(lefts) : len(flat)]
        narrow_refs = refs[len(flat) : len(flat) + len(narrow)]
        outs, (turned, chosen, total, based) = refs[len(flat) + len(narrow) : -4], refs[-4:]
        step = pl.program_id(0)

        def start(at):
            return pl.ds(pl.multiple_of(numbers_ref[at], 16), rows)

        def turn(lo_ref, ls_ref):
            turned[:, :tokens] = lo_ref[...].T
            turned[:, tokens:] = ls_ref[...].T
            for at in range(count):
                chosen[at * rows : (at + 1) * rows, :] = turned[start(at), :]

        def put(product, columns):
            at = 0
            for out, span in zip(outs, spans):
                out[:, :, :columns] = product[at : at + span * rows].reshape(span, rows, columns)
                at += span * rows

        def strip(ro_ref, rs_ref):
            both = jnp.concatenate([ro_ref[...], rs_ref[...]], axis=0)
            put(nn(chosen[...], both).astype(BF16), tile)

        def term(n):
            lo_ref, ls_ref, ro_ref, rs_ref = narrow_refs[4 * n : 4 * n + 4]
            turn(lo_ref, ls_ref)
            both = jnp.concatenate([ro_ref[...], rs_ref[...]], axis=0)
            product = nn(chosen[...], both)
            if n == 0:
                total[...] = product
            else:
                total[...] += product
            if n == len(terms) - 1:
                for at in range(count):
                    based[at * rows : (at + 1) * rows, :] = narrow_refs[-1][start(at), :]
                put((total[...] + wide(based[...])).astype(BF16), LANES)

        for n in range(len(lefts)):
            pl.when(step == owner.index(n) * strips)(partial(turn, *left_refs[2 * n : 2 * n + 2]))
        if len(rights) == 1:
            strip(*right_refs)
        else:
            for n in range(len(rights)):
                pl.when(step // strips == n)(partial(strip, *right_refs[2 * n : 2 * n + 2]))
        for n in range(len(terms)):
            pl.when(step == steps + n)(partial(term, n))

    def column(n):
        return lambda step, s: (0, jnp.clip(step - n * strips, 0, strips - 1) + s[count])

    def full(a):
        return pl.BlockSpec(a.shape, lambda n, s: (0,) * a.ndim)

    right_specs = [pl.BlockSpec((tokens, tile), column(n)) for n in range(len(rights)) for _ in range(2)]
    columns = width + (LANES if table is not None else 0)
    last = steps - (table is None)
    outs = [(span, rows, columns) for span in spans]
    blocks = pl.pallas_call(
        body,
        grid_spec=pltpu.PrefetchScalarGridSpec(
            num_scalar_prefetch=1,
            grid=(steps + len(terms),),
            in_specs=[full(a) for left in lefts for a in left] + right_specs + [full(a) for a in narrow],
            out_specs=[pl.BlockSpec((n, rows, tile), lambda n, s: (0, 0, jnp.minimum(n, last))) for n, _, _ in outs],
            scratch_shapes=[
                pltpu.VMEM((height, 2 * tokens), BF16),
                pltpu.VMEM((count * rows, 2 * tokens), BF16),
                pltpu.VMEM((count * rows, LANES), F32),
                pltpu.VMEM((count * rows, LANES), BF16),
            ],
        ),
        out_shape=[jax.ShapeDtypeStruct(o, BF16) for o in outs],
        compiler_params=pltpu.CompilerParams(vmem_limit_bytes=VMEM),
        cost_estimate=QUICK,
    )(numbers, *flat, *narrow)
    return Sum(blocks)


def nn(left, right):
    return jnp.dot(left, right, preferred_element_type=F32)


def nt(left, right):
    return lax.dot_general(left, right, (((1,), (1,)), ((), ())), preferred_element_type=F32)


def tn(left, right):
    return lax.dot_general(left, right, (((0,), (0,)), ((), ())), preferred_element_type=F32)


def summed(ones, values):
    high = values.astype(BF16)
    low = (values - high.astype(F32)).astype(BF16)
    return nn(ones, high) + nn(ones, low)


def triangle(size, relation, block=None):
    row = lax.broadcasted_iota(jnp.int32, (size, size), 0)
    column = lax.broadcasted_iota(jnp.int32, (size, size), 1)
    chosen = relation(row, column)
    if block is not None:
        chosen = chosen & (row // block == column // block)
    return jnp.where(chosen, 1.0, 0.0).astype(BF16)


def log_decay(gate_pre):
    return (jnp.minimum(gate_pre, 0.0) - jnp.log1p(jnp.exp(-jnp.abs(gate_pre)))) * (1.0 / 16.0)


def sigmoid(v):
    return 1.0 / (1.0 + jnp.exp(-v))


def spec(shape, index=None):
    index = index or (lambda *_: (0,) * len(shape))
    return pl.BlockSpec(shape, index)


def by_head(rows):
    return spec((rows, HEAD_K), lambda h: (0, h))


def kernel_call(body, grid, ins, outs, scratch=()):
    return pl.pallas_call(
        body,
        grid=grid,
        in_specs=[s for _, s in ins],
        out_specs=[s for _, _, s in outs],
        out_shape=[jax.ShapeDtypeStruct(shape, dtype) for shape, dtype, _ in outs],
        scratch_shapes=list(scratch),
        compiler_params=pltpu.CompilerParams(vmem_limit_bytes=VMEM),
        cost_estimate=QUICK,
    )(*[a for a, _ in ins])


MESSAGE = HEAD_V + 16


def unit_columns(rows, columns, start):
    row = lax.broadcasted_iota(jnp.int32, (rows, columns), 0)
    column = lax.broadcasted_iota(jnp.int32, (rows, columns), 1)
    return jnp.where(column == row + start, 1.0, 0.0).astype(BF16)


def first_weights(w_key, w_value, rank_in, rank_out, vectors):
    rows, width = w_key.shape
    rank = rank_in.shape[1]

    def body(wk, wv, ri, ro, *refs):
        vector_refs, out = refs[:-1], refs[-1]
        out[:, :width] = wk[...]
        out[:, width : 2 * width] = wv[...]
        table = nn(ri[...], unit_columns(rank, LANES, 0)) + tn(ro[...], unit_columns(rank, LANES, rank))
        for n, v in enumerate(vector_refs):
            mine = unit_columns(v.shape[1], rows, 0)
            table = table + tn(nn(v[...], mine).astype(BF16), unit_columns(1, LANES, 2 * rank + n))
        out[:, 2 * width :] = table.astype(BF16)

    ins = [w_key, w_value, rank_in, rank_out, *[v.reshape(1, -1) for v in vectors]]
    shape = (rows, 2 * width + LANES)
    return kernel_call(body, (1,), [(a, spec(a.shape)) for a in ins], [(shape, BF16, spec(shape))])[0]


def project(tokens, weights, marks, rank):
    rows, width = tokens.shape
    heads = width // HEAD_K
    at_table = 2 * width // LANES

    def body(x_ref, wk, wv, table, part_ref, marks_ref, n_out, low_out, k_out, v_out, g_out, m_out, vectors_out):
        @pl.when(pl.program_id(0) == 0)
        def _():
            vectors = nt(unit_columns(8, LANES, 2 * rank), table[...])
            vectors_out[...] = vectors
            x = x_ref[...].astype(F32)
            scale = lax.rsqrt(jnp.mean(x * x, axis=1, keepdims=True) + 1e-06)
            n_out[...] = (x * scale * vectors[1:2]).astype(BF16)
            low = nn(n_out[...], table[...]).astype(BF16)
            lane = lax.broadcasted_iota(jnp.int32, (LANES, LANES), 1)
            row = lax.broadcasted_iota(jnp.int32, (LANES, LANES), 0)
            move = jnp.where((lane == row + rank) & (row < rank), 1.0, 0.0).astype(BF16)
            one = jnp.where(lax.broadcasted_iota(jnp.int32, (rows, LANES), 1) == 2 * rank, 1.0, 0.0)
            low_out[...] = (nn(low, move) + one).astype(BF16)

        normed = n_out[...]
        key = nn(normed, wk[...]).astype(BF16)
        value = nn(normed, wv[...]).astype(BF16)
        k_out[...] = key
        v_out[...] = value
        gate = nt(low_out[...], part_ref[...])
        g_out[...] = gate
        decay = log_decay(gate)
        later = summed(triangle(rows, lambda i, j: j > i), decay)
        last = marks_ref[:, 4:5]
        finish = (key.astype(F32) * jnp.exp(later) * last).astype(BF16)
        m_out[0, :HEAD_V] = tn(value, finish).astype(BF16)
        total = jnp.exp(jnp.sum(decay, axis=0, keepdims=True)) * marks_ref[rows - 1 :, 3:4]
        m_out[0, HEAD_V:] = jnp.broadcast_to(total, (MESSAGE - HEAD_V, HEAD_K)).astype(BF16)

    return kernel_call(
        body,
        (heads,),
        [
            (tokens, spec((rows, width))),
            (weights, by_head(width)),
            (weights, spec((width, HEAD_K), lambda h: (0, heads + h))),
            (weights, spec((width, LANES), lambda h: (0, at_table))),
            (weights, spec((HEAD_K, LANES), lambda h: (h, at_table))),
            (marks, spec(marks.shape)),
        ],
        [
            ((rows, width), BF16, spec((rows, width))),
            ((rows, LANES), BF16, spec((rows, LANES))),
            ((rows, width), BF16, by_head(rows)),
            ((rows, width), BF16, by_head(rows)),
            ((rows, width), F32, by_head(rows)),
            ((heads, MESSAGE, HEAD_K), BF16, spec((1, MESSAGE, HEAD_K), lambda h: (h, 0, 0))),
            ((8, width), F32, spec((8, width))),
        ],
    )


def scaled(queries):
    return queries.astype(F32) * HEAD_K ** (-0.5)


def mixer(normed, keys, values, gate_pre, entered, weights, head_gain, tokens, gain, marks, doc_row):
    rows, wide = tokens.shape
    heads = wide // HEAD_K
    blocks = rows // GROUP

    def body(
        n_ref, k_ref, v_ref, g_ref, s_ref, wq, ws, hg_ref, wo, x_ref, gain_ref, marks_ref, doc_ref,
        q_ref, mixed_out, swish_out, gated_out, hidden_out, two_out, states_out, state, total,
    ):
        h = pl.program_id(0)
        q_ref[...] = nn(n_ref[...], wq[...]).astype(BF16)
        swish = nn(n_ref[...], ws[...])
        swish_out[...] = swish
        along = summed(triangle(rows, lambda i, j: j <= i, GROUP), log_decay(g_ref[...]))
        state[...] = s_ref[0].astype(F32)
        causal = triangle(GROUP, lambda i, j: j <= i) > 0
        for n in range(blocks):
            at = slice(n * GROUP, (n + 1) * GROUP)
            marks_n = marks_ref[at]
            run = along[at]
            end = run[GROUP - 1 :]
            key = k_ref[at].astype(F32)
            value = v_ref[at]
            query_in = (scaled(q_ref[at]) * jnp.exp(run)).astype(BF16)
            key_in = (key * jnp.exp(-run)).astype(BF16)
            key_out = (key * jnp.exp(end - run) * marks_n[:, 2:3]).astype(BF16)
            allowed = causal & (marks_n[:, 0:1] == doc_ref[:, at])
            scores = jnp.where(allowed, nt(query_in, key_in), 0.0).astype(BF16)
            before = state[...].astype(BF16)
            states_out[0, n] = before
            mixed_out[at] = nn(scores, value) + marks_n[:, 1:2] * nt(query_in, before)
            kept = marks_n[GROUP - 1 :, 1:2] * jnp.exp(end)
            state[...] = kept * state[...] + tn(value, key_out)
        states_out[0, blocks] = state[...].astype(BF16)
        mixed = mixed_out[...]
        norm = lax.rsqrt(jnp.mean(mixed * mixed, axis=1, keepdims=True) + 1e-05)
        gated = (mixed * norm * hg_ref[...] * (swish * sigmoid(swish))).astype(BF16)
        gated_out[...] = gated
        part = nn(gated, wo[...])

        @pl.when(h == 0)
        def _():
            total[...] = x_ref[...].astype(F32) + part

        @pl.when(h > 0)
        def _():
            total[...] += part

        @pl.when(h == heads - 1)
        def _():
            hidden = total[...]
            hidden_out[...] = hidden
            scale = lax.rsqrt(jnp.mean(hidden * hidden, axis=1, keepdims=True) + 1e-06)
            two_out[...] = (hidden * scale * gain_ref[...]).astype(BF16)

    return kernel_call(
        body,
        (heads,),
        [
            (normed, spec((rows, wide))),
            (keys, by_head(rows)),
            (values, by_head(rows)),
            (gate_pre, by_head(rows)),
            (entered, spec((1, HEAD_V, HEAD_K), lambda h: (h, 0, 0))),
            (weights, by_head(wide)),
            (weights, spec((wide, HEAD_V), lambda h: (0, heads + h))),
            (head_gain, spec((1, HEAD_V))),
            (weights, spec((HEAD_V, wide), lambda h: (h, 2))),
            (tokens, spec((rows, wide))),
            (gain, spec((1, wide))),
            (marks, spec(marks.shape)),
            (doc_row, spec(doc_row.shape)),
        ],
        [
            ((rows, wide), BF16, by_head(rows)),
            ((rows, wide), F32, by_head(rows)),
            ((rows, wide), F32, by_head(rows)),
            ((rows, wide), BF16, by_head(rows)),
            ((rows, wide), F32, spec((rows, wide))),
            ((rows, wide), BF16, spec((rows, wide))),
            ((heads, blocks + 1, HEAD_V, HEAD_K), BF16, spec((1, blocks + 1, HEAD_V, HEAD_K), lambda h: (h, 0, 0, 0))),
        ],
        [pltpu.VMEM((HEAD_V, HEAD_K), F32), pltpu.VMEM((rows, wide), F32)],
    )


def feed(normed_two, cotangent, w_both, w_down, hidden, gain):
    rows, wide = hidden.shape
    inner = w_both.shape[1] // 2
    tile = 256
    steps = inner // tile

    def body(
        n_ref, c_ref, wg, wu, wd, hidden_ref, gain_ref,
        out_ref, inner_out, gate_out, up_out, grad_out, low_out, forward_sum, back_sum,
    ):
        step = pl.program_id(0)
        normed = n_ref[...]
        gate = nn(normed, wg[...])
        up = nn(normed, wu[...])
        soft = sigmoid(gate)
        silu = gate * soft
        product = (silu * up).astype(BF16)
        inner_out[...] = product
        grad = nt(c_ref[...], wd[...])
        grad_up = (grad * silu).astype(BF16)
        grad_gate = (grad * up * (soft * (1.0 + gate * (1.0 - soft)))).astype(BF16)
        up_out[...] = grad_up
        gate_out[...] = grad_gate
        ahead = nn(product, wd[...])
        back = nt(grad_gate, wg[...]) + nt(grad_up, wu[...])

        @pl.when(step == 0)
        def _():
            forward_sum[...] = hidden_ref[...] + ahead
            back_sum[...] = back

        @pl.when(step > 0)
        def _():
            forward_sum[...] += ahead
            back_sum[...] += back

        @pl.when(step == steps - 1)
        def _():
            out_ref[...] = forward_sum[...].astype(BF16)
            hidden = hidden_ref[...]
            scale = lax.rsqrt(jnp.mean(hidden * hidden, axis=1, keepdims=True) + 1e-06)
            unit = hidden * scale
            grad = back_sum[...] * gain_ref[...]
            grad = scale * (grad - unit * jnp.mean(grad * unit, axis=1, keepdims=True))
            grad = c_ref[...].astype(F32) + grad
            grad_out[...] = grad
            low_out[...] = grad.astype(BF16)

    strip = spec((wide, tile), lambda n: (0, n))
    column = spec((rows, tile), lambda n: (0, n))
    whole = spec((rows, wide))
    return kernel_call(
        body,
        (steps,),
        [
            (normed_two, whole),
            (cotangent, whole),
            (w_both, strip),
            (w_both, spec((wide, tile), lambda n: (0, n + steps))),
            (w_down, spec((tile, wide), lambda n: (n, 0))),
            (hidden, whole),
            (gain, spec((1, wide))),
        ],
        [
            ((rows, wide), BF16, whole),
            ((rows, inner), BF16, column),
            ((rows, inner), BF16, column),
            ((rows, inner), BF16, column),
            ((rows, wide), F32, whole),
            ((rows, wide), BF16, whole),
        ],
        [pltpu.VMEM((rows, wide), F32), pltpu.VMEM((rows, wide), F32)],
    )


def head_back(grad_low, weights, mixed, swish, head_gain, queries, gate_pre, decays, marks):
    rows, wide = mixed.shape
    heads = wide // HEAD_K

    def body(gh_ref, wo, mixed_ref, swish_ref, hg_ref, q_ref, g_ref, d_ref, marks_ref, gm_out, gs_out, hg_out, m_out):
        grad = nt(gh_ref[...], wo[...])
        mixed = mixed_ref[...]
        swish = swish_ref[...]
        soft = sigmoid(swish)
        silu = swish * soft
        norm = lax.rsqrt(jnp.mean(mixed * mixed, axis=1, keepdims=True) + 1e-05)
        unit = mixed * norm
        gain = hg_ref[...]
        gs_out[...] = (grad * unit * gain * (soft * (1.0 + swish * (1.0 - soft)))).astype(BF16)
        by_gain = jnp.sum(grad * unit * silu, axis=0, keepdims=True)

        @pl.when(pl.program_id(0) == 0)
        def _():
            hg_out[...] = by_gain

        @pl.when(pl.program_id(0) > 0)
        def _():
            hg_out[...] += by_gain

        inner = grad * gain * silu
        grad_mixed = norm * (inner - unit * jnp.mean(inner * unit, axis=1, keepdims=True))
        gm_out[...] = grad_mixed.astype(BF16)
        along = summed(triangle(rows, lambda i, j: j <= i), log_decay(g_ref[...]))
        query_in = (scaled(q_ref[...]) * jnp.exp(along)).astype(BF16)
        m_out[0, :HEAD_V] = tn((grad_mixed * marks_ref[:, 3:4]).astype(BF16), query_in).astype(BF16)
        m_out[0, HEAD_V:] = d_ref[0]

    return kernel_call(
        body,
        (heads,),
        [
            (grad_low, spec((rows, wide))),
            (weights, spec((HEAD_V, wide), lambda h: (h, 2))),
            (mixed, by_head(rows)),
            (swish, by_head(rows)),
            (head_gain, spec((1, HEAD_V))),
            (queries, by_head(rows)),
            (gate_pre, by_head(rows)),
            (decays, spec((1, MESSAGE - HEAD_V, HEAD_K), lambda h: (h, 0, 0))),
            (marks, spec(marks.shape)),
        ],
        [
            ((rows, wide), BF16, by_head(rows)),
            ((rows, wide), BF16, by_head(rows)),
            ((1, HEAD_V), F32, spec((1, HEAD_V))),
            ((heads, MESSAGE, HEAD_K), BF16, spec((1, MESSAGE, HEAD_K), lambda h: (h, 0, 0))),
        ],
    )


def mixer_back(queries, keys, values, gate_pre, grad_mixed, states, leaving, first, marks, doc_row, rank):
    rows, wide = queries.shape
    heads = wide // HEAD_K
    blocks = rows // GROUP

    def body(
        q_ref, k_ref, v_ref, g_ref, gm_ref, s_ref, l_ref, ro, marks_ref, doc_ref,
        gq_out, gk_out, gv_out, gg_out, low_out, state_grad, slope, low,
    ):
        h = pl.program_id(0)
        gate = g_ref[...]
        along = summed(triangle(rows, lambda i, j: j <= i, GROUP), log_decay(gate))
        state_grad[...] = l_ref[0].astype(F32)
        causal = triangle(GROUP, lambda i, j: j <= i) > 0
        onward = triangle(GROUP, lambda i, j: j >= i)
        for n in reversed(range(blocks)):
            at = slice(n * GROUP, (n + 1) * GROUP)
            marks_n = marks_ref[at]
            run = along[at]
            end = run[GROUP - 1 :]
            key = k_ref[at].astype(F32)
            value = v_ref[at]
            grad = gm_ref[at]
            entering = marks_n[:, 1:2]
            up, down = jnp.exp(run), jnp.exp(-run)
            out = jnp.exp(end - run) * marks_n[:, 2:3]
            query_in = (scaled(q_ref[at]) * up).astype(BF16)
            key_in = (key * down).astype(BF16)
            key_out = (key * out).astype(BF16)
            allowed = causal & (marks_n[:, 0:1] == doc_ref[:, at])
            scores = jnp.where(allowed, nt(query_in, key_in), 0.0).astype(BF16)
            grad_scores = jnp.where(allowed, nt(grad, value), 0.0).astype(BF16)
            leaving = state_grad[...].astype(BF16)
            grad_query = nn(grad_scores, key_in) + entering * nn(grad, s_ref[0, n])
            grad_key_in = tn(grad_scores, query_in)
            grad_key_out = nn(value, leaving)
            gv_out[at] = (tn(scores, grad) + nt(key_out, leaving)).astype(BF16)
            gq_out[at] = (grad_query * up * HEAD_K ** (-0.5)).astype(BF16)
            gk_out[at] = (grad_key_in * down + grad_key_out * out).astype(BF16)
            change = (
                query_in.astype(F32) * grad_query
                - key_in.astype(F32) * grad_key_in
                - key_out.astype(F32) * grad_key_out
            )
            closing = jnp.sum(s_ref[0, n + 1].astype(F32) * leaving.astype(F32), axis=0, keepdims=True)
            slope[at] = summed(onward, change) + closing
            kept = marks_n[GROUP - 1 :, 1:2] * jnp.exp(end)
            state_grad[...] = kept * state_grad[...] + tn(grad, (query_in.astype(F32) * entering).astype(BF16))
        grad_gate = (slope[...] * sigmoid(-gate) * (1.0 / 16.0)).astype(BF16)
        gg_out[...] = grad_gate
        part = nn(grad_gate, ro[...])

        @pl.when(h == 0)
        def _():
            low[...] = part

        @pl.when(h > 0)
        def _():
            low[...] += part

        @pl.when(h == heads - 1)
        def _():
            row = lax.broadcasted_iota(jnp.int32, (LANES, LANES), 0)
            lane = lax.broadcasted_iota(jnp.int32, (LANES, LANES), 1)
            move = jnp.where((row == lane + rank) & (lane < rank), 1.0, 0.0).astype(BF16)
            low_out[...] = nn(low[...].astype(BF16), move).astype(BF16)

    return kernel_call(
        body,
        (heads,),
        [
            (queries, by_head(rows)),
            (keys, by_head(rows)),
            (values, by_head(rows)),
            (gate_pre, by_head(rows)),
            (grad_mixed, by_head(rows)),
            (states, spec((1, blocks + 1, HEAD_V, HEAD_K), lambda h: (h, 0, 0, 0))),
            (leaving, spec((1, HEAD_V, HEAD_K), lambda h: (h, 0, 0))),
            (first, spec((HEAD_K, LANES), lambda h: (h, 2 * wide // LANES))),
            (marks, spec(marks.shape)),
            (doc_row, spec(doc_row.shape)),
        ],
        [((rows, wide), BF16, by_head(rows))] * 4 + [((rows, LANES), BF16, spec((rows, LANES)))],
        [pltpu.VMEM((HEAD_V, HEAD_K), F32), pltpu.VMEM((rows, HEAD_K), F32), pltpu.VMEM((rows, LANES), F32)],
    )


def input_back(grads, first, second, grad_rank, tokens, gain, grad_hidden):
    rows, wide = tokens.shape
    heads = wide // HEAD_K
    places = ((second, 0), (first, 0), (first, heads), (second, heads))

    def body(*refs):
        grad_refs, weight_refs = refs[:4], refs[4:8]
        low_ref, table, x_ref, gain_ref, gh_ref, out_ref, total = refs[8:]
        h = pl.program_id(0)
        part = nt(grad_refs[0][...], weight_refs[0][...])
        for g, w in zip(grad_refs[1:], weight_refs[1:]):
            part = part + nt(g[...], w[...])

        @pl.when(h == 0)
        def _():
            total[...] = part + nt(low_ref[...], table[...])

        @pl.when(h > 0)
        def _():
            total[...] += part

        @pl.when(h == heads - 1)
        def _():
            x = x_ref[...].astype(F32)
            scale = lax.rsqrt(jnp.mean(x * x, axis=1, keepdims=True) + 1e-06)
            unit = x * scale
            grad = total[...] * gain_ref[...]
            out_ref[...] = gh_ref[...] + scale * (grad - unit * jnp.mean(grad * unit, axis=1, keepdims=True))

    def strip(start):
        return spec((wide, HEAD_K), lambda h: (0, start + h))

    whole = spec((rows, wide))
    return kernel_call(
        body,
        (heads,),
        [(g, by_head(rows)) for g in grads]
        + [(w, strip(start)) for w, start in places]
        + [
            (grad_rank, spec((rows, LANES))),
            (first, spec((wide, LANES), lambda h: (0, 2 * wide // LANES))),
            (tokens, whole),
            (gain, spec((1, wide))),
            (grad_hidden, whole),
        ],
        [((rows, wide), F32, whole)],
        [pltpu.VMEM((rows, wide), F32)],
    )[0]


def then(earlier, later):
    scale = later[:, HEAD_V:].astype(F32)
    state = scale[:, :1] * earlier[:, :HEAD_V].astype(F32) + later[:, :HEAD_V].astype(F32)
    return jnp.concatenate([state, scale * earlier[:, HEAD_V:].astype(F32)], axis=1).astype(BF16)


def nothing(like):
    return jnp.concatenate([jnp.zeros_like(like[:, :HEAD_V]), jnp.ones_like(like[:, HEAD_V:])], axis=1)


class Passing:
    def __init__(self, message, backward=False):
        _, y, x, c = place()
        height = lax.axis_size("y")
        self.core, self.sign = c, -1 if backward else 1
        if backward:
            y, x, c = height - 1 - y, 1 - x, 1 - c
        self.y, self.x, self.c = y, x, c
        heads = message.shape[0]
        self.other = flip(message, "c")
        both = jnp.where(c == 0, then(message, self.other), then(self.other, message))
        self.mine = lax.dynamic_slice_in_dim(both, self.core * (heads // 2), heads // 2, 0)

    def by_x(self, done=()):
        self.beside = flip(after(done, self.mine), "x")
        return self.beside

    def by_y(self, done=()):
        beside, mine = after(done, self.beside, self.mine)
        self.before = jnp.where(self.x == 1, beside, nothing(mine))
        self.line = jnp.where(self.x == 1, then(beside, mine), then(mine, beside))
        self.far = [shift(self.line, "y", self.sign * j) for j in range(1, lax.axis_size("y"))]
        return self.far

    def entering(self, done=()):
        before, distant = after(done, self.before, self.far)
        for j, far in enumerate(distant):
            before = jnp.where(self.y > j, then(far, before), before)
        rest = flip(before, "c")
        chip = jnp.where(self.core == 0, jnp.concatenate([before, rest]), jnp.concatenate([rest, before]))
        return jnp.where(self.c == 1, then(chip, self.other), chip)[:, :HEAD_V]


def pair(value):
    return (value, flip(value, "c"))


def document_of(positions, starts):
    return jnp.sum((starts[None, :] <= positions[:, None]).astype(jnp.int32), axis=1) - 1


def documents(starts, rows):
    _, y, x, c = place()
    positions = ((y * 2 + x) * 2 + c) * rows + jnp.arange(rows, dtype=jnp.int32)
    doc = document_of(positions, starts)
    before = document_of(positions - 1, starts)
    blocks = doc.reshape(-1, GROUP)
    entering = (blocks == before.reshape(-1, GROUP)[:, :1]).reshape(-1)
    tail = (blocks == blocks[:, -1:]).reshape(-1)
    columns = [doc, entering, tail, doc == before[0], doc == doc[-1]]
    marks = jnp.stack([a.astype(F32) for a in columns] + [jnp.zeros((rows,), F32)] * 3, axis=1)
    return marks, doc.astype(F32).reshape(1, rows)


def pair(value):
    return (value, flip(value, "c"))


def shards(tokens, cotangent, doc_starts, *weights):
    (
        gain_one, w_query, w_key, w_value, w_swish, rank_in, rank_out, bias, head_gain, w_output, gain_two,
        w_gate, w_up, w_down,
    ) = weights
    rows, width = tokens.shape
    own, rank, ff = w_query.shape[0], rank_in.shape[1], w_gate.shape[1]
    devices = width // own
    _, _, _, c = place()

    table_columns = 2 * width + LANES
    square_weights = jnp.concatenate([w_query, w_swish, w_output], axis=1)

    w_both = lax.all_gather(jnp.concatenate([w_gate, w_up], axis=1), AXES, axis=0, tiled=True)
    first = first_weights(w_key, w_value, rank_in, rank_out, (bias, gain_one, gain_two, head_gain))
    marks, doc_row = documents(doc_starts[0], rows)
    fast = square_plane() and own % 16 == 0
    depth = lax.axis_size("z")
    if fast:
        one = jnp.stack([first] + [shift(first, "z", k) for k in range(1, depth)])
        half = width // 2
        keep = lax.dynamic_slice_in_dim(w_down, c * half, half, 1)
        other = flip(lax.dynamic_slice_in_dim(w_down, (1 - c) * half, half, 1), "c")
        chip_down = jnp.where(c == 0, jnp.concatenate([keep, other]), jnp.concatenate([other, keep]))
        chip_down, square_weights = after(one, chip_down, square_weights)
        one_early, one_late = cross(one, False), cross(one, True)
        two = [shift(square_weights, "z", k) for k in range(1, depth, 2)]
        now = (one_early, one_late, two)
        square_more, one_next = after(now, square_weights, one_early)
        one_corner = cross(one_next, True)
        two_more = [shift(square_more, "z", k) for k in range(2, depth, 2)]
        now = (one_corner, two_more)
        chip_down, one = after(now, chip_down, one)
        three = [shift(chip_down, "z", k) for k in range(1, depth, 2)]
        first = assemble(gathered(one, one_early, one_late, one_corner), own, (width, table_columns))

        def mixed_order(base, odd, even):
            return jnp.stack([base] + [(odd if k % 2 else even)[(k - 1) // 2] for k in range(1, depth)])

        two = mixed_order(square_weights, two, two_more)
        now = (first, three)
        first, two, chip_down = after(now, first, two, chip_down)
        two_early = cross(two, False)
        three_more = [shift(chip_down, "z", k) for k in range(2, depth, 2)]
        three = mixed_order(chip_down, three, three_more)
    else:
        first = lax.all_gather(first, AXES, axis=0, tiled=True)
        second = lax.all_gather(square_weights, AXES, axis=0, tiled=True)
        w_down_all = lax.all_gather(w_down, AXES, axis=0, tiled=True)
    normed, low, keys, values, gate_pre, message, vectors = project(tokens, first, marks, rank)
    row_one, row_two = vectors[1:2], vectors[2:3]
    row_head = vectors[3].reshape(devices, own)[:, : head_gain.shape[0]].reshape(1, HEAD_V)
    if fast:
        message, two, two_early = after(three, message, two, two_early)
    passing = Passing(message)
    if fast:
        two_late = cross(after(passing.mine, two), True)
        now = (passing.by_x(), two_late)
        two_corner = cross(after(now, two_early), True)
        now = (passing.by_y(now), two_corner)
        three = after(now, three)
        three_early = cross(three, False)
        second = assemble(gathered(two, two_early, two_late, two_corner), own, (width, 3 * width))
        now = (passing.entering(now), three_early, second)
        entered, second, three, three_early = after(now, now[0], second, three, three_early)
        three_late, three_corner = cross(three, True), cross(three_early, True)
    else:
        passing.by_x()
        passing.by_y()
        entered = passing.entering()
    both = pair(normed)
    queries, mixed, swish, gated, hidden, normed_two, states = mixer(
        normed, keys, values, gate_pre, entered, second, row_head, tokens, row_two, marks, doc_row
    )
    if fast:
        hidden, three = after((three_late, three_corner), hidden, three)
        w_down_all = assemble(
            gathered(three, three_early, three_late, three_corner), chip_down.shape[0], (ff, width), True
        )
    output, inner, grad_gate, grad_up, grad_hidden, grad_low = feed(
        normed_two, cotangent, w_both, w_down_all, hidden, row_two
    )

    down = weight_grads([(pair(inner), [pair(cotangent)])], 512, True)
    grad_low, gate_pair, up_pair, two_pair = after(down.blocks, grad_low, pair(grad_gate), pair(grad_up), pair(normed_two))
    grad_mixed, grad_swish, grad_head_gain, message_back = head_back(
        grad_low, second, mixed, swish, row_head, queries, gate_pre, message[:, HEAD_V:], marks
    )
    now = (down.first(), message_back)
    passing = Passing(after(now, message_back), True)
    now = passing.mine
    two_pair, gate_pair = after(now, two_pair, gate_pair)
    gate = weight_grads([(two_pair, [gate_pair])], ff // 2)
    now = (passing.by_x(), down.second(now), gate.blocks)
    up = weight_grads([after(now, (two_pair, [up_pair]))], ff // 2)
    now = (passing.by_y(now), gate.first(now), up.blocks)
    leaving = passing.entering(now)
    now = leaving
    down_sum = down.third(now)
    grad_query, grad_key, grad_value, grad_gate_pre, grad_rank = mixer_back(
        queries, keys, values, gate_pre, grad_mixed, states, leaving, first, marks, doc_row, rank
    )
    now = (up.first(now), grad_query)
    inside_pairs = [pair(a) for a in after(now, grad_query, grad_key, grad_value, grad_rank, grad_gate_pre)]
    swish_pair = after(now, pair(grad_swish))
    middle = weight_grads([(both, [swish_pair]), (pair(gated), [pair(grad_low)])], width)
    now = (inside_pairs, middle.blocks, gate.second(now))
    head_terms = grad_head_gain + flip(grad_head_gain, "c")
    head_terms = jnp.pad(head_terms.reshape(devices, -1), ((0, 0), (0, own - head_gain.shape[0]))).reshape(width, 1)
    base = jnp.pad(head_terms.astype(BF16), ((0, 0), (2 * rank + 3, LANES - 2 * rank - 4)))
    inside_pairs = after(now, inside_pairs)
    inside = weight_grads(
        [(both, inside_pairs[:3])],
        width,
        table=([(both, inside_pairs[3]), (inside_pairs[4], pair(low))], base),
    )
    gate_sum = gate.third(now)
    now = (inside.blocks, up.second(now), middle.first(now))
    input_grad = input_back(
        (grad_query, grad_key, grad_value, grad_swish), first, second, after(now, grad_rank), tokens, row_one,
        grad_hidden,
    )
    up_sum = up.third(now)
    now = (input_grad, inside.first(now), middle.second(now))
    inside.second(now)
    middle_sum = middle.third(now)
    inside_sum = inside.third()

    chip_half = ff // devices
    keep = lax.dynamic_slice_in_dim(down_sum, c * chip_half, chip_half, 0)
    other = flip(lax.dynamic_slice_in_dim(down_sum, (1 - c) * chip_half, chip_half, 0), "c")
    down_sum = jnp.where(c == 0, jnp.concatenate([keep, other], 1), jnp.concatenate([other, keep], 1))
    g_query, g_key, g_value = (inside_sum[:, n * width : (n + 1) * width] for n in range(3))
    g_swish, g_output = middle_sum[:, :width], middle_sum[:, width:]
    g_rank_in, g_rank_out, g_bias, g_head = (
        inside_sum[:, 3 * width + a : 3 * width + b]
        for a, b in ((0, rank), (rank, 2 * rank), (2 * rank, 2 * rank + 1), (2 * rank + 3, 2 * rank + 4))
    )
    g_gate, g_up = gate_sum, up_sum

    def gain_grad(gain, *terms):
        return sum(jnp.sum(wide(w) * g, axis=1) for w, g in terms) / wide(gain)

    g_gain_one = gain_grad(
        gain_one, (w_query, g_query), (w_key, g_key), (w_value, g_value), (w_swish, g_swish), (rank_in, g_rank_in)
    )
    g_gain_two = gain_grad(gain_two, (w_gate, g_gate), (w_up, g_up))
    return (
        output, input_grad, g_gain_one, g_query, g_key, g_value, g_swish, g_rank_in, g_rank_out.T, g_bias[:, 0],
        g_head[: head_gain.shape[0], 0], g_output, g_gain_two, g_gate, g_up, down_sum,
    )


def solution(mesh):
    fsdp, seq = mesh.shape["fsdp"], mesh.shape["seq"]
    inner = Mesh(mesh.devices.reshape(fsdp, seq // 4, 2, 2), AXES)
    rows, vector, columns = P(AXES, None), P(AXES), P(None, AXES)
    in_specs = (rows, rows, P("z", None), vector, rows, rows, rows, rows, rows, columns, vector, vector, rows, vector) + (rows,) * 3
    out_specs = (rows, rows, vector) + (rows,) * 5 + (columns, vector, vector, rows, vector) + (rows,) * 3
    return jax.shard_map(shards, mesh=inner, in_specs=in_specs, out_specs=out_specs, check_vma=False)
```

```python
from functools import partial

import jax
import jax.numpy as jnp
from jax import lax
from jax.experimental import pallas as pl
from jax.experimental.pallas import tpu as pltpu
from jax.sharding import Mesh
from jax.sharding import PartitionSpec as P

HEAD_K = 256
HEAD_V = 256
GROUP = 64
LANES = 128
TOGETHER = 2
AXES = ("z", "y", "x", "c")
VMEM = 56 * 1024 * 1024
QUICK = pl.CostEstimate(flops=0, bytes_accessed=0, transcendentals=0)
F32 = jnp.float32
BF16 = jnp.bfloat16


def shift(value, axis, step):
    size = lax.axis_size(axis)
    return lax.ppermute(value, axis, [(i, (i + step) % size) for i in range(size)])


def flip(value, axis):
    return shift(value, axis, 1)


def place():
    return tuple(lax.axis_index(a) for a in AXES)


def after(done, *values):
    out = lax.optimization_barrier((values, done))[0]
    return out[0] if len(values) == 1 else out


def square_plane():
    return lax.axis_size("y") == 2


def cross(value, late):
    perm = [(i, i ^ (2 if (i % 2 == 0) != late else 4)) for i in range(8)]
    return lax.ppermute(value, ("y", "x", "c"), perm)


def neighbour(early, late, core):
    _, y, x, _ = place()
    by_x = jnp.where(core == 0, early, late)
    by_y = jnp.where(core == 0, late, early)
    return (y + by_y) % 2, (x + by_x) % 2


def gathered(own, early, late, corner):
    pieces = [(own, 0, 0, 0), (early, 1, 0, 0), (late, 0, 1, 0), (corner, 1, 1, 0)]
    return pieces + [(flip(a, "c"), i, j, 1) for a, i, j, _ in pieces]


def sources(pieces):
    z, _, _, c = place()
    depth = lax.axis_size("z")
    chips, cores = [], []
    for _, early, late, other in pieces:
        core = (c + other) % 2
        y, x = neighbour(early, late, core)
        for k in range(depth):
            chips.append((((z - k) % depth) * 2 + y) * 2 + x)
            cores.append(core)
    return jnp.stack(chips + cores).astype(jnp.int32)


def assemble(pieces, rows, shape, by_columns=False):
    where = sources(pieces)
    arrays = [p[0] for p in pieces]
    depth = arrays[0].shape[0]
    blocks = [(n, k) for n in range(len(pieces)) for k in range(depth)]
    total = len(blocks)

    def body(where_ref, *refs):
        ins, out, sem = refs[: len(arrays)], refs[-2], refs[-1]
        for at, (n, k) in enumerate(blocks):
            chip, core = where_ref[at], where_ref[total + at]
            if by_columns:
                width = shape[1] // 2
                goal = out.at[
                    pl.ds(pl.multiple_of(chip * rows, rows), rows),
                    pl.ds(pl.multiple_of(core * width, width), width),
                ]
            else:
                goal = out.at[pl.ds(pl.multiple_of((chip * 2 + core) * rows, rows), rows), :]
            pltpu.make_async_copy(ins[n].at[k], goal, sem).start()
        pltpu.make_async_copy(out, out, sem).wait()

    return pl.pallas_call(
        body,
        grid_spec=pltpu.PrefetchScalarGridSpec(
            num_scalar_prefetch=1,
            grid=(1,),
            in_specs=[pl.BlockSpec(memory_space=pl.ANY)] * len(arrays),
            out_specs=pl.BlockSpec(shape, lambda n, s: (0, 0)),
            scratch_shapes=[pltpu.SemaphoreType.DMA],
        ),
        out_shape=jax.ShapeDtypeStruct(shape, BF16),
        compiler_params=pltpu.CompilerParams(vmem_limit_bytes=VMEM),
        cost_estimate=QUICK,
    )(where, *arrays)


def layout():
    _, _, _, c = place()
    depth, height = lax.axis_size("z"), lax.axis_size("y")
    if not square_plane():
        return [jnp.arange(depth * height * 2, dtype=jnp.int32)]

    def column(early, late):
        y, x = neighbour(early, late, c)
        return (jnp.arange(depth, dtype=jnp.int32) * 2 + y) * 2 + x

    return [jnp.concatenate([column(1, 0), column(1, 1)]), column(0, 1), column(0, 0)]


def wide(a):
    return a.astype(F32)


class Sum:
    def __init__(self, blocks):
        self.blocks = blocks

    def first(self, done=()):
        self.arrived = cross(after(done, self.blocks[0]), False) if square_plane() else ()
        return self.arrived

    def second(self, done=(), *others):
        parts = (self, *others)
        if not square_plane():
            for p in parts:
                p.through = ()
            return ()
        depth = lax.axis_size("z")
        sums = []
        for p in parts:
            arrived, kept = after(done, p.arrived, p.blocks[1])
            sums.append((wide(kept) + wide(arrived[depth:])).astype(BF16))
        through = cross(sums[0] if len(sums) == 1 else jnp.concatenate(sums, axis=2), True)
        at = 0
        for p, part in zip(parts, sums):
            p.through = through[:, :, at : at + part.shape[2]]
            at += part.shape[2]
        return through

    def total(self):
        depth = lax.axis_size("z")
        return (wide(self.blocks[2]) + wide(self.arrived[:depth]) + wide(self.through)).astype(BF16)

    def third(self, *others):
        parts = (self, *others)
        if square_plane():
            axes, totals = "z", [p.total() for p in parts]
        else:
            axes, totals = ("z", "y", "x"), [p.blocks[0] for p in parts]
        total = totals[0] if len(totals) == 1 else jnp.concatenate(totals, axis=2)
        return lax.psum_scatter(total.reshape(-1, total.shape[-1]), axes, scatter_dimension=0, tiled=True)

    def third_terms(self):
        if not square_plane():
            return [self.third()]
        depth = lax.axis_size("z")
        total, z = self.total(), lax.axis_index("z")
        block = [lax.dynamic_index_in_dim(total, (z + k) % depth, 0, False) for k in range(depth)]
        return [block[0]] + [shift(block[k], "z", k) for k in range(1, depth)]


def weight_grads(groups, tile, halves=False, table=None):
    _, _, _, c = place()
    chips = layout()
    spans = [a.shape[0] for a in chips]
    chips = jnp.concatenate(chips)
    count = chips.shape[0]
    lefts = [left for left, _ in groups]
    rights = [right for _, group in groups for right in group]
    owner = [n for n, (_, group) in enumerate(groups) for _ in group]
    height, tokens = lefts[0][0].shape
    each = rights[0][0].shape[1] // (2 if halves else 1)
    width = each * len(rights)
    rows = height // (count if halves else 2 * count)
    starts = chips * rows if halves else (chips * 2 + c) * rows

    if rows % 16:
        products = []
        for n, right in zip(owner, rights):
            product = nn(jnp.concatenate(lefts[n], axis=1), jnp.concatenate(right)).astype(BF16)
            if halves:
                product = lax.dynamic_slice_in_dim(product, c * each, each, 1).reshape(count, rows, each)
            else:
                product = lax.dynamic_index_in_dim(product.reshape(count, 2, rows, each), c, 1, False)
            products.append(product)
        if table is not None:
            product = wide(table[1])
            for left, right in table[0]:
                product = product + nn(jnp.concatenate(left, axis=1), jnp.concatenate(right))
            product = product.astype(BF16).reshape(count, 2, rows, LANES)
            products.append(lax.dynamic_index_in_dim(product, c, 1, False))
        product = jnp.take(jnp.concatenate(products, axis=2), chips, axis=0)
        blocks, at = [], 0
        for span in spans:
            blocks.append(product[at : at + span])
            at += span
        return Sum(blocks)

    strips = each // tile
    first_tile = c * strips if halves else jnp.int32(0)
    numbers = jnp.concatenate([starts, first_tile[None]]).astype(jnp.int32)

    steps = width // tile
    terms, base = table if table is not None else ((), None)
    flat = [a for left in lefts for a in left] + [a for right in rights for a in right]
    narrow = [a for left, right in terms for a in (*left, *right)]
    if table is not None:
        narrow.append(base)

    def body(numbers_ref, *refs):
        left_refs, right_refs = refs[: 2 * len(lefts)], refs[2 * len(lefts) : len(flat)]
        narrow_refs = refs[len(flat) : len(flat) + len(narrow)]
        outs, (chosen, total, based) = refs[len(flat) + len(narrow) : -3], refs[-3:]
        step = pl.program_id(0)

        def start(at):
            return pl.ds(pl.multiple_of(numbers_ref[at], 16), rows)

        def choose(lo_ref, ls_ref):
            for at in range(count):
                chosen[at * rows : (at + 1) * rows, :tokens] = lo_ref[start(at), :]
                chosen[at * rows : (at + 1) * rows, tokens:] = ls_ref[start(at), :]

        def put(product, columns):
            at = 0
            for out, span in zip(outs, spans):
                out[:, :, :columns] = product[at : at + span * rows].reshape(span, rows, columns)
                at += span * rows

        def strip(ro_ref, rs_ref):
            both = jnp.concatenate([ro_ref[...], rs_ref[...]], axis=0)
            put(nn(chosen[...], both).astype(BF16), tile)

        def term(n):
            lo_ref, ls_ref, ro_ref, rs_ref = narrow_refs[4 * n : 4 * n + 4]
            choose(lo_ref, ls_ref)
            both = jnp.concatenate([ro_ref[...], rs_ref[...]], axis=0)
            product = nn(chosen[...], both)
            if n == 0:
                total[...] = product
            else:
                total[...] += product
            if n == len(terms) - 1:
                for at in range(count):
                    based[at * rows : (at + 1) * rows, :] = narrow_refs[-1][start(at), :]
                put((total[...] + wide(based[...])).astype(BF16), LANES)

        for n in range(len(lefts)):
            pl.when(step == owner.index(n) * strips)(partial(choose, *left_refs[2 * n : 2 * n + 2]))
        if len(rights) == 1:
            strip(*right_refs)
        else:
            for n in range(len(rights)):
                pl.when(step // strips == n)(partial(strip, *right_refs[2 * n : 2 * n + 2]))
        for n in range(len(terms)):
            pl.when(step == steps + n)(partial(term, n))

    def column(n):
        return lambda step, s: (0, jnp.clip(step - n * strips, 0, strips - 1) + s[count])

    def full(a):
        return pl.BlockSpec(a.shape, lambda n, s: (0,) * a.ndim)

    right_specs = [pl.BlockSpec((tokens, tile), column(n)) for n in range(len(rights)) for _ in range(2)]
    columns = width + (LANES if table is not None else 0)
    last = steps - (table is None)
    outs = [(span, rows, columns) for span in spans]
    blocks = pl.pallas_call(
        body,
        grid_spec=pltpu.PrefetchScalarGridSpec(
            num_scalar_prefetch=1,
            grid=(steps + len(terms),),
            in_specs=[full(a) for left in lefts for a in left] + right_specs + [full(a) for a in narrow],
            out_specs=[pl.BlockSpec((n, rows, tile), lambda n, s: (0, 0, jnp.minimum(n, last))) for n, _, _ in outs],
            scratch_shapes=[
                pltpu.VMEM((count * rows, 2 * tokens), BF16),
                pltpu.VMEM((count * rows, LANES), F32),
                pltpu.VMEM((count * rows, LANES), BF16),
            ],
        ),
        out_shape=[jax.ShapeDtypeStruct(o, BF16) for o in outs],
        compiler_params=pltpu.CompilerParams(vmem_limit_bytes=VMEM),
        cost_estimate=QUICK,
    )(numbers, *flat, *narrow)
    return Sum(blocks)


def nn(left, right):
    return jnp.dot(left, right, preferred_element_type=F32)


def nt(left, right):
    return lax.dot_general(left, right, (((1,), (1,)), ((), ())), preferred_element_type=F32)


def tn(left, right):
    return lax.dot_general(left, right, (((0,), (0,)), ((), ())), preferred_element_type=F32)


def summed(ones, values):
    high = values.astype(BF16)
    low = (values - high.astype(F32)).astype(BF16)
    return nn(ones, high) + nn(ones, low)


def triangle(size, relation, block=None):
    row = lax.broadcasted_iota(jnp.int32, (size, size), 0)
    column = lax.broadcasted_iota(jnp.int32, (size, size), 1)
    chosen = relation(row, column)
    if block is not None:
        chosen = chosen & (row // block == column // block)
    return jnp.where(chosen, 1.0, 0.0).astype(BF16)


def log_decay(gate_pre):
    return (jnp.minimum(gate_pre, 0.0) - jnp.log1p(jnp.exp(-jnp.abs(gate_pre)))) * (1.0 / 16.0)


def sigmoid(v):
    return 1.0 / (1.0 + jnp.exp(-v))


def spec(shape, index=None):
    index = index or (lambda *_: (0,) * len(shape))
    return pl.BlockSpec(shape, index)


def by_head(rows, start=0):
    return spec((rows, TOGETHER * HEAD_K), lambda h: (0, start + h))


def spans(count=TOGETHER):
    return [slice(n * HEAD_K, (n + 1) * HEAD_K) for n in range(count)]


def by_spans(function, *arrays):
    return jnp.concatenate([function(*[a[:, at] for a in arrays]) for at in spans()], axis=1)


def head_mean(values):
    return by_spans(lambda a: jnp.broadcast_to(jnp.mean(a, axis=1, keepdims=True), a.shape), values)


def repeated(row):
    return jnp.concatenate([row] * TOGETHER, axis=1)


def kernel_call(body, grid, ins, outs, scratch=()):
    return pl.pallas_call(
        body,
        grid=grid,
        in_specs=[s for _, s in ins],
        out_specs=[s for _, _, s in outs],
        out_shape=[jax.ShapeDtypeStruct(shape, dtype) for shape, dtype, _ in outs],
        scratch_shapes=list(scratch),
        compiler_params=pltpu.CompilerParams(vmem_limit_bytes=VMEM),
        cost_estimate=QUICK,
    )(*[a for a, _ in ins])


MESSAGE = HEAD_V + 16


def unit_columns(rows, columns, start):
    row = lax.broadcasted_iota(jnp.int32, (rows, columns), 0)
    column = lax.broadcasted_iota(jnp.int32, (rows, columns), 1)
    return jnp.where(column == row + start, 1.0, 0.0).astype(BF16)


def first_weights(w_key, w_value, turned_in, rank_out, vectors):
    rows, width = w_key.shape
    rank = turned_in.shape[0]

    def body(wk, wv, ri, ro, *refs):
        vector_refs, out = refs[:-1], refs[-1]
        out[:, :width] = wk[...]
        out[:, width : 2 * width] = wv[...]
        table = tn(ri[...], unit_columns(rank, LANES, 0)) + tn(ro[...], unit_columns(rank, LANES, rank))
        for n, v in enumerate(vector_refs):
            mine = unit_columns(v.shape[1], rows, 0)
            table = table + tn(nn(v[...], mine).astype(BF16), unit_columns(1, LANES, 2 * rank + n))
        out[:, 2 * width :] = table.astype(BF16)

    ins = [w_key, w_value, turned_in, rank_out, *[v.reshape(1, -1) for v in vectors]]
    shape = (rows, 2 * width + LANES)
    return kernel_call(body, (1,), [(a, spec(a.shape)) for a in ins], [(shape, BF16, spec(shape))])[0]


def project(tokens, weights, marks, rank):
    rows, width = tokens.shape
    heads = width // HEAD_K
    steps = heads // TOGETHER
    at_table = 2 * width // LANES

    def body(
        x_ref, wk, wv, table, part_ref, marks_ref, n_out, turned_out, low_out, k_out, v_out, g_out, m_out, vectors_out
    ):
        @pl.when(pl.program_id(0) == 0)
        def _():
            vectors = nt(unit_columns(8, LANES, 2 * rank), table[...])
            vectors_out[...] = vectors
            x = x_ref[...].astype(F32)
            scale = lax.rsqrt(jnp.mean(x * x, axis=1, keepdims=True) + 1e-06)
            n_out[...] = (x * scale * vectors[1:2]).astype(BF16)
            turned_out[...] = n_out[...].T
            low = nn(n_out[...], table[...]).astype(BF16)
            lane = lax.broadcasted_iota(jnp.int32, (LANES, LANES), 1)
            row = lax.broadcasted_iota(jnp.int32, (LANES, LANES), 0)
            move = jnp.where((lane == row + rank) & (row < rank), 1.0, 0.0).astype(BF16)
            one = jnp.where(lax.broadcasted_iota(jnp.int32, (rows, LANES), 1) == 2 * rank, 1.0, 0.0)
            low_out[...] = (nn(low, move) + one).astype(BF16)

        normed = n_out[...]
        key = nn(normed, wk[...]).astype(BF16)
        value = nn(normed, wv[...]).astype(BF16)
        k_out[...] = key
        v_out[...] = value
        gate = nt(low_out[...], part_ref[...])
        g_out[...] = gate
        decay = log_decay(gate)
        later = summed(triangle(rows, lambda i, j: j > i), decay)
        last = marks_ref[:, 4:5]
        finish = (key.astype(F32) * jnp.exp(later) * last).astype(BF16)
        total = jnp.exp(jnp.sum(decay, axis=0, keepdims=True)) * marks_ref[rows - 1 :, 3:4]
        for n, at in enumerate(spans()):
            m_out[n, :HEAD_V] = tn(value[:, at], finish[:, at]).astype(BF16)
            m_out[n, HEAD_V:] = jnp.broadcast_to(total[:, at], (MESSAGE - HEAD_V, HEAD_K)).astype(BF16)

    return kernel_call(
        body,
        (steps,),
        [
            (tokens, spec((rows, width))),
            (weights, by_head(width)),
            (weights, by_head(width, steps)),
            (weights, spec((width, LANES), lambda h: (0, at_table))),
            (weights, spec((TOGETHER * HEAD_K, LANES), lambda h: (h, at_table))),
            (marks, spec(marks.shape)),
        ],
        [
            ((rows, width), BF16, spec((rows, width))),
            ((width, rows), BF16, spec((width, rows))),
            ((rows, LANES), BF16, spec((rows, LANES))),
            ((rows, width), BF16, by_head(rows)),
            ((rows, width), BF16, by_head(rows)),
            ((rows, width), F32, by_head(rows)),
            ((heads, MESSAGE, HEAD_K), BF16, spec((TOGETHER, MESSAGE, HEAD_K), lambda h: (h, 0, 0))),
            ((8, width), F32, spec((8, width))),
        ],
    )


def scaled(queries):
    return queries.astype(F32) * HEAD_K ** (-0.5)


def mixer(normed, keys, values, gate_pre, entered, weights, head_gain, tokens, gain, marks, doc_row):
    rows, wide = tokens.shape
    heads = wide // HEAD_K
    steps = heads // TOGETHER
    blocks = rows // GROUP

    def body(
        n_ref, k_ref, v_ref, g_ref, s_ref, wq, ws, hg_ref, wo, x_ref, gain_ref, marks_ref, doc_ref,
        q_ref, mixed_out, swish_out, gated_out, hidden_out, two_out, two_turned, states_out, state, total,
    ):
        h = pl.program_id(0)
        q_ref[...] = nn(n_ref[...], wq[...]).astype(BF16)
        swish = nn(n_ref[...], ws[...])
        swish_out[...] = swish
        along = summed(triangle(rows, lambda i, j: j <= i, GROUP), log_decay(g_ref[...]))
        causal = triangle(GROUP, lambda i, j: j <= i) > 0
        run_all, key_all = along, k_ref[...].astype(F32)
        query_all = (scaled(q_ref[...]) * jnp.exp(run_all)).astype(BF16)
        key_in_all = (key_all * jnp.exp(-run_all)).astype(BF16)
        for head in range(TOGETHER):
            state[head] = s_ref[head].astype(F32)
        for n in range(blocks):
            at = slice(n * GROUP, (n + 1) * GROUP)
            marks_n = marks_ref[at]
            allowed = causal & (marks_n[:, 0:1] == doc_ref[:, at])
            run = run_all[at]
            end = run[GROUP - 1 :]
            key_out_all = (key_all[at] * jnp.exp(end - run) * marks_n[:, 2:3]).astype(BF16)
            kept = marks_n[GROUP - 1 :, 1:2] * jnp.exp(end)
            for head, lanes in enumerate(spans()):
                value = v_ref[at, lanes]
                query_in = query_all[at, lanes]
                scores = jnp.where(allowed, nt(query_in, key_in_all[at, lanes]), 0.0).astype(BF16)
                before = state[head].astype(BF16)
                states_out[head, n] = before
                mixed_out[at, lanes] = nn(scores, value) + marks_n[:, 1:2] * nt(query_in, before)
                state[head] = kept[:, lanes] * state[head] + tn(value, key_out_all[:, lanes])
        for head in range(TOGETHER):
            states_out[head, blocks] = state[head].astype(BF16)
        mixed = mixed_out[...]
        norm = lax.rsqrt(head_mean(mixed * mixed) + 1e-05)
        gated = (mixed * norm * repeated(hg_ref[...]) * (swish * sigmoid(swish))).astype(BF16)
        gated_out[...] = gated.T
        part = nn(gated, wo[...])

        @pl.when(h == 0)
        def _():
            total[...] = x_ref[...].astype(F32) + part

        @pl.when(h > 0)
        def _():
            total[...] += part

        @pl.when(h == steps - 1)
        def _():
            hidden = total[...]
            hidden_out[...] = hidden
            scale = lax.rsqrt(jnp.mean(hidden * hidden, axis=1, keepdims=True) + 1e-06)
            two_out[...] = (hidden * scale * gain_ref[...]).astype(BF16)
            two_turned[...] = two_out[...].T

    return kernel_call(
        body,
        (steps,),
        [
            (normed, spec((rows, wide))),
            (keys, by_head(rows)),
            (values, by_head(rows)),
            (gate_pre, by_head(rows)),
            (entered, spec((TOGETHER, HEAD_V, HEAD_K), lambda h: (h, 0, 0))),
            (weights, by_head(wide)),
            (weights, by_head(wide, steps)),
            (head_gain, spec((1, HEAD_V))),
            (weights, spec((TOGETHER * HEAD_V, wide), lambda h: (h, 2))),
            (tokens, spec((rows, wide))),
            (gain, spec((1, wide))),
            (marks, spec(marks.shape)),
            (doc_row, spec(doc_row.shape)),
        ],
        [
            ((rows, wide), BF16, by_head(rows)),
            ((rows, wide), F32, by_head(rows)),
            ((rows, wide), F32, by_head(rows)),
            ((wide, rows), BF16, spec((TOGETHER * HEAD_V, rows), lambda h: (h, 0))),
            ((rows, wide), F32, spec((rows, wide))),
            ((rows, wide), BF16, spec((rows, wide))),
            ((wide, rows), BF16, spec((wide, rows))),
            ((heads, blocks + 1, HEAD_V, HEAD_K), BF16, spec((TOGETHER, blocks + 1, HEAD_V, HEAD_K), lambda h: (h, 0, 0, 0))),
        ],
        [pltpu.VMEM((TOGETHER, HEAD_V, HEAD_K), F32), pltpu.VMEM((rows, wide), F32)],
    )


def feed(normed_two, cotangent, w_both, w_down, hidden, gain):
    rows, wide = hidden.shape
    inner = w_both.shape[1] // 2
    tile = inner // 2 if inner % 256 == 0 else inner
    steps = inner // tile

    def body(
        n_ref, c_ref, wg, wu, wd, hidden_ref, gain_ref,
        out_ref, inner_out, gate_out, up_out, grad_out, low_out, forward_sum, back_sum,
    ):
        step = pl.program_id(0)
        normed = n_ref[...]
        gate = nn(normed, wg[...])
        up = nn(normed, wu[...])
        soft = sigmoid(gate)
        silu = gate * soft
        product = (silu * up).astype(BF16)
        inner_out[...] = product.T
        grad = nt(c_ref[...], wd[...])
        grad_up = (grad * silu).astype(BF16)
        grad_gate = (grad * up * (soft * (1.0 + gate * (1.0 - soft)))).astype(BF16)
        up_out[...] = grad_up
        gate_out[...] = grad_gate
        ahead = nn(product, wd[...])
        back = nt(grad_gate, wg[...]) + nt(grad_up, wu[...])

        @pl.when(step == 0)
        def _():
            forward_sum[...] = hidden_ref[...] + ahead
            back_sum[...] = back

        @pl.when(step > 0)
        def _():
            forward_sum[...] += ahead
            back_sum[...] += back

        @pl.when(step == steps - 1)
        def _():
            out_ref[...] = forward_sum[...].astype(BF16)
            hidden = hidden_ref[...]
            scale = lax.rsqrt(jnp.mean(hidden * hidden, axis=1, keepdims=True) + 1e-06)
            unit = hidden * scale
            grad = back_sum[...] * gain_ref[...]
            grad = scale * (grad - unit * jnp.mean(grad * unit, axis=1, keepdims=True))
            grad = c_ref[...].astype(F32) + grad
            grad_out[...] = grad
            low_out[...] = grad.astype(BF16)

    strip = spec((wide, tile), lambda n: (0, n))
    column = spec((rows, tile), lambda n: (0, n))
    whole = spec((rows, wide))
    return kernel_call(
        body,
        (steps,),
        [
            (normed_two, whole),
            (cotangent, whole),
            (w_both, strip),
            (w_both, spec((wide, tile), lambda n: (0, n + steps))),
            (w_down, spec((tile, wide), lambda n: (n, 0))),
            (hidden, whole),
            (gain, spec((1, wide))),
        ],
        [
            ((rows, wide), BF16, whole),
            ((inner, rows), BF16, spec((tile, rows), lambda n: (n, 0))),
            ((rows, inner), BF16, column),
            ((rows, inner), BF16, column),
            ((rows, wide), F32, whole),
            ((rows, wide), BF16, whole),
        ],
        [pltpu.VMEM((rows, wide), F32), pltpu.VMEM((rows, wide), F32)],
    )


def head_back(grad_low, weights, mixed, swish, head_gain, queries, gate_pre, decays, marks):
    rows, wide = mixed.shape
    heads = wide // HEAD_K
    steps = heads // TOGETHER

    def body(gh_ref, wo, mixed_ref, swish_ref, hg_ref, q_ref, g_ref, d_ref, marks_ref, gm_out, gs_out, hg_out, m_out):
        grad = nt(gh_ref[...], wo[...])
        mixed = mixed_ref[...]
        swish = swish_ref[...]
        soft = sigmoid(swish)
        silu = swish * soft
        norm = lax.rsqrt(head_mean(mixed * mixed) + 1e-05)
        unit = mixed * norm
        gain = repeated(hg_ref[...])
        gs_out[...] = (grad * unit * gain * (soft * (1.0 + swish * (1.0 - soft)))).astype(BF16)
        by_gain = jnp.sum(grad * unit * silu, axis=0, keepdims=True)
        by_gain = sum(by_gain[:, at] for at in spans())

        @pl.when(pl.program_id(0) == 0)
        def _():
            hg_out[...] = by_gain

        @pl.when(pl.program_id(0) > 0)
        def _():
            hg_out[...] += by_gain

        inner = grad * gain * silu
        grad_mixed = norm * (inner - unit * head_mean(inner * unit))
        gm_out[...] = grad_mixed.astype(BF16)
        along = summed(triangle(rows, lambda i, j: j <= i), log_decay(g_ref[...]))
        query_in = (scaled(q_ref[...]) * jnp.exp(along)).astype(BF16)
        entry = (grad_mixed * marks_ref[:, 3:4]).astype(BF16)
        for n, at in enumerate(spans()):
            m_out[n, :HEAD_V] = tn(entry[:, at], query_in[:, at]).astype(BF16)
            m_out[n, HEAD_V:] = d_ref[n]

    return kernel_call(
        body,
        (steps,),
        [
            (grad_low, spec((rows, wide))),
            (weights, spec((TOGETHER * HEAD_V, wide), lambda h: (h, 2))),
            (mixed, by_head(rows)),
            (swish, by_head(rows)),
            (head_gain, spec((1, HEAD_V))),
            (queries, by_head(rows)),
            (gate_pre, by_head(rows)),
            (decays, spec((TOGETHER, MESSAGE - HEAD_V, HEAD_K), lambda h: (h, 0, 0))),
            (marks, spec(marks.shape)),
        ],
        [
            ((rows, wide), BF16, by_head(rows)),
            ((rows, wide), BF16, by_head(rows)),
            ((1, HEAD_V), F32, spec((1, HEAD_V))),
            ((heads, MESSAGE, HEAD_K), BF16, spec((TOGETHER, MESSAGE, HEAD_K), lambda h: (h, 0, 0))),
        ],
    )


def mixer_back(queries, keys, values, gate_pre, grad_mixed, states, leaving, first, marks, doc_row, rank):
    rows, wide = queries.shape
    heads = wide // HEAD_K
    steps = heads // TOGETHER
    blocks = rows // GROUP

    def body(
        q_ref, k_ref, v_ref, g_ref, gm_ref, s_ref, l_ref, ro, marks_ref, doc_ref,
        gq_out, gk_out, gv_out, gg_out, low_out, state_grad, slope, low,
    ):
        h = pl.program_id(0)
        gate = g_ref[...]
        along = summed(triangle(rows, lambda i, j: j <= i, GROUP), log_decay(gate))
        causal = triangle(GROUP, lambda i, j: j <= i) > 0
        onward = triangle(GROUP, lambda i, j: j >= i)
        for head in range(TOGETHER):
            state_grad[head] = l_ref[head].astype(F32)
        for n in reversed(range(blocks)):
            at = slice(n * GROUP, (n + 1) * GROUP)
            marks_n = marks_ref[at]
            entering = marks_n[:, 1:2]
            allowed = causal & (marks_n[:, 0:1] == doc_ref[:, at])
            run_all = along[at]
            for head, lanes in enumerate(spans()):
                run = run_all[:, lanes]
                end = run[GROUP - 1 :]
                key = k_ref[at, lanes].astype(F32)
                value = v_ref[at, lanes]
                grad = gm_ref[at, lanes]
                up, down = jnp.exp(run), jnp.exp(-run)
                out = jnp.exp(end - run) * marks_n[:, 2:3]
                query_in = (scaled(q_ref[at, lanes]) * up).astype(BF16)
                key_in = (key * down).astype(BF16)
                key_out = (key * out).astype(BF16)
                scores = jnp.where(allowed, nt(query_in, key_in), 0.0).astype(BF16)
                grad_scores = jnp.where(allowed, nt(grad, value), 0.0).astype(BF16)
                leaving = state_grad[head].astype(BF16)
                grad_query = nn(grad_scores, key_in) + entering * nn(grad, s_ref[head, n])
                grad_key_in = tn(grad_scores, query_in)
                grad_key_out = nn(value, leaving)
                gv_out[at, lanes] = (tn(scores, grad) + nt(key_out, leaving)).astype(BF16)
                gq_out[at, lanes] = (grad_query * up * HEAD_K ** (-0.5)).astype(BF16)
                gk_out[at, lanes] = (grad_key_in * down + grad_key_out * out).astype(BF16)
                change = (
                    query_in.astype(F32) * grad_query
                    - key_in.astype(F32) * grad_key_in
                    - key_out.astype(F32) * grad_key_out
                )
                closing = jnp.sum(s_ref[head, n + 1].astype(F32) * leaving.astype(F32), axis=0, keepdims=True)
                slope[at, lanes] = summed(onward, change) + closing
                kept = marks_n[GROUP - 1 :, 1:2] * jnp.exp(end)
                state_grad[head] = kept * state_grad[head] + tn(grad, (query_in.astype(F32) * entering).astype(BF16))
        grad_gate = (slope[...] * sigmoid(-gate) * (1.0 / 16.0)).astype(BF16)
        gg_out[...] = grad_gate.T
        part = nn(grad_gate, ro[...])

        @pl.when(h == 0)
        def _():
            low[...] = part

        @pl.when(h > 0)
        def _():
            low[...] += part

        @pl.when(h == steps - 1)
        def _():
            row = lax.broadcasted_iota(jnp.int32, (LANES, LANES), 0)
            lane = lax.broadcasted_iota(jnp.int32, (LANES, LANES), 1)
            move = jnp.where((row == lane + rank) & (lane < rank), 1.0, 0.0).astype(BF16)
            low_out[...] = nn(low[...].astype(BF16), move).astype(BF16)

    return kernel_call(
        body,
        (steps,),
        [
            (queries, by_head(rows)),
            (keys, by_head(rows)),
            (values, by_head(rows)),
            (gate_pre, by_head(rows)),
            (grad_mixed, by_head(rows)),
            (states, spec((TOGETHER, blocks + 1, HEAD_V, HEAD_K), lambda h: (h, 0, 0, 0))),
            (leaving, spec((TOGETHER, HEAD_V, HEAD_K), lambda h: (h, 0, 0))),
            (first, spec((TOGETHER * HEAD_K, LANES), lambda h: (h, 2 * wide // LANES))),
            (marks, spec(marks.shape)),
            (doc_row, spec(doc_row.shape)),
        ],
        [((rows, wide), BF16, by_head(rows))] * 3
        + [
            ((wide, rows), BF16, spec((TOGETHER * HEAD_K, rows), lambda h: (h, 0))),
            ((rows, LANES), BF16, spec((rows, LANES))),
        ],
        [
            pltpu.VMEM((TOGETHER, HEAD_V, HEAD_K), F32),
            pltpu.VMEM((rows, TOGETHER * HEAD_K), F32),
            pltpu.VMEM((rows, LANES), F32),
        ],
    )


def input_back(grads, first, second, grad_rank, tokens, gain, grad_hidden):
    rows, wide = tokens.shape
    steps = wide // HEAD_K // TOGETHER
    places = ((second, 0), (first, 0), (first, steps), (second, steps))

    def body(*refs):
        grad_refs, weight_refs = refs[:4], refs[4:8]
        low_ref, table, x_ref, gain_ref, gh_ref, out_ref, total = refs[8:]
        h = pl.program_id(0)
        part = nt(grad_refs[0][...], weight_refs[0][...])
        for g, w in zip(grad_refs[1:], weight_refs[1:]):
            part = part + nt(g[...], w[...])

        @pl.when(h == 0)
        def _():
            total[...] = part + nt(low_ref[...], table[...])

        @pl.when(h > 0)
        def _():
            total[...] += part

        @pl.when(h == steps - 1)
        def _():
            x = x_ref[...].astype(F32)
            scale = lax.rsqrt(jnp.mean(x * x, axis=1, keepdims=True) + 1e-06)
            unit = x * scale
            grad = total[...] * gain_ref[...]
            out_ref[...] = gh_ref[...] + scale * (grad - unit * jnp.mean(grad * unit, axis=1, keepdims=True))

    whole = spec((rows, wide))
    return kernel_call(
        body,
        (steps,),
        [(g, by_head(rows)) for g in grads]
        + [(w, by_head(wide, start)) for w, start in places]
        + [
            (grad_rank, spec((rows, LANES))),
            (first, spec((wide, LANES), lambda h: (0, 2 * wide // LANES))),
            (tokens, whole),
            (gain, spec((1, wide))),
            (grad_hidden, whole),
        ],
        [((rows, wide), F32, whole)],
        [pltpu.VMEM((rows, wide), F32)],
    )[0]


def finish(terms, weights, turned_in, gain, middle, w_middle, rank, head_rows):
    rows, width = weights[0].shape
    count = len(weights)

    def body(*refs):
        term_refs, weight_refs = refs[: len(terms)], refs[len(terms) : len(terms) + count]
        in_ref, gain_ref, middle_ref, wm_ref = refs[len(terms) + count : len(terms) + count + 4]
        outs, middle_outs = refs[len(terms) + count + 4 : -7], refs[-7:-5]
        in_out, out_out, bias_out, head_out, gain_out = refs[-5:]

        def summed_terms(at):
            total = term_refs[0][:, at].astype(F32)
            for t in term_refs[1:]:
                total = total + t[:, at].astype(F32)
            return total

        for n, out in enumerate(middle_outs):
            out[...] = middle_ref[:, n * width : (n + 1) * width].astype(F32)
        by_row = jnp.sum(wm_ref[...].astype(F32) * middle_outs[0][...], axis=1, keepdims=True)
        for n, out in enumerate(outs):
            out[...] = summed_terms(slice(n * width, (n + 1) * width))
            by_row = by_row + jnp.sum(weight_refs[n][...].astype(F32) * out[...], axis=1, keepdims=True)
        table = summed_terms(slice(count * width, count * width + LANES))
        lane = lax.broadcasted_iota(jnp.int32, (rows, LANES), 1)
        turned = jnp.where(lane == LANES - 1, by_row, table).T
        in_out[...] = turned[:rank]
        out_out[...] = turned[rank : 2 * rank]
        bias_out[...] = turned[2 * rank : 2 * rank + 1]
        head_out[...] = turned[2 * rank + 3 : 2 * rank + 4, :head_rows]
        by_rank = jnp.sum(in_ref[...].astype(F32) * turned[:rank], axis=0, keepdims=True)
        gain_out[...] = (turned[LANES - 1 :] + by_rank) / gain_ref[...].astype(F32)

    ins = [*terms, *weights, turned_in, gain, middle, w_middle]
    shapes = [(rows, width)] * (count + 2) + [(rank, rows), (rank, rows), (1, rows), (1, head_rows), (1, rows)]
    return kernel_call(body, (1,), [(a, spec(a.shape)) for a in ins], [(o, F32, spec(o)) for o in shapes])


def then(earlier, later):
    scale = later[:, HEAD_V:].astype(F32)
    state = scale[:, :1] * earlier[:, :HEAD_V].astype(F32) + later[:, :HEAD_V].astype(F32)
    return jnp.concatenate([state, scale * earlier[:, HEAD_V:].astype(F32)], axis=1).astype(BF16)


def nothing(like):
    return jnp.concatenate([jnp.zeros_like(like[:, :HEAD_V]), jnp.ones_like(like[:, HEAD_V:])], axis=1)


class Passing:
    def __init__(self, message, backward=False):
        _, y, x, c = place()
        height = lax.axis_size("y")
        self.core, self.sign = c, -1 if backward else 1
        if backward:
            y, x, c = height - 1 - y, 1 - x, 1 - c
        self.y, self.x, self.c = y, x, c
        heads = message.shape[0]
        self.other = flip(message, "c")
        both = jnp.where(c == 0, then(message, self.other), then(self.other, message))
        self.mine = lax.dynamic_slice_in_dim(both, self.core * (heads // 2), heads // 2, 0)

    def near(self, done=()):
        if square_plane():
            mine = after(done, self.mine)
            self.arrived = (cross(mine, False), cross(mine, True))
        else:
            self.arrived = flip(after(done, self.mine), "x")
        return self.arrived

    def distant(self, done=()):
        if square_plane():
            self.far = cross(after(done, self.arrived[0]), True)
            return self.far
        beside, mine = after(done, self.arrived, self.mine)
        self.before = jnp.where(self.x == 1, beside, nothing(mine))
        self.line = jnp.where(self.x == 1, then(beside, mine), then(mine, beside))
        self.far = [shift(self.line, "y", self.sign * j) for j in range(1, lax.axis_size("y"))]
        return self.far

    def entering(self, done=()):
        if square_plane():
            (early, late), corner = after(done, self.arrived, self.far)
            beside = jnp.where(self.core == 0, early, late)
            along = jnp.where(self.core == 0, late, early)
            line = jnp.where(self.x == 1, then(corner, along), then(along, corner))
            before = jnp.where(self.x == 1, beside, nothing(beside))
            before = jnp.where(self.y == 1, then(line, before), before)
        else:
            before, distant = after(done, self.before, self.far)
            for j, far in enumerate(distant):
                before = jnp.where(self.y > j, then(far, before), before)
        rest = flip(before, "c")
        chip = jnp.where(self.core == 0, jnp.concatenate([before, rest]), jnp.concatenate([rest, before]))
        return jnp.where(self.c == 1, then(chip, self.other), chip)[:, :HEAD_V]


def pair(value):
    return (value, flip(value, "c"))


def document_of(positions, starts):
    return jnp.sum((starts[None, :] <= positions[:, None]).astype(jnp.int32), axis=1) - 1


def documents(starts, rows):
    _, y, x, c = place()
    positions = ((y * 2 + x) * 2 + c) * rows + jnp.arange(rows, dtype=jnp.int32)
    doc = document_of(positions, starts)
    before = document_of(positions - 1, starts)
    blocks = doc.reshape(-1, GROUP)
    entering = (blocks == before.reshape(-1, GROUP)[:, :1]).reshape(-1)
    tail = (blocks == blocks[:, -1:]).reshape(-1)
    columns = [doc, entering, tail, doc == before[0], doc == doc[-1]]
    marks = jnp.stack([a.astype(F32) for a in columns] + [jnp.zeros((rows,), F32)] * 3, axis=1)
    return marks, doc.astype(F32).reshape(1, rows)


def pair(value):
    return (value, flip(value, "c"))


def shards(tokens, cotangent, doc_starts, *weights):
    (
        gain_one, w_query, w_key, w_value, w_swish, rank_in, rank_out, bias, head_gain, w_output, gain_two,
        w_gate, w_up, w_down,
    ) = weights
    rows, width = tokens.shape
    own, rank, ff = w_query.shape[0], rank_in.shape[1], w_gate.shape[1]
    devices = width // own
    _, _, _, c = place()

    table_columns = 2 * width + LANES
    square_weights = jnp.concatenate([w_query, w_swish, w_output], axis=1)

    first = first_weights(w_key, w_value, rank_in.T, rank_out, (bias, gain_one, gain_two, head_gain))
    wait_for = first
    marks, doc_row = documents(doc_starts[0], rows)
    fast = square_plane() and own % 16 == 0
    depth = lax.axis_size("z")

    def by_distance(base, odd, even):
        return jnp.stack([base] + [(odd if k % 2 else even)[(k - 1) // 2] for k in range(1, depth)])

    def odd_shifts(a):
        return [shift(a, "z", k) for k in range(1, depth, 2)]

    def even_shifts(a):
        return [shift(a, "z", k) for k in range(2, depth, 2)]

    if fast:
        half = width // 2
        keep = lax.dynamic_slice_in_dim(w_down, c * half, half, 1)
        other = flip(lax.dynamic_slice_in_dim(w_down, (1 - c) * half, half, 1), "c")
        chip_down = jnp.where(c == 0, jnp.concatenate([keep, other]), jnp.concatenate([other, keep]))
        one = by_distance(first, odd_shifts(first), even_shifts(first))
        one_early, one_late = cross(one, False), cross(one, True)
        now = (one_early, one_late)
        square_weights, one_next = after(now, square_weights, one_early)
        one_corner = cross(one_next, True)
        two_odd = odd_shifts(square_weights)
        now = (one_corner, two_odd)
        square_weights, one = after(now, square_weights, one)
        wait_for = two_even = even_shifts(square_weights)
        two = by_distance(square_weights, two_odd, two_even)
        one, two = after(two, one, two)
        first = assemble(gathered(one, one_early, one_late, one_corner), own, (width, table_columns))
        two_early = cross(two, False)
        first, two, chip_down = after((first, two_early), first, two, chip_down)
        two_late = cross(two, True)
        three_odd = odd_shifts(chip_down)
    else:
        first = lax.all_gather(first, AXES, axis=0, tiled=True)
        second = lax.all_gather(square_weights, AXES, axis=0, tiled=True)
        w_down_all = lax.all_gather(w_down, AXES, axis=0, tiled=True)
    gate_shard, up_shard = after(wait_for, w_gate, w_up)
    w_both = lax.all_gather(jnp.concatenate([gate_shard, up_shard], axis=1), AXES, axis=0, tiled=True)
    normed, normed_turned, low, keys, values, gate_pre, message, vectors = project(tokens, first, marks, rank)
    row_one, row_two = vectors[1:2], vectors[2:3]
    row_head = vectors[3].reshape(devices, own)[:, : head_gain.shape[0]].reshape(1, HEAD_V)
    if fast:
        message, two_early, chip_down = after((two_late, three_odd), message, two_early, chip_down)
    passing = Passing(message)
    if fast:
        two_next, three_next = after(passing.mine, two_early, chip_down)
        two_corner = cross(two_next, True)
        three_even = even_shifts(three_next)
        now = (passing.near(), two_corner, three_even)
        now = passing.distant(now)
        three, two, two_early, two_late, two_corner = after(
            now, by_distance(chip_down, three_odd, three_even), two, two_early, two_late, two_corner
        )
        three_early = cross(three, False)
        second = assemble(gathered(two, two_early, two_late, two_corner), own, (width, 3 * width))
        entered = passing.entering(now)
        entered, second, three, three_early = after((entered, second, three_early), entered, second, three, three_early)
        three_late, three_corner = cross(three, True), cross(three_early, True)
    else:
        passing.near()
        passing.distant()
        entered = passing.entering()
    queries, mixed, swish, gated, hidden, normed_two, two_turned, states = mixer(
        normed, keys, values, gate_pre, entered, second, row_head, tokens, row_two, marks, doc_row
    )
    if fast:
        hidden, three = after((three_late, three_corner), hidden, three)
        w_down_all = assemble(
            gathered(three, three_early, three_late, three_corner), chip_down.shape[0], (ff, width), True
        )
    output, inner, grad_gate, grad_up, grad_hidden, grad_low = feed(
        normed_two, cotangent, w_both, w_down_all, hidden, row_two
    )

    both = pair(normed_turned)
    two_pair = pair(two_turned)
    down = weight_grads([(pair(inner), [pair(cotangent)])], 512, True)
    grad_low, gate_pair, up_pair = after(down.blocks, grad_low, pair(grad_gate), pair(grad_up))
    grad_mixed, grad_swish, grad_head_gain, message_back = head_back(
        grad_low, second, mixed, swish, row_head, queries, gate_pre, message[:, HEAD_V:], marks
    )
    gate = weight_grads([(two_pair, [gate_pair])], ff // 2)
    now = (down.first(), message_back, gate.blocks)
    passing = Passing(after(now, message_back), True)
    now = passing.mine
    up = weight_grads([(two_pair, [after(now, up_pair)])], ff // 2)
    now = (passing.near(), down.second(now), up.blocks)
    down_part = down.third()
    swish_pair, gated_pair, low_pair = after(now, pair(grad_swish), pair(gated), pair(grad_low))
    middle = weight_grads([(both, [swish_pair]), (gated_pair, [low_pair])], width)
    now = (passing.distant(now), gate.first(now), middle.blocks)
    leaving = passing.entering(now)
    now = leaving
    grad_query, grad_key, grad_value, grad_gate_pre, grad_rank = mixer_back(
        queries, keys, values, gate_pre, grad_mixed, states, leaving, first, marks, doc_row, rank
    )
    now = (up.first(now), grad_query)
    gate.second(now, up)
    inside_pairs = [pair(a) for a in after(now, grad_query, grad_key, grad_value, grad_rank, grad_gate_pre)]
    head_terms = grad_head_gain + flip(grad_head_gain, "c")
    head_terms = jnp.pad(head_terms.reshape(devices, -1), ((0, 0), (0, own - head_gain.shape[0]))).reshape(width, 1)
    base = jnp.pad(head_terms.astype(BF16), ((0, 0), (2 * rank + 3, LANES - 2 * rank - 4)))
    inside = weight_grads(
        [(both, inside_pairs[:3])],
        width,
        table=([(both, inside_pairs[3]), (inside_pairs[4], pair(low))], base),
    )
    now = (inside.blocks, gate.through, up.through, down_part)
    gates_part = gate.third(up)
    input_grad = input_back(
        (grad_query, grad_key, grad_value, grad_swish), first, second, after(now, grad_rank), tokens, row_one,
        grad_hidden,
    )
    now = (input_grad, middle.first(now), inside.first(now))
    now = (inside.second(now), middle.second(now))
    middle_part = middle.third()
    inside_terms = inside.third_terms()

    chip_half = ff // devices
    down_sum = wide(down_part)
    keep = lax.dynamic_slice_in_dim(down_sum, c * chip_half, chip_half, 0)
    other = flip(lax.dynamic_slice_in_dim(down_sum, (1 - c) * chip_half, chip_half, 0), "c")
    down_sum = jnp.where(c == 0, jnp.concatenate([keep, other], 1), jnp.concatenate([other, keep], 1))
    g_gate, g_up = wide(gates_part[:, :ff]), wide(gates_part[:, ff:])
    g_gain_two = (jnp.sum(wide(w_gate) * g_gate, axis=1) + jnp.sum(wide(w_up) * g_up, axis=1)) / wide(gain_two)
    g_query, g_key, g_value, g_swish, g_output, g_rank_in, g_rank_out, g_bias, g_head, g_gain_one = finish(
        inside_terms, (w_query, w_key, w_value), rank_in.T, gain_one.reshape(1, own), middle_part, w_swish,
        rank, head_gain.shape[0],
    )
    return (
        output, input_grad, g_gain_one[0], g_query, g_key, g_value, g_swish, g_rank_in.T, g_rank_out, g_bias[0], g_head[0],
        g_output, g_gain_two, g_gate, g_up, down_sum,
    )


def solution(mesh):
    fsdp, seq = mesh.shape["fsdp"], mesh.shape["seq"]
    inner = Mesh(mesh.devices.reshape(fsdp, seq // 4, 2, 2), AXES)
    rows, vector, columns = P(AXES, None), P(AXES), P(None, AXES)
    in_specs = (rows, rows, P("z", None), vector, rows, rows, rows, rows, rows, columns, vector, vector, rows, vector) + (rows,) * 3
    out_specs = (rows, rows, vector) + (rows,) * 5 + (columns, vector, vector, rows, vector) + (rows,) * 3
    return jax.shard_map(shards, mesh=inner, in_specs=in_specs, out_specs=out_specs, check_vma=False)
```

```python
from functools import partial

import jax
import jax.numpy as jnp
from jax import lax
from jax.experimental import pallas as pl
from jax.experimental.pallas import tpu as pltpu
from jax.sharding import Mesh
from jax.sharding import PartitionSpec as P

HEAD_K = 256
HEAD_V = 256
GROUP = 64
LANES = 128
TOGETHER = 2
AXES = ("z", "y", "x", "c")
VMEM = 56 * 1024 * 1024
QUICK = pl.CostEstimate(flops=0, bytes_accessed=0, transcendentals=0)
F32 = jnp.float32
BF16 = jnp.bfloat16


def shift(value, axis, step):
    size = lax.axis_size(axis)
    return lax.ppermute(value, axis, [(i, (i + step) % size) for i in range(size)])


def flip(value, axis):
    return shift(value, axis, 1)


def place():
    return tuple(lax.axis_index(a) for a in AXES)


def after(done, *values):
    out = lax.optimization_barrier((values, done))[0]
    return out[0] if len(values) == 1 else out


def square_plane():
    return lax.axis_size("y") == 2


def cross(value, late):
    perm = [(i, i ^ (2 if (i % 2 == 0) != late else 4)) for i in range(8)]
    return lax.ppermute(value, ("y", "x", "c"), perm)


def neighbour(early, late, core):
    _, y, x, _ = place()
    by_x = jnp.where(core == 0, early, late)
    by_y = jnp.where(core == 0, late, early)
    return (y + by_y) % 2, (x + by_x) % 2


def gathered(own, early, late, corner, others=()):
    pieces = [(own, 0, 0, 0), (early, 1, 0, 0), (late, 0, 1, 0), (corner, 1, 1, 0)]
    others = list(others) + [flip(a, "c") for a, _, _, _ in pieces[len(others) :]]
    return pieces + [(a, i, j, 1) for a, (_, i, j, _) in zip(others, pieces)]


def sources(pieces):
    z, _, _, c = place()
    depth = lax.axis_size("z")
    chips, cores = [], []
    for _, early, late, other in pieces:
        core = (c + other) % 2
        y, x = neighbour(early, late, core)
        for k in range(depth):
            chips.append((((z - k) % depth) * 2 + y) * 2 + x)
            cores.append(core)
    return jnp.stack(chips + cores).astype(jnp.int32)


def assemble(pieces, rows, shape, by_columns=False):
    where = sources(pieces)
    arrays = [p[0] for p in pieces]
    depth = arrays[0].shape[0]
    blocks = [(n, k) for n in range(len(pieces)) for k in range(depth)]
    total = len(blocks)

    def body(where_ref, *refs):
        ins, out, sem = refs[: len(arrays)], refs[-2], refs[-1]
        for at, (n, k) in enumerate(blocks):
            chip, core = where_ref[at], where_ref[total + at]
            if by_columns:
                width = shape[1] // 2
                goal = out.at[
                    pl.ds(pl.multiple_of(chip * rows, rows), rows),
                    pl.ds(pl.multiple_of(core * width, width), width),
                ]
            else:
                goal = out.at[pl.ds(pl.multiple_of((chip * 2 + core) * rows, rows), rows), :]
            pltpu.make_async_copy(ins[n].at[k], goal, sem).start()
        pltpu.make_async_copy(out, out, sem).wait()

    return pl.pallas_call(
        body,
        grid_spec=pltpu.PrefetchScalarGridSpec(
            num_scalar_prefetch=1,
            grid=(1,),
            in_specs=[pl.BlockSpec(memory_space=pl.ANY)] * len(arrays),
            out_specs=pl.BlockSpec(shape, lambda n, s: (0, 0)),
            scratch_shapes=[pltpu.SemaphoreType.DMA],
        ),
        out_shape=jax.ShapeDtypeStruct(shape, BF16),
        compiler_params=pltpu.CompilerParams(vmem_limit_bytes=VMEM),
        cost_estimate=QUICK,
    )(where, *arrays)


def layout(by_z):
    _, _, _, c = place()
    depth, height = lax.axis_size("z"), lax.axis_size("y")
    if not square_plane():
        return [jnp.arange(depth * height * 2, dtype=jnp.int32)]

    def column(early, late):
        y, x = neighbour(early, late, c)
        return (jnp.arange(depth, dtype=jnp.int32) * 2 + y) * 2 + x

    columns = [column(1, 0), column(1, 1), column(0, 1), column(0, 0)]
    if by_z:
        return [jnp.stack(columns, axis=1).reshape(-1)]
    return [jnp.concatenate(columns[:2]), *columns[2:]]


def wide(a):
    return a.astype(F32)


class Sum:
    def __init__(self, blocks):
        self.blocks = blocks
        self.depth = lax.axis_size("z")

    def zeroth(self, done=()):
        if square_plane():
            (blocks,) = after(done, self.blocks, ())[0]
            _, rows, width = blocks.shape
            part = lax.psum_scatter(blocks.reshape(-1, width), "z", scatter_dimension=0, tiled=True)
            part = part.reshape(4, rows, width)
            self.blocks, self.depth = [part[:2], part[2:3], part[3:]], 1
        return self.blocks

    def first(self, done=()):
        self.arrived = cross(after(done, self.blocks[0]), False) if square_plane() else ()
        return self.arrived

    def second(self, done=(), *others):
        parts = (self, *others)
        if not square_plane():
            for p in parts:
                p.through = ()
            return ()
        sums = []
        for p in parts:
            arrived, kept = after(done, p.arrived, p.blocks[1])
            sums.append((wide(kept) + wide(arrived[p.depth :])).astype(BF16))
        through = cross(sums[0] if len(sums) == 1 else jnp.concatenate(sums, axis=2), True)
        at = 0
        for p, part in zip(parts, sums):
            p.through = through[:, :, at : at + part.shape[2]]
            at += part.shape[2]
        return through

    def total(self):
        return (wide(self.blocks[2]) + wide(self.arrived[: self.depth]) + wide(self.through)).astype(BF16)

    def result(self):
        return self.total()[0] if square_plane() else self.third()

    def third(self, *others):
        parts = (self, *others)
        if square_plane():
            axes, totals = "z", [p.total() for p in parts]
        else:
            axes, totals = ("z", "y", "x"), [p.blocks[0] for p in parts]
        total = totals[0] if len(totals) == 1 else jnp.concatenate(totals, axis=2)
        return lax.psum_scatter(total.reshape(-1, total.shape[-1]), axes, scatter_dimension=0, tiled=True)

    def third_terms(self):
        if not square_plane():
            return [self.third()]
        depth = lax.axis_size("z")
        total, z = self.total(), lax.axis_index("z")
        block = [lax.dynamic_index_in_dim(total, (z + k) % depth, 0, False) for k in range(depth)]
        return [block[0]] + [shift(block[k], "z", k) for k in range(1, depth)]


def weight_grads(groups, tile, halves=False, table=None, by_z=False):
    _, _, _, c = place()
    chips = layout(by_z)
    spans = [a.shape[0] for a in chips]
    chips = jnp.concatenate(chips)
    count = chips.shape[0]
    lefts = [left for left, _ in groups]
    rights = [right for _, group in groups for right in group]
    owner = [n for n, (_, group) in enumerate(groups) for _ in group]
    height, tokens = lefts[0][0].shape
    each = rights[0][0].shape[1] // (2 if halves else 1)
    width = each * len(rights)
    rows = height // (count if halves else 2 * count)
    starts = chips * rows if halves else (chips * 2 + c) * rows

    if rows % 16:
        products = []
        for n, right in zip(owner, rights):
            product = nn(jnp.concatenate(lefts[n], axis=1), jnp.concatenate(right)).astype(BF16)
            if halves:
                product = lax.dynamic_slice_in_dim(product, c * each, each, 1).reshape(count, rows, each)
            else:
                product = lax.dynamic_index_in_dim(product.reshape(count, 2, rows, each), c, 1, False)
            products.append(product)
        if table is not None:
            product = wide(table[1])
            for left, right in table[0]:
                product = product + nn(jnp.concatenate(left, axis=1), jnp.concatenate(right))
            product = product.astype(BF16).reshape(count, 2, rows, LANES)
            products.append(lax.dynamic_index_in_dim(product, c, 1, False))
        product = jnp.take(jnp.concatenate(products, axis=2), chips, axis=0)
        blocks, at = [], 0
        for span in spans:
            blocks.append(product[at : at + span])
            at += span
        return Sum(blocks)

    strips = each // tile
    first_tile = c * strips if halves else jnp.int32(0)
    numbers = jnp.concatenate([starts, first_tile[None]]).astype(jnp.int32)

    steps = width // tile
    terms, base = table if table is not None else ((), None)
    flat = [a for left in lefts for a in left] + [a for right in rights for a in right]
    narrow = [a for left, right in terms for a in (*left, *right)]
    if table is not None:
        narrow.append(base)

    def body(numbers_ref, *refs):
        left_refs, right_refs = refs[: 2 * len(lefts)], refs[2 * len(lefts) : len(flat)]
        narrow_refs = refs[len(flat) : len(flat) + len(narrow)]
        outs, (chosen, total, based) = refs[len(flat) + len(narrow) : -3], refs[-3:]
        step = pl.program_id(0)

        def start(at):
            return pl.ds(pl.multiple_of(numbers_ref[at], 16), rows)

        def choose(lo_ref, ls_ref):
            for at in range(count):
                chosen[at * rows : (at + 1) * rows, :tokens] = lo_ref[start(at), :]
                chosen[at * rows : (at + 1) * rows, tokens:] = ls_ref[start(at), :]

        def put(product, columns):
            at = 0
            for out, span in zip(outs, spans):
                out[:, :, :columns] = product[at : at + span * rows].reshape(span, rows, columns)
                at += span * rows

        def strip(ro_ref, rs_ref):
            both = jnp.concatenate([ro_ref[...], rs_ref[...]], axis=0)
            put(nn(chosen[...], both).astype(BF16), tile)

        def term(n):
            lo_ref, ls_ref, ro_ref, rs_ref = narrow_refs[4 * n : 4 * n + 4]
            choose(lo_ref, ls_ref)
            both = jnp.concatenate([ro_ref[...], rs_ref[...]], axis=0)
            product = nn(chosen[...], both)
            if n == 0:
                total[...] = product
            else:
                total[...] += product
            if n == len(terms) - 1:
                for at in range(count):
                    based[at * rows : (at + 1) * rows, :] = narrow_refs[-1][start(at), :]
                put((total[...] + wide(based[...])).astype(BF16), LANES)

        for n in range(len(lefts)):
            pl.when(step == owner.index(n) * strips)(partial(choose, *left_refs[2 * n : 2 * n + 2]))
        if len(rights) == 1:
            strip(*right_refs)
        else:
            for n in range(len(rights)):
                pl.when(step // strips == n)(partial(strip, *right_refs[2 * n : 2 * n + 2]))
        for n in range(len(terms)):
            pl.when(step == steps + n)(partial(term, n))

    def column(n):
        return lambda step, s: (0, jnp.clip(step - n * strips, 0, strips - 1) + s[count])

    def full(a):
        return pl.BlockSpec(a.shape, lambda n, s: (0,) * a.ndim)

    right_specs = [pl.BlockSpec((tokens, tile), column(n)) for n in range(len(rights)) for _ in range(2)]
    columns = width + (LANES if table is not None else 0)
    last = steps - (table is None)
    outs = [(span, rows, columns) for span in spans]
    blocks = pl.pallas_call(
        body,
        grid_spec=pltpu.PrefetchScalarGridSpec(
            num_scalar_prefetch=1,
            grid=(steps + len(terms),),
            in_specs=[full(a) for left in lefts for a in left] + right_specs + [full(a) for a in narrow],
            out_specs=[pl.BlockSpec((n, rows, tile), lambda n, s: (0, 0, jnp.minimum(n, last))) for n, _, _ in outs],
            scratch_shapes=[
                pltpu.VMEM((count * rows, 2 * tokens), BF16),
                pltpu.VMEM((count * rows, LANES), F32),
                pltpu.VMEM((count * rows, LANES), BF16),
            ],
        ),
        out_shape=[jax.ShapeDtypeStruct(o, BF16) for o in outs],
        compiler_params=pltpu.CompilerParams(vmem_limit_bytes=VMEM),
        cost_estimate=QUICK,
    )(numbers, *flat, *narrow)
    return Sum(blocks)


def nn(left, right):
    return jnp.dot(left, right, preferred_element_type=F32)


def nt(left, right):
    return lax.dot_general(left, right, (((1,), (1,)), ((), ())), preferred_element_type=F32)


def tn(left, right):
    return lax.dot_general(left, right, (((0,), (0,)), ((), ())), preferred_element_type=F32)


def summed(ones, values):
    high = values.astype(BF16)
    low = (values - high.astype(F32)).astype(BF16)
    return nn(ones, high) + nn(ones, low)


def triangle(size, relation, block=None):
    row = lax.broadcasted_iota(jnp.int32, (size, size), 0)
    column = lax.broadcasted_iota(jnp.int32, (size, size), 1)
    chosen = relation(row, column)
    if block is not None:
        chosen = chosen & (row // block == column // block)
    return jnp.where(chosen, 1.0, 0.0).astype(BF16)


def log_decay(gate_pre):
    return (jnp.minimum(gate_pre, 0.0) - jnp.log1p(jnp.exp(-jnp.abs(gate_pre)))) * (1.0 / 16.0)


def sigmoid(v):
    return 1.0 / (1.0 + jnp.exp(-v))


def spec(shape, index=None):
    index = index or (lambda *_: (0,) * len(shape))
    return pl.BlockSpec(shape, index)


def by_head(rows, start=0):
    return spec((rows, TOGETHER * HEAD_K), lambda h: (0, start + h))


def spans(count=TOGETHER):
    return [slice(n * HEAD_K, (n + 1) * HEAD_K) for n in range(count)]


def by_spans(function, *arrays):
    return jnp.concatenate([function(*[a[:, at] for a in arrays]) for at in spans()], axis=1)


def head_mean(values):
    return by_spans(lambda a: jnp.broadcast_to(jnp.mean(a, axis=1, keepdims=True), a.shape), values)


def repeated(row):
    return jnp.concatenate([row] * TOGETHER, axis=1)


def kernel_call(body, grid, ins, outs, scratch=()):
    return pl.pallas_call(
        body,
        grid=grid,
        in_specs=[s for _, s in ins],
        out_specs=[s for _, _, s in outs],
        out_shape=[jax.ShapeDtypeStruct(shape, dtype) for shape, dtype, _ in outs],
        scratch_shapes=list(scratch),
        compiler_params=pltpu.CompilerParams(vmem_limit_bytes=VMEM),
        cost_estimate=QUICK,
    )(*[a for a, _ in ins])


MESSAGE = HEAD_V + 16


def unit_columns(rows, columns, start):
    row = lax.broadcasted_iota(jnp.int32, (rows, columns), 0)
    column = lax.broadcasted_iota(jnp.int32, (rows, columns), 1)
    return jnp.where(column == row + start, 1.0, 0.0).astype(BF16)


def first_weights(w_key, w_value, turned_in, rank_out, vectors):
    rows, width = w_key.shape
    rank = turned_in.shape[0]

    def body(wk, wv, ri, ro, *refs):
        vector_refs, out = refs[:-1], refs[-1]
        out[:, :width] = wk[...]
        out[:, width : 2 * width] = wv[...]
        table = tn(ri[...], unit_columns(rank, LANES, 0)) + tn(ro[...], unit_columns(rank, LANES, rank))
        for n, v in enumerate(vector_refs):
            mine = unit_columns(v.shape[1], rows, 0)
            table = table + tn(nn(v[...], mine).astype(BF16), unit_columns(1, LANES, 2 * rank + n))
        out[:, 2 * width :] = table.astype(BF16)

    ins = [w_key, w_value, turned_in, rank_out, *[v.reshape(1, -1) for v in vectors]]
    shape = (rows, 2 * width + LANES)
    return kernel_call(body, (1,), [(a, spec(a.shape)) for a in ins], [(shape, BF16, spec(shape))])[0]


def project(tokens, weights, marks, rank):
    rows, width = tokens.shape
    heads = width // HEAD_K
    steps = heads // TOGETHER
    at_table = 2 * width // LANES

    def body(
        x_ref, wk, wv, table, part_ref, marks_ref, n_out, turned_out, low_out, k_out, v_out, g_out, m_out, vectors_out
    ):
        @pl.when(pl.program_id(0) == 0)
        def _():
            vectors = nt(unit_columns(8, LANES, 2 * rank), table[...])
            vectors_out[...] = vectors
            x = x_ref[...].astype(F32)
            scale = lax.rsqrt(jnp.mean(x * x, axis=1, keepdims=True) + 1e-06)
            n_out[...] = (x * scale * vectors[1:2]).astype(BF16)
            turned_out[...] = n_out[...].T
            low = nn(n_out[...], table[...]).astype(BF16)
            lane = lax.broadcasted_iota(jnp.int32, (LANES, LANES), 1)
            row = lax.broadcasted_iota(jnp.int32, (LANES, LANES), 0)
            move = jnp.where((lane == row + rank) & (row < rank), 1.0, 0.0).astype(BF16)
            one = jnp.where(lax.broadcasted_iota(jnp.int32, (rows, LANES), 1) == 2 * rank, 1.0, 0.0)
            low_out[...] = (nn(low, move) + one).astype(BF16)

        normed = n_out[...]
        key = nn(normed, wk[...]).astype(BF16)
        value = nn(normed, wv[...]).astype(BF16)
        k_out[...] = key
        v_out[...] = value
        gate = nt(low_out[...], part_ref[...])
        g_out[...] = gate
        decay = log_decay(gate)
        later = summed(triangle(rows, lambda i, j: j > i), decay)
        last = marks_ref[:, 4:5]
        finish = (key.astype(F32) * jnp.exp(later) * last).astype(BF16)
        total = jnp.exp(jnp.sum(decay, axis=0, keepdims=True)) * marks_ref[rows - 1 :, 3:4]
        for n, at in enumerate(spans()):
            m_out[n, :HEAD_V] = tn(value[:, at], finish[:, at]).astype(BF16)
            m_out[n, HEAD_V:] = jnp.broadcast_to(total[:, at], (MESSAGE - HEAD_V, HEAD_K)).astype(BF16)

    return kernel_call(
        body,
        (steps,),
        [
            (tokens, spec((rows, width))),
            (weights, by_head(width)),
            (weights, by_head(width, steps)),
            (weights, spec((width, LANES), lambda h: (0, at_table))),
            (weights, spec((TOGETHER * HEAD_K, LANES), lambda h: (h, at_table))),
            (marks, spec(marks.shape)),
        ],
        [
            ((rows, width), BF16, spec((rows, width))),
            ((width, rows), BF16, spec((width, rows))),
            ((rows, LANES), BF16, spec((rows, LANES))),
            ((rows, width), BF16, by_head(rows)),
            ((rows, width), BF16, by_head(rows)),
            ((rows, width), F32, by_head(rows)),
            ((heads, MESSAGE, HEAD_K), BF16, spec((TOGETHER, MESSAGE, HEAD_K), lambda h: (h, 0, 0))),
            ((8, width), F32, spec((8, width))),
        ],
    )


def scaled(queries):
    return queries.astype(F32) * HEAD_K ** (-0.5)


def mixer(normed, keys, values, gate_pre, entered, weights, head_gain, tokens, gain, marks, doc_row):
    rows, wide = tokens.shape
    heads = wide // HEAD_K
    steps = heads // TOGETHER
    blocks = rows // GROUP

    def body(
        n_ref, k_ref, v_ref, g_ref, s_ref, wq, ws, hg_ref, wo, x_ref, gain_ref, marks_ref, doc_ref,
        q_ref, mixed_out, swish_out, gated_out, hidden_out, two_out, two_turned, states_out, state, total,
    ):
        h = pl.program_id(0)
        q_ref[...] = nn(n_ref[...], wq[...]).astype(BF16)
        swish = nn(n_ref[...], ws[...])
        swish_out[...] = swish
        along = summed(triangle(rows, lambda i, j: j <= i, GROUP), log_decay(g_ref[...]))
        causal = triangle(GROUP, lambda i, j: j <= i) > 0
        run_all, key_all = along, k_ref[...].astype(F32)
        query_all = (scaled(q_ref[...]) * jnp.exp(run_all)).astype(BF16)
        key_in_all = (key_all * jnp.exp(-run_all)).astype(BF16)
        for head in range(TOGETHER):
            state[head] = s_ref[head].astype(F32)
        for n in range(blocks):
            at = slice(n * GROUP, (n + 1) * GROUP)
            marks_n = marks_ref[at]
            allowed = causal & (marks_n[:, 0:1] == doc_ref[:, at])
            run = run_all[at]
            end = run[GROUP - 1 :]
            key_out_all = (key_all[at] * jnp.exp(end - run) * marks_n[:, 2:3]).astype(BF16)
            kept = marks_n[GROUP - 1 :, 1:2] * jnp.exp(end)
            for head, lanes in enumerate(spans()):
                value = v_ref[at, lanes]
                query_in = query_all[at, lanes]
                scores = jnp.where(allowed, nt(query_in, key_in_all[at, lanes]), 0.0).astype(BF16)
                before = state[head].astype(BF16)
                states_out[head, n] = before
                mixed_out[at, lanes] = nn(scores, value) + marks_n[:, 1:2] * nt(query_in, before)
                state[head] = kept[:, lanes] * state[head] + tn(value, key_out_all[:, lanes])
        for head in range(TOGETHER):
            states_out[head, blocks] = state[head].astype(BF16)
        mixed = mixed_out[...]
        norm = lax.rsqrt(head_mean(mixed * mixed) + 1e-05)
        gated = (mixed * norm * repeated(hg_ref[...]) * (swish * sigmoid(swish))).astype(BF16)
        gated_out[...] = gated.T
        part = nn(gated, wo[...])

        @pl.when(h == 0)
        def _():
            total[...] = x_ref[...].astype(F32) + part

        @pl.when(h > 0)
        def _():
            total[...] += part

        @pl.when(h == steps - 1)
        def _():
            hidden = total[...]
            hidden_out[...] = hidden
            scale = lax.rsqrt(jnp.mean(hidden * hidden, axis=1, keepdims=True) + 1e-06)
            two_out[...] = (hidden * scale * gain_ref[...]).astype(BF16)
            two_turned[...] = two_out[...].T

    return kernel_call(
        body,
        (steps,),
        [
            (normed, spec((rows, wide))),
            (keys, by_head(rows)),
            (values, by_head(rows)),
            (gate_pre, by_head(rows)),
            (entered, spec((TOGETHER, HEAD_V, HEAD_K), lambda h: (h, 0, 0))),
            (weights, by_head(wide)),
            (weights, by_head(wide, steps)),
            (head_gain, spec((1, HEAD_V))),
            (weights, spec((TOGETHER * HEAD_V, wide), lambda h: (h, 2))),
            (tokens, spec((rows, wide))),
            (gain, spec((1, wide))),
            (marks, spec(marks.shape)),
            (doc_row, spec(doc_row.shape)),
        ],
        [
            ((rows, wide), BF16, by_head(rows)),
            ((rows, wide), F32, by_head(rows)),
            ((rows, wide), F32, by_head(rows)),
            ((wide, rows), BF16, spec((TOGETHER * HEAD_V, rows), lambda h: (h, 0))),
            ((rows, wide), F32, spec((rows, wide))),
            ((rows, wide), BF16, spec((rows, wide))),
            ((wide, rows), BF16, spec((wide, rows))),
            ((heads, blocks + 1, HEAD_V, HEAD_K), BF16, spec((TOGETHER, blocks + 1, HEAD_V, HEAD_K), lambda h: (h, 0, 0, 0))),
        ],
        [pltpu.VMEM((TOGETHER, HEAD_V, HEAD_K), F32), pltpu.VMEM((rows, wide), F32)],
    )


def feed(normed_two, cotangent, w_both, w_down, hidden, gain):
    rows, wide = hidden.shape
    inner = w_both.shape[1] // 2
    tile = inner // 2 if inner % 256 == 0 else inner
    steps = inner // tile

    def body(
        n_ref, c_ref, wg, wu, wd, hidden_ref, gain_ref,
        out_ref, inner_out, gate_out, up_out, grad_out, low_out, forward_sum, back_sum,
    ):
        step = pl.program_id(0)
        normed = n_ref[...]
        gate = nn(normed, wg[...])
        up = nn(normed, wu[...])
        soft = sigmoid(gate)
        silu = gate * soft
        product = (silu * up).astype(BF16)
        inner_out[...] = product.T
        grad = nt(c_ref[...], wd[...])
        grad_up = (grad * silu).astype(BF16)
        grad_gate = (grad * up * (soft * (1.0 + gate * (1.0 - soft)))).astype(BF16)
        up_out[...] = grad_up
        gate_out[...] = grad_gate
        ahead = nn(product, wd[...])
        back = nt(grad_gate, wg[...]) + nt(grad_up, wu[...])

        @pl.when(step == 0)
        def _():
            forward_sum[...] = hidden_ref[...] + ahead
            back_sum[...] = back

        @pl.when(step > 0)
        def _():
            forward_sum[...] += ahead
            back_sum[...] += back

        @pl.when(step == steps - 1)
        def _():
            out_ref[...] = forward_sum[...].astype(BF16)
            hidden = hidden_ref[...]
            scale = lax.rsqrt(jnp.mean(hidden * hidden, axis=1, keepdims=True) + 1e-06)
            unit = hidden * scale
            grad = back_sum[...] * gain_ref[...]
            grad = scale * (grad - unit * jnp.mean(grad * unit, axis=1, keepdims=True))
            grad = c_ref[...].astype(F32) + grad
            grad_out[...] = grad
            low_out[...] = grad.astype(BF16)

    strip = spec((wide, tile), lambda n: (0, n))
    column = spec((rows, tile), lambda n: (0, n))
    whole = spec((rows, wide))
    return kernel_call(
        body,
        (steps,),
        [
            (normed_two, whole),
            (cotangent, whole),
            (w_both, strip),
            (w_both, spec((wide, tile), lambda n: (0, n + steps))),
            (w_down, spec((tile, wide), lambda n: (n, 0))),
            (hidden, whole),
            (gain, spec((1, wide))),
        ],
        [
            ((rows, wide), BF16, whole),
            ((inner, rows), BF16, spec((tile, rows), lambda n: (n, 0))),
            ((rows, inner), BF16, column),
            ((rows, inner), BF16, column),
            ((rows, wide), F32, whole),
            ((rows, wide), BF16, whole),
        ],
        [pltpu.VMEM((rows, wide), F32), pltpu.VMEM((rows, wide), F32)],
    )


def head_back(grad_low, weights, mixed, swish, head_gain, queries, gate_pre, decays, marks):
    rows, wide = mixed.shape
    heads = wide // HEAD_K
    steps = heads // TOGETHER

    def body(gh_ref, wo, mixed_ref, swish_ref, hg_ref, q_ref, g_ref, d_ref, marks_ref, gm_out, gs_out, hg_out, m_out):
        grad = nt(gh_ref[...], wo[...])
        mixed = mixed_ref[...]
        swish = swish_ref[...]
        soft = sigmoid(swish)
        silu = swish * soft
        norm = lax.rsqrt(head_mean(mixed * mixed) + 1e-05)
        unit = mixed * norm
        gain = repeated(hg_ref[...])
        gs_out[...] = (grad * unit * gain * (soft * (1.0 + swish * (1.0 - soft)))).astype(BF16)
        by_gain = jnp.sum(grad * unit * silu, axis=0, keepdims=True)
        by_gain = sum(by_gain[:, at] for at in spans())

        @pl.when(pl.program_id(0) == 0)
        def _():
            hg_out[...] = by_gain

        @pl.when(pl.program_id(0) > 0)
        def _():
            hg_out[...] += by_gain

        inner = grad * gain * silu
        grad_mixed = norm * (inner - unit * head_mean(inner * unit))
        gm_out[...] = grad_mixed.astype(BF16)
        along = summed(triangle(rows, lambda i, j: j <= i), log_decay(g_ref[...]))
        query_in = (scaled(q_ref[...]) * jnp.exp(along)).astype(BF16)
        entry = (grad_mixed * marks_ref[:, 3:4]).astype(BF16)
        for n, at in enumerate(spans()):
            m_out[n, :HEAD_V] = tn(entry[:, at], query_in[:, at]).astype(BF16)
            m_out[n, HEAD_V:] = d_ref[n]

    return kernel_call(
        body,
        (steps,),
        [
            (grad_low, spec((rows, wide))),
            (weights, spec((TOGETHER * HEAD_V, wide), lambda h: (h, 2))),
            (mixed, by_head(rows)),
            (swish, by_head(rows)),
            (head_gain, spec((1, HEAD_V))),
            (queries, by_head(rows)),
            (gate_pre, by_head(rows)),
            (decays, spec((TOGETHER, MESSAGE - HEAD_V, HEAD_K), lambda h: (h, 0, 0))),
            (marks, spec(marks.shape)),
        ],
        [
            ((rows, wide), BF16, by_head(rows)),
            ((rows, wide), BF16, by_head(rows)),
            ((1, HEAD_V), F32, spec((1, HEAD_V))),
            ((heads, MESSAGE, HEAD_K), BF16, spec((TOGETHER, MESSAGE, HEAD_K), lambda h: (h, 0, 0))),
        ],
    )


def mixer_back(queries, keys, values, gate_pre, grad_mixed, states, leaving, first, marks, doc_row, rank):
    rows, wide = queries.shape
    heads = wide // HEAD_K
    steps = heads // TOGETHER
    blocks = rows // GROUP

    def body(
        q_ref, k_ref, v_ref, g_ref, gm_ref, s_ref, l_ref, ro, marks_ref, doc_ref,
        gq_out, gk_out, gv_out, gg_out, low_out, state_grad, slope, low,
    ):
        h = pl.program_id(0)
        gate = g_ref[...]
        along = summed(triangle(rows, lambda i, j: j <= i, GROUP), log_decay(gate))
        causal = triangle(GROUP, lambda i, j: j <= i) > 0
        onward = triangle(GROUP, lambda i, j: j >= i)
        for head in range(TOGETHER):
            state_grad[head] = l_ref[head].astype(F32)
        for n in reversed(range(blocks)):
            at = slice(n * GROUP, (n + 1) * GROUP)
            marks_n = marks_ref[at]
            entering = marks_n[:, 1:2]
            allowed = causal & (marks_n[:, 0:1] == doc_ref[:, at])
            run_all = along[at]
            for head, lanes in enumerate(spans()):
                run = run_all[:, lanes]
                end = run[GROUP - 1 :]
                key = k_ref[at, lanes].astype(F32)
                value = v_ref[at, lanes]
                grad = gm_ref[at, lanes]
                up, down = jnp.exp(run), jnp.exp(-run)
                out = jnp.exp(end - run) * marks_n[:, 2:3]
                query_in = (scaled(q_ref[at, lanes]) * up).astype(BF16)
                key_in = (key * down).astype(BF16)
                key_out = (key * out).astype(BF16)
                scores = jnp.where(allowed, nt(query_in, key_in), 0.0).astype(BF16)
                grad_scores = jnp.where(allowed, nt(grad, value), 0.0).astype(BF16)
                leaving = state_grad[head].astype(BF16)
                grad_query = nn(grad_scores, key_in) + entering * nn(grad, s_ref[head, n])
                grad_key_in = tn(grad_scores, query_in)
                grad_key_out = nn(value, leaving)
                gv_out[at, lanes] = (tn(scores, grad) + nt(key_out, leaving)).astype(BF16)
                gq_out[at, lanes] = (grad_query * up * HEAD_K ** (-0.5)).astype(BF16)
                gk_out[at, lanes] = (grad_key_in * down + grad_key_out * out).astype(BF16)
                change = (
                    query_in.astype(F32) * grad_query
                    - key_in.astype(F32) * grad_key_in
                    - key_out.astype(F32) * grad_key_out
                )
                closing = jnp.sum(s_ref[head, n + 1].astype(F32) * leaving.astype(F32), axis=0, keepdims=True)
                slope[at, lanes] = summed(onward, change) + closing
                kept = marks_n[GROUP - 1 :, 1:2] * jnp.exp(end)
                state_grad[head] = kept * state_grad[head] + tn(grad, (query_in.astype(F32) * entering).astype(BF16))
        grad_gate = (slope[...] * sigmoid(-gate) * (1.0 / 16.0)).astype(BF16)
        gg_out[...] = grad_gate.T
        part = nn(grad_gate, ro[...])

        @pl.when(h == 0)
        def _():
            low[...] = part

        @pl.when(h > 0)
        def _():
            low[...] += part

        @pl.when(h == steps - 1)
        def _():
            row = lax.broadcasted_iota(jnp.int32, (LANES, LANES), 0)
            lane = lax.broadcasted_iota(jnp.int32, (LANES, LANES), 1)
            move = jnp.where((row == lane + rank) & (lane < rank), 1.0, 0.0).astype(BF16)
            low_out[...] = nn(low[...].astype(BF16), move).astype(BF16)

    return kernel_call(
        body,
        (steps,),
        [
            (queries, by_head(rows)),
            (keys, by_head(rows)),
            (values, by_head(rows)),
            (gate_pre, by_head(rows)),
            (grad_mixed, by_head(rows)),
            (states, spec((TOGETHER, blocks + 1, HEAD_V, HEAD_K), lambda h: (h, 0, 0, 0))),
            (leaving, spec((TOGETHER, HEAD_V, HEAD_K), lambda h: (h, 0, 0))),
            (first, spec((TOGETHER * HEAD_K, LANES), lambda h: (h, 2 * wide // LANES))),
            (marks, spec(marks.shape)),
            (doc_row, spec(doc_row.shape)),
        ],
        [((rows, wide), BF16, by_head(rows))] * 3
        + [
            ((wide, rows), BF16, spec((TOGETHER * HEAD_K, rows), lambda h: (h, 0))),
            ((rows, LANES), BF16, spec((rows, LANES))),
        ],
        [
            pltpu.VMEM((TOGETHER, HEAD_V, HEAD_K), F32),
            pltpu.VMEM((rows, TOGETHER * HEAD_K), F32),
            pltpu.VMEM((rows, LANES), F32),
        ],
    )


def input_back(grads, first, second, grad_rank, tokens, gain, grad_hidden):
    rows, wide = tokens.shape
    steps = wide // HEAD_K // TOGETHER
    places = ((second, 0), (first, 0), (first, steps), (second, steps))

    def body(*refs):
        grad_refs, weight_refs = refs[:4], refs[4:8]
        low_ref, table, x_ref, gain_ref, gh_ref, out_ref, total = refs[8:]
        h = pl.program_id(0)
        part = nt(grad_refs[0][...], weight_refs[0][...])
        for g, w in zip(grad_refs[1:], weight_refs[1:]):
            part = part + nt(g[...], w[...])

        @pl.when(h == 0)
        def _():
            total[...] = part + nt(low_ref[...], table[...])

        @pl.when(h > 0)
        def _():
            total[...] += part

        @pl.when(h == steps - 1)
        def _():
            x = x_ref[...].astype(F32)
            scale = lax.rsqrt(jnp.mean(x * x, axis=1, keepdims=True) + 1e-06)
            unit = x * scale
            grad = total[...] * gain_ref[...]
            out_ref[...] = gh_ref[...] + scale * (grad - unit * jnp.mean(grad * unit, axis=1, keepdims=True))

    whole = spec((rows, wide))
    return kernel_call(
        body,
        (steps,),
        [(g, by_head(rows)) for g in grads]
        + [(w, by_head(wide, start)) for w, start in places]
        + [
            (grad_rank, spec((rows, LANES))),
            (first, spec((wide, LANES), lambda h: (0, 2 * wide // LANES))),
            (tokens, whole),
            (gain, spec((1, wide))),
            (grad_hidden, whole),
        ],
        [((rows, wide), F32, whole)],
        [pltpu.VMEM((rows, wide), F32)],
    )[0]


def finish(terms, weights, turned_in, gain, middle, w_middle, rank, head_rows):
    rows, width = weights[0].shape
    count = len(weights)

    def body(*refs):
        term_refs, weight_refs = refs[: len(terms)], refs[len(terms) : len(terms) + count]
        in_ref, gain_ref, wm_ref = refs[len(terms) + count : len(terms) + count + 3]
        middle_refs = refs[len(terms) + count + 3 : len(terms) + count + 3 + len(middle)]
        outs, middle_outs = refs[len(terms) + count + 3 + len(middle) : -7], refs[-7:-5]
        in_out, out_out, bias_out, head_out, gain_out = refs[-5:]

        def summed_terms(at, term_refs=term_refs):
            total = term_refs[0][:, at].astype(F32)
            for t in term_refs[1:]:
                total = total + t[:, at].astype(F32)
            return total

        for n, out in enumerate(middle_outs):
            out[...] = summed_terms(slice(n * width, (n + 1) * width), middle_refs)
        by_row = jnp.sum(wm_ref[...].astype(F32) * middle_outs[0][...], axis=1, keepdims=True)
        for n, out in enumerate(outs):
            out[...] = summed_terms(slice(n * width, (n + 1) * width))
            by_row = by_row + jnp.sum(weight_refs[n][...].astype(F32) * out[...], axis=1, keepdims=True)
        table = summed_terms(slice(count * width, count * width + LANES))
        lane = lax.broadcasted_iota(jnp.int32, (rows, LANES), 1)
        turned = jnp.where(lane == LANES - 1, by_row, table).T
        in_out[...] = turned[:rank]
        out_out[...] = turned[rank : 2 * rank]
        bias_out[...] = turned[2 * rank : 2 * rank + 1]
        head_out[...] = turned[2 * rank + 3 : 2 * rank + 4, :head_rows]
        by_rank = jnp.sum(in_ref[...].astype(F32) * turned[:rank], axis=0, keepdims=True)
        gain_out[...] = (turned[LANES - 1 :] + by_rank) / gain_ref[...].astype(F32)

    ins = [*terms, *weights, turned_in, gain, w_middle, *middle]
    shapes = [(rows, width)] * (count + 2) + [(rank, rows), (rank, rows), (1, rows), (1, head_rows), (1, rows)]
    return kernel_call(body, (1,), [(a, spec(a.shape)) for a in ins], [(o, F32, spec(o)) for o in shapes])


def then(earlier, later):
    scale = later[:, HEAD_V:].astype(F32)
    state = scale[:, :1] * earlier[:, :HEAD_V].astype(F32) + later[:, :HEAD_V].astype(F32)
    return jnp.concatenate([state, scale * earlier[:, HEAD_V:].astype(F32)], axis=1).astype(BF16)


def nothing(like):
    return jnp.concatenate([jnp.zeros_like(like[:, :HEAD_V]), jnp.ones_like(like[:, HEAD_V:])], axis=1)


class Passing:
    def __init__(self, message, backward=False):
        _, y, x, c = place()
        height = lax.axis_size("y")
        self.core, self.sign = c, -1 if backward else 1
        if backward:
            y, x, c = height - 1 - y, 1 - x, 1 - c
        self.y, self.x, self.c = y, x, c
        heads = message.shape[0]
        self.other = flip(message, "c")
        both = jnp.where(c == 0, then(message, self.other), then(self.other, message))
        self.mine = lax.dynamic_slice_in_dim(both, self.core * (heads // 2), heads // 2, 0)

    def near(self, done=()):
        if square_plane():
            mine = after(done, self.mine)
            self.arrived = (cross(mine, False), cross(mine, True))
        else:
            self.arrived = flip(after(done, self.mine), "x")
        return self.arrived

    def distant(self, done=()):
        if square_plane():
            self.far = cross(after(done, self.arrived[1]), False)
            return self.far
        beside, mine = after(done, self.arrived, self.mine)
        self.before = jnp.where(self.x == 1, beside, nothing(mine))
        self.line = jnp.where(self.x == 1, then(beside, mine), then(mine, beside))
        self.far = [shift(self.line, "y", self.sign * j) for j in range(1, lax.axis_size("y"))]
        return self.far

    def entering(self, done=()):
        if square_plane():
            (early, late), corner = after(done, self.arrived, self.far)
            beside = jnp.where(self.core == 0, early, late)
            along = jnp.where(self.core == 0, late, early)
            line = jnp.where(self.x == 1, then(corner, along), then(along, corner))
            before = jnp.where(self.x == 1, beside, nothing(beside))
            before = jnp.where(self.y == 1, then(line, before), before)
        else:
            before, distant = after(done, self.before, self.far)
            for j, far in enumerate(distant):
                before = jnp.where(self.y > j, then(far, before), before)
        rest = flip(before, "c")
        chip = jnp.where(self.core == 0, jnp.concatenate([before, rest]), jnp.concatenate([rest, before]))
        return jnp.where(self.c == 1, then(chip, self.other), chip)[:, :HEAD_V]


def pair(value):
    return (value, flip(value, "c"))


def document_of(positions, starts):
    return jnp.sum((starts[None, :] <= positions[:, None]).astype(jnp.int32), axis=1) - 1


def documents(starts, rows):
    _, y, x, c = place()
    positions = ((y * 2 + x) * 2 + c) * rows + jnp.arange(rows, dtype=jnp.int32)
    doc = document_of(positions, starts)
    before = document_of(positions - 1, starts)
    blocks = doc.reshape(-1, GROUP)
    entering = (blocks == before.reshape(-1, GROUP)[:, :1]).reshape(-1)
    tail = (blocks == blocks[:, -1:]).reshape(-1)
    columns = [doc, entering, tail, doc == before[0], doc == doc[-1]]
    marks = jnp.stack([a.astype(F32) for a in columns] + [jnp.zeros((rows,), F32)] * 3, axis=1)
    return marks, doc.astype(F32).reshape(1, rows)


def pair(value):
    return (value, flip(value, "c"))


def shards(tokens, cotangent, doc_starts, *weights):
    (
        gain_one, w_query, w_key, w_value, w_swish, rank_in, rank_out, bias, head_gain, w_output, gain_two,
        w_gate, w_up, w_down,
    ) = weights
    rows, width = tokens.shape
    own, rank, ff = w_query.shape[0], rank_in.shape[1], w_gate.shape[1]
    devices = width // own
    _, _, _, c = place()

    table_columns = 2 * width + LANES
    square_weights = jnp.concatenate([w_query, w_swish, w_output], axis=1)

    first = first_weights(w_key, w_value, rank_in.T, rank_out, (bias, gain_one, gain_two, head_gain))
    wait_for = first
    marks, doc_row = documents(doc_starts[0], rows)
    fast = square_plane() and own % 16 == 0
    depth = lax.axis_size("z")

    def by_distance(base, odd, even):
        return jnp.stack([base] + [(odd if k % 2 else even)[(k - 1) // 2] for k in range(1, depth)])

    def odd_shifts(a):
        return [shift(a, "z", k) for k in range(1, depth, 2)]

    def even_shifts(a):
        return [shift(a, "z", k) for k in range(2, depth, 2)]

    if fast:
        half = width // 2
        keep = lax.dynamic_slice_in_dim(w_down, c * half, half, 1)
        other = flip(lax.dynamic_slice_in_dim(w_down, (1 - c) * half, half, 1), "c")
        chip_down = jnp.where(c == 0, jnp.concatenate([keep, other]), jnp.concatenate([other, keep]))
        one = by_distance(first, odd_shifts(first), even_shifts(first))
        square_next = after(one, square_weights)
        one_early, one_late, one_other = cross(one, False), cross(one, True), flip(one, "c")
        two_odd = odd_shifts(square_next)
        now = (one_early, one_late, two_odd, one_other)
        one_next, one_late, square_next = after(now, one_early, one_late, square_weights)
        one_corner = cross(one_next, True)
        two_even = even_shifts(square_next)
        one_others = [one_other, flip(one_next, "c"), flip(one_late, "c")]
        wait_for = now = (one_corner, two_even, one_others)
        one, two, chip_down = after(now, one, by_distance(square_weights, two_odd, two_even), chip_down)
        first = assemble(gathered(one, one_early, one_late, one_corner, one_others), own, (width, table_columns))
        two_early = cross(two, False)
        three_odd = odd_shifts(chip_down)
        first, two, chip_down = after((first, two_early, three_odd), first, two, chip_down)
        two_late = cross(two, True)
        three_even = even_shifts(chip_down)
    else:
        first = lax.all_gather(first, AXES, axis=0, tiled=True)
        second = lax.all_gather(square_weights, AXES, axis=0, tiled=True)
        w_down_all = lax.all_gather(w_down, AXES, axis=0, tiled=True)
    gate_shard, up_shard = after(wait_for, w_gate, w_up)
    w_both = lax.all_gather(jnp.concatenate([gate_shard, up_shard], axis=1), AXES, axis=0, tiled=True)
    normed, normed_turned, low, keys, values, gate_pre, message, vectors = project(tokens, first, marks, rank)
    row_one, row_two = vectors[1:2], vectors[2:3]
    row_head = vectors[3].reshape(devices, own)[:, : head_gain.shape[0]].reshape(1, HEAD_V)
    if fast:
        message, two_early, two_late = after((two_late, three_even), message, two_early, two_late)
    both, down_pair = pair(normed_turned), pair(cotangent)
    passing = Passing(message)
    if fast:
        two_next, two_late = after(passing.mine, two_early, two_late)
        two_corner = cross(two_next, True)
        two_others = [flip(a, "c") for a in (two, two_next, two_late)]
        now = (passing.near(), two_corner, both, down_pair, two_others)
        two_corner = after(now, two_corner)
        two_others.append(flip(two_corner, "c"))
        three = by_distance(chip_down, three_odd, three_even)
        now = (passing.distant(now), two_others, three)
        three, two = after(now, three, two)
        three_early = cross(three, False)
        second = assemble(gathered(two, two_early, two_late, two_corner, two_others), own, (width, 3 * width))
        entered = passing.entering(now)
        now = (entered, second, three_early)
        entered, second, three, three_early = after(now, entered, second, three, three_early)
        three_late, three_corner = cross(three, True), cross(three_early, True)
    else:
        passing.near()
        passing.distant()
        entered = passing.entering()
    queries, mixed, swish, gated, hidden, normed_two, two_turned, states = mixer(
        normed, keys, values, gate_pre, entered, second, row_head, tokens, row_two, marks, doc_row
    )
    if fast:
        hidden, three = after((three_late, three_corner), hidden, three)
        w_down_all = assemble(
            gathered(three, three_early, three_late, three_corner), chip_down.shape[0], (ff, width), True
        )
    two_pair, gated_pair = pair(two_turned), pair(gated)
    output, inner, grad_gate, grad_up, grad_hidden, grad_low = feed(
        normed_two, cotangent, w_both, w_down_all, hidden, row_two
    )

    gate_pair = pair(grad_gate)
    inner, grad_up, grad_low = after(gate_pair, inner, grad_up, grad_low)
    gate = weight_grads([(two_pair, [gate_pair])], ff // 2)
    inner_pair, up_pair = pair(inner), pair(grad_up)
    inner_pair, grad_low = after(gate.blocks, inner_pair, grad_low)
    down = weight_grads([(inner_pair, [down_pair])], 512, True, by_z=True)
    down_blocks = down.blocks
    down.zeroth()
    grad_low = after(down_blocks, grad_low)
    grad_mixed, grad_swish, grad_head_gain, message_back = head_back(
        grad_low, second, mixed, swish, row_head, queries, gate_pre, message[:, HEAD_V:], marks
    )
    now = (gate.first(), message_back)
    passing = Passing(after(now, message_back), True)
    now = passing.mine
    swish_pair, low_pair = pair(after(now, grad_swish)), pair(after(now, grad_low))
    up = weight_grads([(two_pair, [after(now, up_pair)])], ff // 2)
    middle = weight_grads([(both, [swish_pair]), (gated_pair, [low_pair])], width)
    now = (passing.near(), gate.second(now), up.blocks, middle.blocks)
    now = passing.distant(now)
    leaving = passing.entering(now)
    now = leaving
    grad_query, grad_key, grad_value, grad_gate_pre, grad_rank = mixer_back(
        queries, keys, values, gate_pre, grad_mixed, states, leaving, first, marks, doc_row, rank
    )
    now = (up.first(now), grad_query)
    up.second(now)
    middle.first(now)
    inside_pairs = [pair(a) for a in after(now, grad_query, grad_key, grad_value, grad_rank, grad_gate_pre)]
    head_terms = grad_head_gain + flip(grad_head_gain, "c")
    head_terms = jnp.pad(head_terms.reshape(devices, -1), ((0, 0), (0, own - head_gain.shape[0]))).reshape(width, 1)
    base = jnp.pad(head_terms.astype(BF16), ((0, 0), (2 * rank + 3, LANES - 2 * rank - 4)))
    inside = weight_grads(
        [(both, inside_pairs[:3])],
        width,
        table=([(both, inside_pairs[3]), (inside_pairs[4], pair(low))], base),
    )
    now = (inside.blocks, middle.arrived, up.through)
    gate.through, up.through = after(inside.blocks, gate.through, up.through)
    gates_part = gate.third(up)
    input_grad = input_back(
        (grad_query, grad_key, grad_value, grad_swish), first, second, after(now, grad_rank), tokens, row_one,
        grad_hidden,
    )
    now = (input_grad, inside.first(now), middle.second(now))
    down.first(now)
    middle_terms = middle.third_terms()
    inside.second(now)
    down.second(inside.through)
    inside_terms = inside.third_terms()
    down_part = down.result()

    chip_half = ff // devices
    down_sum = wide(down_part)
    keep = lax.dynamic_slice_in_dim(down_sum, c * chip_half, chip_half, 0)
    other = flip(lax.dynamic_slice_in_dim(down_sum, (1 - c) * chip_half, chip_half, 0), "c")
    down_sum = jnp.where(c == 0, jnp.concatenate([keep, other], 1), jnp.concatenate([other, keep], 1))
    g_gate, g_up = wide(gates_part[:, :ff]), wide(gates_part[:, ff:])
    g_gain_two = (jnp.sum(wide(w_gate) * g_gate, axis=1) + jnp.sum(wide(w_up) * g_up, axis=1)) / wide(gain_two)
    g_query, g_key, g_value, g_swish, g_output, g_rank_in, g_rank_out, g_bias, g_head, g_gain_one = finish(
        inside_terms, (w_query, w_key, w_value), rank_in.T, gain_one.reshape(1, own), middle_terms, w_swish,
        rank, head_gain.shape[0],
    )
    return (
        output, input_grad, g_gain_one[0], g_query, g_key, g_value, g_swish, g_rank_in.T, g_rank_out, g_bias[0], g_head[0],
        g_output, g_gain_two, g_gate, g_up, down_sum,
    )


def solution(mesh):
    fsdp, seq = mesh.shape["fsdp"], mesh.shape["seq"]
    inner = Mesh(mesh.devices.reshape(fsdp, seq // 4, 2, 2), AXES)
    rows, vector, columns = P(AXES, None), P(AXES), P(None, AXES)
    in_specs = (rows, rows, P("z", None), vector, rows, rows, rows, rows, rows, columns, vector, vector, rows, vector) + (rows,) * 3
    out_specs = (rows, rows, vector) + (rows,) * 5 + (columns, vector, vector, rows, vector) + (rows,) * 3
    return jax.shard_map(shards, mesh=inner, in_specs=in_specs, out_specs=out_specs, check_vma=False)
```

```python
from functools import partial

import jax
import jax.numpy as jnp
from jax import lax
from jax.experimental import pallas as pl
from jax.experimental.pallas import tpu as pltpu
from jax.sharding import Mesh
from jax.sharding import PartitionSpec as P

HEAD_K = 256
HEAD_V = 256
GROUP = 64
LANES = 128
TOGETHER = 2
AXES = ("z", "y", "x", "c")
VMEM = 56 * 1024 * 1024
QUICK = pl.CostEstimate(flops=0, bytes_accessed=0, transcendentals=0)
F32 = jnp.float32
BF16 = jnp.bfloat16


def shift(value, axis, step):
    size = lax.axis_size(axis)
    return lax.ppermute(value, axis, [(i, (i + step) % size) for i in range(size)])


def flip(value, axis):
    return shift(value, axis, 1)


def place():
    return tuple(lax.axis_index(a) for a in AXES)


def after(done, *values):
    out = lax.optimization_barrier((values, done))[0]
    return out[0] if len(values) == 1 else out


def square_plane():
    return lax.axis_size("y") == 2


def cross(value, late):
    perm = [(i, i ^ (2 if (i % 2 == 0) != late else 4)) for i in range(8)]
    return lax.ppermute(value, ("y", "x", "c"), perm)


def neighbour(early, late, core):
    _, y, x, _ = place()
    by_x = jnp.where(core == 0, early, late)
    by_y = jnp.where(core == 0, late, early)
    return (y + by_y) % 2, (x + by_x) % 2


def gathered(own, early, late, corner, others=()):
    pieces = [(own, 0, 0, 0), (early, 1, 0, 0), (late, 0, 1, 0), (corner, 1, 1, 0)]
    others = list(others) + [flip(a, "c") for a, _, _, _ in pieces[len(others) :]]
    return pieces + [(a, i, j, 1) for a, (_, i, j, _) in zip(others, pieces)]


def sources(pieces):
    z, _, _, c = place()
    depth = lax.axis_size("z")
    chips, cores = [], []
    for _, early, late, other in pieces:
        core = (c + other) % 2
        y, x = neighbour(early, late, core)
        for k in range(depth):
            chips.append((((z - k) % depth) * 2 + y) * 2 + x)
            cores.append(core)
    return jnp.stack(chips + cores).astype(jnp.int32)


def assemble(pieces, rows, shape, by_columns=False):
    where = sources(pieces)
    arrays = [p[0] for p in pieces]
    depth = arrays[0].shape[0]
    blocks = [(n, k) for n in range(len(pieces)) for k in range(depth)]
    total = len(blocks)

    def body(where_ref, *refs):
        ins, out, sem = refs[: len(arrays)], refs[-2], refs[-1]
        for at, (n, k) in enumerate(blocks):
            chip, core = where_ref[at], where_ref[total + at]
            if by_columns:
                width = shape[1] // 2
                goal = out.at[
                    pl.ds(pl.multiple_of(chip * rows, rows), rows),
                    pl.ds(pl.multiple_of(core * width, width), width),
                ]
            else:
                goal = out.at[pl.ds(pl.multiple_of((chip * 2 + core) * rows, rows), rows), :]
            pltpu.make_async_copy(ins[n].at[k], goal, sem).start()
        pltpu.make_async_copy(out, out, sem).wait()

    return pl.pallas_call(
        body,
        grid_spec=pltpu.PrefetchScalarGridSpec(
            num_scalar_prefetch=1,
            grid=(1,),
            in_specs=[pl.BlockSpec(memory_space=pl.ANY)] * len(arrays),
            out_specs=pl.BlockSpec(shape, lambda n, s: (0, 0)),
            scratch_shapes=[pltpu.SemaphoreType.DMA],
        ),
        out_shape=jax.ShapeDtypeStruct(shape, BF16),
        compiler_params=pltpu.CompilerParams(vmem_limit_bytes=VMEM),
        cost_estimate=QUICK,
    )(where, *arrays)


def layout(by_z):
    _, _, _, c = place()
    depth, height = lax.axis_size("z"), lax.axis_size("y")
    if not square_plane():
        return [jnp.arange(depth * height * 2, dtype=jnp.int32)]

    def column(early, late):
        y, x = neighbour(early, late, c)
        return (jnp.arange(depth, dtype=jnp.int32) * 2 + y) * 2 + x

    columns = [column(1, 0), column(1, 1), column(0, 1), column(0, 0)]
    if by_z:
        return [jnp.stack(columns, axis=1).reshape(-1)]
    return [jnp.concatenate(columns[:2]), *columns[2:]]


def wide(a):
    return a.astype(F32)


class Sum:
    def __init__(self, blocks):
        self.blocks = blocks
        self.depth = lax.axis_size("z")

    def zeroth(self, done=()):
        if square_plane():
            (blocks,) = after(done, self.blocks, ())[0]
            _, rows, width = blocks.shape
            part = lax.psum_scatter(blocks.reshape(-1, width), "z", scatter_dimension=0, tiled=True)
            part = part.reshape(4, rows, width)
            self.blocks, self.depth = [part[:2], part[2:3], part[3:]], 1
        return self.blocks

    def first(self, done=()):
        self.arrived = cross(after(done, self.blocks[0]), False) if square_plane() else ()
        return self.arrived

    def second(self, done=(), *others):
        parts = (self, *others)
        if not square_plane():
            for p in parts:
                p.through = ()
            return ()
        sums = []
        for p in parts:
            arrived, kept = after(done, p.arrived, p.blocks[1])
            sums.append((wide(kept) + wide(arrived[p.depth :])).astype(BF16))
        through = cross(sums[0] if len(sums) == 1 else jnp.concatenate(sums, axis=2), True)
        at = 0
        for p, part in zip(parts, sums):
            p.through = through[:, :, at : at + part.shape[2]]
            at += part.shape[2]
        return through

    def total(self):
        return (wide(self.blocks[2]) + wide(self.arrived[: self.depth]) + wide(self.through)).astype(BF16)

    def result(self):
        return self.total()[0] if square_plane() else self.third()

    def third(self, *others):
        parts = (self, *others)
        if square_plane():
            axes, totals = "z", [p.total() for p in parts]
        else:
            axes, totals = ("z", "y", "x"), [p.blocks[0] for p in parts]
        total = totals[0] if len(totals) == 1 else jnp.concatenate(totals, axis=2)
        return lax.psum_scatter(total.reshape(-1, total.shape[-1]), axes, scatter_dimension=0, tiled=True)

    def third_terms(self):
        if not square_plane():
            return [self.third()]
        depth = lax.axis_size("z")
        total, z = self.total(), lax.axis_index("z")
        block = [lax.dynamic_index_in_dim(total, (z + k) % depth, 0, False) for k in range(depth)]
        return [block[0]] + [shift(block[k], "z", k) for k in range(1, depth)]


def weight_grads(groups, tile, halves=False, table=None, by_z=False):
    _, _, _, c = place()
    chips = layout(by_z)
    spans = [a.shape[0] for a in chips]
    chips = jnp.concatenate(chips)
    count = chips.shape[0]
    lefts = [left for left, _ in groups]
    rights = [right for _, group in groups for right in group]
    owner = [n for n, (_, group) in enumerate(groups) for _ in group]
    height, tokens = lefts[0][0].shape
    each = rights[0][0].shape[1] // (2 if halves else 1)
    width = each * len(rights)
    rows = height // (count if halves else 2 * count)
    starts = chips * rows if halves else (chips * 2 + c) * rows

    if rows % 16:
        products = []
        for n, right in zip(owner, rights):
            product = nn(jnp.concatenate(lefts[n], axis=1), jnp.concatenate(right)).astype(BF16)
            if halves:
                product = lax.dynamic_slice_in_dim(product, c * each, each, 1).reshape(count, rows, each)
            else:
                product = lax.dynamic_index_in_dim(product.reshape(count, 2, rows, each), c, 1, False)
            products.append(product)
        if table is not None:
            product = wide(table[1])
            for left, right in table[0]:
                product = product + nn(jnp.concatenate(left, axis=1), jnp.concatenate(right))
            product = product.astype(BF16).reshape(count, 2, rows, LANES)
            products.append(lax.dynamic_index_in_dim(product, c, 1, False))
        product = jnp.take(jnp.concatenate(products, axis=2), chips, axis=0)
        blocks, at = [], 0
        for span in spans:
            blocks.append(product[at : at + span])
            at += span
        return Sum(blocks)

    strips = each // tile
    first_tile = c * strips if halves else jnp.int32(0)
    numbers = jnp.concatenate([starts, first_tile[None]]).astype(jnp.int32)

    steps = width // tile
    terms, base = table if table is not None else ((), None)
    flat = [a for left in lefts for a in left] + [a for right in rights for a in right]
    narrow = [a for left, right in terms for a in (*left, *right)]
    if table is not None:
        narrow.append(base)

    def body(numbers_ref, *refs):
        left_refs, right_refs = refs[: 2 * len(lefts)], refs[2 * len(lefts) : len(flat)]
        narrow_refs = refs[len(flat) : len(flat) + len(narrow)]
        outs, (chosen, total, based) = refs[len(flat) + len(narrow) : -3], refs[-3:]
        step = pl.program_id(0)

        def start(at):
            return pl.ds(pl.multiple_of(numbers_ref[at], 16), rows)

        def choose(lo_ref, ls_ref):
            for at in range(count):
                chosen[at * rows : (at + 1) * rows, :tokens] = lo_ref[start(at), :]
                chosen[at * rows : (at + 1) * rows, tokens:] = ls_ref[start(at), :]

        def put(product, columns):
            at = 0
            for out, span in zip(outs, spans):
                out[:, :, :columns] = product[at : at + span * rows].reshape(span, rows, columns)
                at += span * rows

        def strip(ro_ref, rs_ref):
            both = jnp.concatenate([ro_ref[...], rs_ref[...]], axis=0)
            put(nn(chosen[...], both).astype(BF16), tile)

        def term(n):
            lo_ref, ls_ref, ro_ref, rs_ref = narrow_refs[4 * n : 4 * n + 4]
            choose(lo_ref, ls_ref)
            both = jnp.concatenate([ro_ref[...], rs_ref[...]], axis=0)
            product = nn(chosen[...], both)
            if n == 0:
                total[...] = product
            else:
                total[...] += product
            if n == len(terms) - 1:
                for at in range(count):
                    based[at * rows : (at + 1) * rows, :] = narrow_refs[-1][start(at), :]
                put((total[...] + wide(based[...])).astype(BF16), LANES)

        for n in range(len(lefts)):
            pl.when(step == owner.index(n) * strips)(partial(choose, *left_refs[2 * n : 2 * n + 2]))
        if len(rights) == 1:
            strip(*right_refs)
        else:
            for n in range(len(rights)):
                pl.when(step // strips == n)(partial(strip, *right_refs[2 * n : 2 * n + 2]))
        for n in range(len(terms)):
            pl.when(step == steps + n)(partial(term, n))

    def column(n):
        return lambda step, s: (0, jnp.clip(step - n * strips, 0, strips - 1) + s[count])

    def full(a):
        return pl.BlockSpec(a.shape, lambda n, s: (0,) * a.ndim)

    right_specs = [pl.BlockSpec((tokens, tile), column(n)) for n in range(len(rights)) for _ in range(2)]
    columns = width + (LANES if table is not None else 0)
    last = steps - (table is None)
    outs = [(span, rows, columns) for span in spans]
    blocks = pl.pallas_call(
        body,
        grid_spec=pltpu.PrefetchScalarGridSpec(
            num_scalar_prefetch=1,
            grid=(steps + len(terms),),
            in_specs=[full(a) for left in lefts for a in left] + right_specs + [full(a) for a in narrow],
            out_specs=[pl.BlockSpec((n, rows, tile), lambda n, s: (0, 0, jnp.minimum(n, last))) for n, _, _ in outs],
            scratch_shapes=[
                pltpu.VMEM((count * rows, 2 * tokens), BF16),
                pltpu.VMEM((count * rows, LANES), F32),
                pltpu.VMEM((count * rows, LANES), BF16),
            ],
        ),
        out_shape=[jax.ShapeDtypeStruct(o, BF16) for o in outs],
        compiler_params=pltpu.CompilerParams(vmem_limit_bytes=VMEM),
        cost_estimate=QUICK,
    )(numbers, *flat, *narrow)
    return Sum(blocks)


def nn(left, right):
    return jnp.dot(left, right, preferred_element_type=F32)


def nt(left, right):
    return lax.dot_general(left, right, (((1,), (1,)), ((), ())), preferred_element_type=F32)


def tn(left, right):
    return lax.dot_general(left, right, (((0,), (0,)), ((), ())), preferred_element_type=F32)


def summed(ones, values):
    high = values.astype(BF16)
    low = (values - high.astype(F32)).astype(BF16)
    return nn(ones, high) + nn(ones, low)


def triangle(size, relation, block=None):
    row = lax.broadcasted_iota(jnp.int32, (size, size), 0)
    column = lax.broadcasted_iota(jnp.int32, (size, size), 1)
    chosen = relation(row, column)
    if block is not None:
        chosen = chosen & (row // block == column // block)
    return jnp.where(chosen, 1.0, 0.0).astype(BF16)


def log_decay(gate_pre):
    return (jnp.minimum(gate_pre, 0.0) - jnp.log1p(jnp.exp(-jnp.abs(gate_pre)))) * (1.0 / 16.0)


def sigmoid(v):
    return 1.0 / (1.0 + jnp.exp(-v))


def spec(shape, index=None):
    index = index or (lambda *_: (0,) * len(shape))
    return pl.BlockSpec(shape, index)


def by_head(rows, start=0):
    return spec((rows, TOGETHER * HEAD_K), lambda h: (0, start + h))


def spans(count=TOGETHER):
    return [slice(n * HEAD_K, (n + 1) * HEAD_K) for n in range(count)]


def by_spans(function, *arrays):
    return jnp.concatenate([function(*[a[:, at] for a in arrays]) for at in spans()], axis=1)


def head_mean(values):
    return by_spans(lambda a: jnp.broadcast_to(jnp.mean(a, axis=1, keepdims=True), a.shape), values)


def repeated(row):
    return jnp.concatenate([row] * TOGETHER, axis=1)


def kernel_call(body, grid, ins, outs, scratch=()):
    return pl.pallas_call(
        body,
        grid=grid,
        in_specs=[s for _, s in ins],
        out_specs=[s for _, _, s in outs],
        out_shape=[jax.ShapeDtypeStruct(shape, dtype) for shape, dtype, _ in outs],
        scratch_shapes=list(scratch),
        compiler_params=pltpu.CompilerParams(vmem_limit_bytes=VMEM),
        cost_estimate=QUICK,
    )(*[a for a, _ in ins])


MESSAGE = HEAD_V + 16


def unit_columns(rows, columns, start):
    row = lax.broadcasted_iota(jnp.int32, (rows, columns), 0)
    column = lax.broadcasted_iota(jnp.int32, (rows, columns), 1)
    return jnp.where(column == row + start, 1.0, 0.0).astype(BF16)


def first_weights(w_key, w_value, turned_in, rank_out, vectors):
    rows, width = w_key.shape
    rank = turned_in.shape[0]

    def body(wk, wv, ri, ro, *refs):
        vector_refs, out = refs[:-1], refs[-1]
        out[:, :width] = wk[...]
        out[:, width : 2 * width] = wv[...]
        table = tn(ri[...], unit_columns(rank, LANES, 0)) + tn(ro[...], unit_columns(rank, LANES, rank))
        for n, v in enumerate(vector_refs):
            mine = unit_columns(v.shape[1], rows, 0)
            table = table + tn(nn(v[...], mine).astype(BF16), unit_columns(1, LANES, 2 * rank + n))
        out[:, 2 * width :] = table.astype(BF16)

    ins = [w_key, w_value, turned_in, rank_out, *[v.reshape(1, -1) for v in vectors]]
    shape = (rows, 2 * width + LANES)
    return kernel_call(body, (1,), [(a, spec(a.shape)) for a in ins], [(shape, BF16, spec(shape))])[0]


def project(tokens, weights, marks, rank):
    rows, width = tokens.shape
    heads = width // HEAD_K
    steps = heads // TOGETHER
    at_table = 2 * width // LANES

    def body(
        x_ref, wk, wv, table, part_ref, marks_ref, n_out, turned_out, low_out, k_out, v_out, g_out, m_out, vectors_out
    ):
        @pl.when(pl.program_id(0) == 0)
        def _():
            vectors = nt(unit_columns(8, LANES, 2 * rank), table[...])
            vectors_out[...] = vectors
            x = x_ref[...].astype(F32)
            scale = lax.rsqrt(jnp.mean(x * x, axis=1, keepdims=True) + 1e-06)
            n_out[...] = (x * scale * vectors[1:2]).astype(BF16)
            turned_out[...] = n_out[...].T
            low = nn(n_out[...], table[...]).astype(BF16)
            lane = lax.broadcasted_iota(jnp.int32, (LANES, LANES), 1)
            row = lax.broadcasted_iota(jnp.int32, (LANES, LANES), 0)
            move = jnp.where((lane == row + rank) & (row < rank), 1.0, 0.0).astype(BF16)
            one = jnp.where(lax.broadcasted_iota(jnp.int32, (rows, LANES), 1) == 2 * rank, 1.0, 0.0)
            low_out[...] = (nn(low, move) + one).astype(BF16)

        normed = n_out[...]
        key = nn(normed, wk[...]).astype(BF16)
        value = nn(normed, wv[...]).astype(BF16)
        k_out[...] = key
        v_out[...] = value
        gate = nt(low_out[...], part_ref[...])
        g_out[...] = gate
        decay = log_decay(gate)
        later = summed(triangle(rows, lambda i, j: j > i), decay)
        last = marks_ref[:, 4:5]
        finish = (key.astype(F32) * jnp.exp(later) * last).astype(BF16)
        total = jnp.exp(jnp.sum(decay, axis=0, keepdims=True)) * marks_ref[rows - 1 :, 3:4]
        for n, at in enumerate(spans()):
            m_out[n, :HEAD_V] = tn(value[:, at], finish[:, at]).astype(BF16)
            m_out[n, HEAD_V:] = jnp.broadcast_to(total[:, at], (MESSAGE - HEAD_V, HEAD_K)).astype(BF16)

    return kernel_call(
        body,
        (steps,),
        [
            (tokens, spec((rows, width))),
            (weights, by_head(width)),
            (weights, by_head(width, steps)),
            (weights, spec((width, LANES), lambda h: (0, at_table))),
            (weights, spec((TOGETHER * HEAD_K, LANES), lambda h: (h, at_table))),
            (marks, spec(marks.shape)),
        ],
        [
            ((rows, width), BF16, spec((rows, width))),
            ((width, rows), BF16, spec((width, rows))),
            ((rows, LANES), BF16, spec((rows, LANES))),
            ((rows, width), BF16, by_head(rows)),
            ((rows, width), BF16, by_head(rows)),
            ((rows, width), F32, by_head(rows)),
            ((heads, MESSAGE, HEAD_K), BF16, spec((TOGETHER, MESSAGE, HEAD_K), lambda h: (h, 0, 0))),
            ((8, width), F32, spec((8, width))),
        ],
    )


def scaled(queries):
    return queries.astype(F32) * HEAD_K ** (-0.5)


def mixer(normed, keys, values, gate_pre, entered, weights, head_gain, tokens, gain, marks, doc_row):
    rows, wide = tokens.shape
    heads = wide // HEAD_K
    steps = heads // TOGETHER
    blocks = rows // GROUP

    def body(
        n_ref, k_ref, v_ref, g_ref, s_ref, wq, ws, hg_ref, wo, x_ref, gain_ref, marks_ref, doc_ref,
        q_ref, mixed_out, swish_out, gated_out, hidden_out, two_out, two_turned, states_out, state, total,
    ):
        h = pl.program_id(0)
        q_ref[...] = nn(n_ref[...], wq[...]).astype(BF16)
        swish = nn(n_ref[...], ws[...])
        swish_out[...] = swish
        along = summed(triangle(rows, lambda i, j: j <= i, GROUP), log_decay(g_ref[...]))
        causal = triangle(GROUP, lambda i, j: j <= i) > 0
        run_all, key_all = along, k_ref[...].astype(F32)
        query_all = (scaled(q_ref[...]) * jnp.exp(run_all)).astype(BF16)
        key_in_all = (key_all * jnp.exp(-run_all)).astype(BF16)
        for head in range(TOGETHER):
            state[head] = s_ref[head].astype(F32)
        for n in range(blocks):
            at = slice(n * GROUP, (n + 1) * GROUP)
            marks_n = marks_ref[at]
            allowed = causal & (marks_n[:, 0:1] == doc_ref[:, at])
            run = run_all[at]
            end = run[GROUP - 1 :]
            key_out_all = (key_all[at] * jnp.exp(end - run) * marks_n[:, 2:3]).astype(BF16)
            kept = marks_n[GROUP - 1 :, 1:2] * jnp.exp(end)
            for head, lanes in enumerate(spans()):
                value = v_ref[at, lanes]
                query_in = query_all[at, lanes]
                scores = jnp.where(allowed, nt(query_in, key_in_all[at, lanes]), 0.0).astype(BF16)
                before = state[head].astype(BF16)
                states_out[head, n] = before
                mixed_out[at, lanes] = nn(scores, value) + marks_n[:, 1:2] * nt(query_in, before)
                state[head] = kept[:, lanes] * state[head] + tn(value, key_out_all[:, lanes])
        for head in range(TOGETHER):
            states_out[head, blocks] = state[head].astype(BF16)
        mixed = mixed_out[...]
        norm = lax.rsqrt(head_mean(mixed * mixed) + 1e-05)
        gated = (mixed * norm * repeated(hg_ref[...]) * (swish * sigmoid(swish))).astype(BF16)
        gated_out[...] = gated.T
        part = nn(gated, wo[...])

        @pl.when(h == 0)
        def _():
            total[...] = x_ref[...].astype(F32) + part

        @pl.when(h > 0)
        def _():
            total[...] += part

        @pl.when(h == steps - 1)
        def _():
            hidden = total[...]
            hidden_out[...] = hidden
            scale = lax.rsqrt(jnp.mean(hidden * hidden, axis=1, keepdims=True) + 1e-06)
            two_out[...] = (hidden * scale * gain_ref[...]).astype(BF16)
            two_turned[...] = two_out[...].T

    return kernel_call(
        body,
        (steps,),
        [
            (normed, spec((rows, wide))),
            (keys, by_head(rows)),
            (values, by_head(rows)),
            (gate_pre, by_head(rows)),
            (entered, spec((TOGETHER, HEAD_V, HEAD_K), lambda h: (h, 0, 0))),
            (weights, by_head(wide)),
            (weights, by_head(wide, steps)),
            (head_gain, spec((1, HEAD_V))),
            (weights, spec((TOGETHER * HEAD_V, wide), lambda h: (h, 2))),
            (tokens, spec((rows, wide))),
            (gain, spec((1, wide))),
            (marks, spec(marks.shape)),
            (doc_row, spec(doc_row.shape)),
        ],
        [
            ((rows, wide), BF16, by_head(rows)),
            ((rows, wide), F32, by_head(rows)),
            ((rows, wide), F32, by_head(rows)),
            ((wide, rows), BF16, spec((TOGETHER * HEAD_V, rows), lambda h: (h, 0))),
            ((rows, wide), F32, spec((rows, wide))),
            ((rows, wide), BF16, spec((rows, wide))),
            ((wide, rows), BF16, spec((wide, rows))),
            ((heads, blocks + 1, HEAD_V, HEAD_K), BF16, spec((TOGETHER, blocks + 1, HEAD_V, HEAD_K), lambda h: (h, 0, 0, 0))),
        ],
        [pltpu.VMEM((TOGETHER, HEAD_V, HEAD_K), F32), pltpu.VMEM((rows, wide), F32)],
    )


def feed(normed_two, cotangent, w_both, w_down, hidden, gain):
    rows, wide = hidden.shape
    inner = w_both.shape[1] // 2
    tile = inner // 2 if inner % 256 == 0 else inner
    steps = inner // tile

    def body(
        n_ref, c_ref, wg, wu, wd, hidden_ref, gain_ref,
        out_ref, inner_out, gate_out, up_out, grad_out, low_out, forward_sum, back_sum,
    ):
        step = pl.program_id(0)
        normed = n_ref[...]
        gate = nn(normed, wg[...])
        up = nn(normed, wu[...])
        soft = sigmoid(gate)
        silu = gate * soft
        product = (silu * up).astype(BF16)
        inner_out[...] = product.T
        grad = nt(c_ref[...], wd[...])
        grad_up = (grad * silu).astype(BF16)
        grad_gate = (grad * up * (soft * (1.0 + gate * (1.0 - soft)))).astype(BF16)
        up_out[...] = grad_up
        gate_out[...] = grad_gate
        ahead = nn(product, wd[...])
        back = nt(grad_gate, wg[...]) + nt(grad_up, wu[...])

        @pl.when(step == 0)
        def _():
            forward_sum[...] = hidden_ref[...] + ahead
            back_sum[...] = back

        @pl.when(step > 0)
        def _():
            forward_sum[...] += ahead
            back_sum[...] += back

        @pl.when(step == steps - 1)
        def _():
            out_ref[...] = forward_sum[...].astype(BF16)
            hidden = hidden_ref[...]
            scale = lax.rsqrt(jnp.mean(hidden * hidden, axis=1, keepdims=True) + 1e-06)
            unit = hidden * scale
            grad = back_sum[...] * gain_ref[...]
            grad = scale * (grad - unit * jnp.mean(grad * unit, axis=1, keepdims=True))
            grad = c_ref[...].astype(F32) + grad
            grad_out[...] = grad
            low_out[...] = grad.astype(BF16)

    strip = spec((wide, tile), lambda n: (0, n))
    column = spec((rows, tile), lambda n: (0, n))
    whole = spec((rows, wide))
    return kernel_call(
        body,
        (steps,),
        [
            (normed_two, whole),
            (cotangent, whole),
            (w_both, strip),
            (w_both, spec((wide, tile), lambda n: (0, n + steps))),
            (w_down, spec((tile, wide), lambda n: (n, 0))),
            (hidden, whole),
            (gain, spec((1, wide))),
        ],
        [
            ((rows, wide), BF16, whole),
            ((inner, rows), BF16, spec((tile, rows), lambda n: (n, 0))),
            ((rows, inner), BF16, column),
            ((rows, inner), BF16, column),
            ((rows, wide), F32, whole),
            ((rows, wide), BF16, whole),
        ],
        [pltpu.VMEM((rows, wide), F32), pltpu.VMEM((rows, wide), F32)],
    )


def head_back(grad_low, weights, mixed, swish, head_gain, queries, gate_pre, decays, marks):
    rows, wide = mixed.shape
    heads = wide // HEAD_K
    steps = heads // TOGETHER

    def body(gh_ref, wo, mixed_ref, swish_ref, hg_ref, q_ref, g_ref, d_ref, marks_ref, gm_out, gs_out, hg_out, m_out):
        grad = nt(gh_ref[...], wo[...])
        mixed = mixed_ref[...]
        swish = swish_ref[...]
        soft = sigmoid(swish)
        silu = swish * soft
        norm = lax.rsqrt(head_mean(mixed * mixed) + 1e-05)
        unit = mixed * norm
        gain = repeated(hg_ref[...])
        gs_out[...] = (grad * unit * gain * (soft * (1.0 + swish * (1.0 - soft)))).astype(BF16)
        by_gain = jnp.sum(grad * unit * silu, axis=0, keepdims=True)
        by_gain = sum(by_gain[:, at] for at in spans())

        @pl.when(pl.program_id(0) == 0)
        def _():
            hg_out[...] = by_gain

        @pl.when(pl.program_id(0) > 0)
        def _():
            hg_out[...] += by_gain

        inner = grad * gain * silu
        grad_mixed = norm * (inner - unit * head_mean(inner * unit))
        gm_out[...] = grad_mixed.astype(BF16)
        along = summed(triangle(rows, lambda i, j: j <= i), log_decay(g_ref[...]))
        query_in = (scaled(q_ref[...]) * jnp.exp(along)).astype(BF16)
        entry = (grad_mixed * marks_ref[:, 3:4]).astype(BF16)
        for n, at in enumerate(spans()):
            m_out[n, :HEAD_V] = tn(entry[:, at], query_in[:, at]).astype(BF16)
            m_out[n, HEAD_V:] = d_ref[n]

    return kernel_call(
        body,
        (steps,),
        [
            (grad_low, spec((rows, wide))),
            (weights, spec((TOGETHER * HEAD_V, wide), lambda h: (h, 2))),
            (mixed, by_head(rows)),
            (swish, by_head(rows)),
            (head_gain, spec((1, HEAD_V))),
            (queries, by_head(rows)),
            (gate_pre, by_head(rows)),
            (decays, spec((TOGETHER, MESSAGE - HEAD_V, HEAD_K), lambda h: (h, 0, 0))),
            (marks, spec(marks.shape)),
        ],
        [
            ((rows, wide), BF16, by_head(rows)),
            ((rows, wide), BF16, by_head(rows)),
            ((1, HEAD_V), F32, spec((1, HEAD_V))),
            ((heads, MESSAGE, HEAD_K), BF16, spec((TOGETHER, MESSAGE, HEAD_K), lambda h: (h, 0, 0))),
        ],
    )


def mixer_back(queries, keys, values, gate_pre, grad_mixed, states, leaving, first, marks, doc_row, rank):
    rows, wide = queries.shape
    heads = wide // HEAD_K
    steps = heads // TOGETHER
    blocks = rows // GROUP

    def body(
        q_ref, k_ref, v_ref, g_ref, gm_ref, s_ref, l_ref, ro, marks_ref, doc_ref,
        gq_out, gk_out, gv_out, gg_out, low_out, state_grad, slope, low,
    ):
        h = pl.program_id(0)
        gate = g_ref[...]
        along = summed(triangle(rows, lambda i, j: j <= i, GROUP), log_decay(gate))
        causal = triangle(GROUP, lambda i, j: j <= i) > 0
        onward = triangle(GROUP, lambda i, j: j >= i)
        for head in range(TOGETHER):
            state_grad[head] = l_ref[head].astype(F32)
        for n in reversed(range(blocks)):
            at = slice(n * GROUP, (n + 1) * GROUP)
            marks_n = marks_ref[at]
            entering = marks_n[:, 1:2]
            allowed = causal & (marks_n[:, 0:1] == doc_ref[:, at])
            run_all = along[at]
            for head, lanes in enumerate(spans()):
                run = run_all[:, lanes]
                end = run[GROUP - 1 :]
                key = k_ref[at, lanes].astype(F32)
                value = v_ref[at, lanes]
                grad = gm_ref[at, lanes]
                up, down = jnp.exp(run), jnp.exp(-run)
                out = jnp.exp(end - run) * marks_n[:, 2:3]
                query_in = (scaled(q_ref[at, lanes]) * up).astype(BF16)
                key_in = (key * down).astype(BF16)
                key_out = (key * out).astype(BF16)
                scores = jnp.where(allowed, nt(query_in, key_in), 0.0).astype(BF16)
                grad_scores = jnp.where(allowed, nt(grad, value), 0.0).astype(BF16)
                leaving = state_grad[head].astype(BF16)
                grad_query = nn(grad_scores, key_in) + entering * nn(grad, s_ref[head, n])
                grad_key_in = tn(grad_scores, query_in)
                grad_key_out = nn(value, leaving)
                gv_out[at, lanes] = (tn(scores, grad) + nt(key_out, leaving)).astype(BF16)
                gq_out[at, lanes] = (grad_query * up * HEAD_K ** (-0.5)).astype(BF16)
                gk_out[at, lanes] = (grad_key_in * down + grad_key_out * out).astype(BF16)
                change = (
                    query_in.astype(F32) * grad_query
                    - key_in.astype(F32) * grad_key_in
                    - key_out.astype(F32) * grad_key_out
                )
                closing = jnp.sum(s_ref[head, n + 1].astype(F32) * leaving.astype(F32), axis=0, keepdims=True)
                slope[at, lanes] = summed(onward, change) + closing
                kept = marks_n[GROUP - 1 :, 1:2] * jnp.exp(end)
                state_grad[head] = kept * state_grad[head] + tn(grad, (query_in.astype(F32) * entering).astype(BF16))
        grad_gate = (slope[...] * sigmoid(-gate) * (1.0 / 16.0)).astype(BF16)
        gg_out[...] = grad_gate.T
        part = nn(grad_gate, ro[...])

        @pl.when(h == 0)
        def _():
            low[...] = part

        @pl.when(h > 0)
        def _():
            low[...] += part

        @pl.when(h == steps - 1)
        def _():
            row = lax.broadcasted_iota(jnp.int32, (LANES, LANES), 0)
            lane = lax.broadcasted_iota(jnp.int32, (LANES, LANES), 1)
            move = jnp.where((row == lane + rank) & (lane < rank), 1.0, 0.0).astype(BF16)
            low_out[...] = nn(low[...].astype(BF16), move).astype(BF16)

    return kernel_call(
        body,
        (steps,),
        [
            (queries, by_head(rows)),
            (keys, by_head(rows)),
            (values, by_head(rows)),
            (gate_pre, by_head(rows)),
            (grad_mixed, by_head(rows)),
            (states, spec((TOGETHER, blocks + 1, HEAD_V, HEAD_K), lambda h: (h, 0, 0, 0))),
            (leaving, spec((TOGETHER, HEAD_V, HEAD_K), lambda h: (h, 0, 0))),
            (first, spec((TOGETHER * HEAD_K, LANES), lambda h: (h, 2 * wide // LANES))),
            (marks, spec(marks.shape)),
            (doc_row, spec(doc_row.shape)),
        ],
        [((rows, wide), BF16, by_head(rows))] * 3
        + [
            ((wide, rows), BF16, spec((TOGETHER * HEAD_K, rows), lambda h: (h, 0))),
            ((rows, LANES), BF16, spec((rows, LANES))),
        ],
        [
            pltpu.VMEM((TOGETHER, HEAD_V, HEAD_K), F32),
            pltpu.VMEM((rows, TOGETHER * HEAD_K), F32),
            pltpu.VMEM((rows, LANES), F32),
        ],
    )


def input_back(grads, first, second, grad_rank, tokens, gain, grad_hidden):
    rows, wide = tokens.shape
    steps = wide // HEAD_K // TOGETHER
    places = ((second, 0), (first, 0), (first, steps), (second, steps))

    def body(*refs):
        grad_refs, weight_refs = refs[:4], refs[4:8]
        low_ref, table, x_ref, gain_ref, gh_ref, out_ref, total = refs[8:]
        h = pl.program_id(0)
        part = nt(grad_refs[0][...], weight_refs[0][...])
        for g, w in zip(grad_refs[1:], weight_refs[1:]):
            part = part + nt(g[...], w[...])

        @pl.when(h == 0)
        def _():
            total[...] = part + nt(low_ref[...], table[...])

        @pl.when(h > 0)
        def _():
            total[...] += part

        @pl.when(h == steps - 1)
        def _():
            x = x_ref[...].astype(F32)
            scale = lax.rsqrt(jnp.mean(x * x, axis=1, keepdims=True) + 1e-06)
            unit = x * scale
            grad = total[...] * gain_ref[...]
            out_ref[...] = gh_ref[...] + scale * (grad - unit * jnp.mean(grad * unit, axis=1, keepdims=True))

    whole = spec((rows, wide))
    return kernel_call(
        body,
        (steps,),
        [(g, by_head(rows)) for g in grads]
        + [(w, by_head(wide, start)) for w, start in places]
        + [
            (grad_rank, spec((rows, LANES))),
            (first, spec((wide, LANES), lambda h: (0, 2 * wide // LANES))),
            (tokens, whole),
            (gain, spec((1, wide))),
            (grad_hidden, whole),
        ],
        [((rows, wide), F32, whole)],
        [pltpu.VMEM((rows, wide), F32)],
    )[0]


def finish(terms, weights, turned_in, gain, middle, w_middle, rank, head_rows):
    rows, width = weights[0].shape
    count = len(weights)

    def body(*refs):
        term_refs, weight_refs = refs[: len(terms)], refs[len(terms) : len(terms) + count]
        in_ref, gain_ref, wm_ref = refs[len(terms) + count : len(terms) + count + 3]
        middle_refs = refs[len(terms) + count + 3 : len(terms) + count + 3 + len(middle)]
        outs, middle_outs = refs[len(terms) + count + 3 + len(middle) : -7], refs[-7:-5]
        in_out, out_out, bias_out, head_out, gain_out = refs[-5:]

        def summed_terms(at, term_refs=term_refs):
            total = term_refs[0][:, at].astype(F32)
            for t in term_refs[1:]:
                total = total + t[:, at].astype(F32)
            return total

        for n, out in enumerate(middle_outs):
            out[...] = summed_terms(slice(n * width, (n + 1) * width), middle_refs)
        by_row = jnp.sum(wm_ref[...].astype(F32) * middle_outs[0][...], axis=1, keepdims=True)
        for n, out in enumerate(outs):
            out[...] = summed_terms(slice(n * width, (n + 1) * width))
            by_row = by_row + jnp.sum(weight_refs[n][...].astype(F32) * out[...], axis=1, keepdims=True)
        table = summed_terms(slice(count * width, count * width + LANES))
        lane = lax.broadcasted_iota(jnp.int32, (rows, LANES), 1)
        turned = jnp.where(lane == LANES - 1, by_row, table).T
        in_out[...] = turned[:rank]
        out_out[...] = turned[rank : 2 * rank]
        bias_out[...] = turned[2 * rank : 2 * rank + 1]
        head_out[...] = turned[2 * rank + 3 : 2 * rank + 4, :head_rows]
        by_rank = jnp.sum(in_ref[...].astype(F32) * turned[:rank], axis=0, keepdims=True)
        gain_out[...] = (turned[LANES - 1 :] + by_rank) / gain_ref[...].astype(F32)

    ins = [*terms, *weights, turned_in, gain, w_middle, *middle]
    shapes = [(rows, width)] * (count + 2) + [(rank, rows), (rank, rows), (1, rows), (1, head_rows), (1, rows)]
    return kernel_call(body, (1,), [(a, spec(a.shape)) for a in ins], [(o, F32, spec(o)) for o in shapes])


def then(earlier, later):
    scale = later[:, HEAD_V:].astype(F32)
    state = scale[:, :1] * earlier[:, :HEAD_V].astype(F32) + later[:, :HEAD_V].astype(F32)
    return jnp.concatenate([state, scale * earlier[:, HEAD_V:].astype(F32)], axis=1).astype(BF16)


def nothing(like):
    return jnp.concatenate([jnp.zeros_like(like[:, :HEAD_V]), jnp.ones_like(like[:, HEAD_V:])], axis=1)


class Passing:
    def __init__(self, message, backward=False):
        _, y, x, c = place()
        height = lax.axis_size("y")
        self.core, self.sign = c, -1 if backward else 1
        if backward:
            y, x, c = height - 1 - y, 1 - x, 1 - c
        self.y, self.x, self.c = y, x, c
        heads = message.shape[0]
        self.other = flip(message, "c")
        both = jnp.where(c == 0, then(message, self.other), then(self.other, message))
        self.mine = lax.dynamic_slice_in_dim(both, self.core * (heads // 2), heads // 2, 0)

    def near(self, done=()):
        if square_plane():
            mine = after(done, self.mine)
            self.arrived = (cross(mine, False), cross(mine, True))
        else:
            self.arrived = flip(after(done, self.mine), "x")
        return self.arrived

    def distant(self, done=()):
        if square_plane():
            self.far = cross(after(done, self.arrived[1]), False)
            return self.far
        beside, mine = after(done, self.arrived, self.mine)
        self.before = jnp.where(self.x == 1, beside, nothing(mine))
        self.line = jnp.where(self.x == 1, then(beside, mine), then(mine, beside))
        self.far = [shift(self.line, "y", self.sign * j) for j in range(1, lax.axis_size("y"))]
        return self.far

    def entering(self, done=()):
        if square_plane():
            (early, late), corner = after(done, self.arrived, self.far)
            beside = jnp.where(self.core == 0, early, late)
            along = jnp.where(self.core == 0, late, early)
            line = jnp.where(self.x == 1, then(corner, along), then(along, corner))
            before = jnp.where(self.x == 1, beside, nothing(beside))
            before = jnp.where(self.y == 1, then(line, before), before)
        else:
            before, distant = after(done, self.before, self.far)
            for j, far in enumerate(distant):
                before = jnp.where(self.y > j, then(far, before), before)
        rest = flip(before, "c")
        chip = jnp.where(self.core == 0, jnp.concatenate([before, rest]), jnp.concatenate([rest, before]))
        return jnp.where(self.c == 1, then(chip, self.other), chip)[:, :HEAD_V]


def pair(value):
    return (value, flip(value, "c"))


def document_of(positions, starts):
    return jnp.sum((starts[None, :] <= positions[:, None]).astype(jnp.int32), axis=1) - 1


def documents(starts, rows):
    _, y, x, c = place()
    positions = ((y * 2 + x) * 2 + c) * rows + jnp.arange(rows, dtype=jnp.int32)
    doc = document_of(positions, starts)
    before = document_of(positions - 1, starts)
    blocks = doc.reshape(-1, GROUP)
    entering = (blocks == before.reshape(-1, GROUP)[:, :1]).reshape(-1)
    tail = (blocks == blocks[:, -1:]).reshape(-1)
    columns = [doc, entering, tail, doc == before[0], doc == doc[-1]]
    marks = jnp.stack([a.astype(F32) for a in columns] + [jnp.zeros((rows,), F32)] * 3, axis=1)
    return marks, doc.astype(F32).reshape(1, rows)


def pair(value):
    return (value, flip(value, "c"))


def shards(tokens, cotangent, doc_starts, *weights):
    (
        gain_one, w_query, w_key, w_value, w_swish, rank_in, rank_out, bias, head_gain, w_output, gain_two,
        w_gate, w_up, w_down,
    ) = weights
    rows, width = tokens.shape
    own, rank, ff = w_query.shape[0], rank_in.shape[1], w_gate.shape[1]
    devices = width // own
    _, _, _, c = place()

    table_columns = 2 * width + LANES
    square_weights = jnp.concatenate([w_query, w_swish, w_output], axis=1)

    first = first_weights(w_key, w_value, rank_in.T, rank_out, (bias, gain_one, gain_two, head_gain))
    wait_for = first
    marks, doc_row = documents(doc_starts[0], rows)
    fast = square_plane() and own % 16 == 0
    depth = lax.axis_size("z")

    def by_distance(base, odd, even):
        return jnp.stack([base] + [(odd if k % 2 else even)[(k - 1) // 2] for k in range(1, depth)])

    def odd_shifts(a):
        return [shift(a, "z", k) for k in range(1, depth, 2)]

    def even_shifts(a):
        return [shift(a, "z", k) for k in range(2, depth, 2)]

    if fast:
        half = width // 2
        keep = lax.dynamic_slice_in_dim(w_down, c * half, half, 1)
        other = flip(lax.dynamic_slice_in_dim(w_down, (1 - c) * half, half, 1), "c")
        chip_down = jnp.where(c == 0, jnp.concatenate([keep, other]), jnp.concatenate([other, keep]))
        one = by_distance(first, odd_shifts(first), even_shifts(first))
        square_next = after(one, square_weights)
        one_early, one_late, one_other = cross(one, False), cross(one, True), flip(one, "c")
        two_odd = odd_shifts(square_next)
        now = (one_early, one_late, two_odd, one_other)
        one_next, one_late, square_next = after(now, one_early, one_late, square_weights)
        one_corner = cross(one_next, True)
        two_even = even_shifts(square_next)
        one_others = [one_other, flip(one_next, "c"), flip(one_late, "c")]
        wait_for = now = (one_corner, two_even, one_others)
        one, two, chip_down = after(now, one, by_distance(square_weights, two_odd, two_even), chip_down)
        first = assemble(gathered(one, one_early, one_late, one_corner, one_others), own, (width, table_columns))
        two_early = cross(two, False)
        three_odd = odd_shifts(chip_down)
        first, two, chip_down = after((first, two_early, three_odd), first, two, chip_down)
        two_late = cross(two, True)
        three_even = even_shifts(chip_down)
    else:
        first = lax.all_gather(first, AXES, axis=0, tiled=True)
        second = lax.all_gather(square_weights, AXES, axis=0, tiled=True)
        w_down_all = lax.all_gather(w_down, AXES, axis=0, tiled=True)
    gate_shard, up_shard = after(wait_for, w_gate, w_up)
    w_both = lax.all_gather(jnp.concatenate([gate_shard, up_shard], axis=1), AXES, axis=0, tiled=True)
    normed, normed_turned, low, keys, values, gate_pre, message, vectors = project(tokens, first, marks, rank)
    row_one, row_two = vectors[1:2], vectors[2:3]
    row_head = vectors[3].reshape(devices, own)[:, : head_gain.shape[0]].reshape(1, HEAD_V)
    if fast:
        message, two_early, two_late = after((two_late, three_even), message, two_early, two_late)
    both, down_pair = pair(normed_turned), pair(cotangent)
    passing = Passing(message)
    if fast:
        two_next, two_late = after(passing.mine, two_early, two_late)
        two_corner = cross(two_next, True)
        two_others = [flip(a, "c") for a in (two, two_next, two_late)]
        now = (passing.near(), two_corner, both, down_pair, two_others)
        two_corner = after(now, two_corner)
        two_others.append(flip(two_corner, "c"))
        three = by_distance(chip_down, three_odd, three_even)
        now = (passing.distant(now), two_others, three)
        three, two = after(now, three, two)
        three_early = cross(three, False)
        second = assemble(gathered(two, two_early, two_late, two_corner, two_others), own, (width, 3 * width))
        entered = passing.entering(now)
        now = (entered, second, three_early)
        entered, second, three, three_early = after(now, entered, second, three, three_early)
        three_late, three_corner = cross(three, True), cross(three_early, True)
    else:
        passing.near()
        passing.distant()
        entered = passing.entering()
    queries, mixed, swish, gated, hidden, normed_two, two_turned, states = mixer(
        normed, keys, values, gate_pre, entered, second, row_head, tokens, row_two, marks, doc_row
    )
    if fast:
        hidden, three = after((three_late, three_corner), hidden, three)
        w_down_all = assemble(
            gathered(three, three_early, three_late, three_corner), chip_down.shape[0], (ff, width), True
        )
    two_pair, gated_pair = pair(two_turned), pair(gated)
    output, inner, grad_gate, grad_up, grad_hidden, grad_low = feed(
        normed_two, cotangent, w_both, w_down_all, hidden, row_two
    )

    gate_pair = pair(grad_gate)
    grad_mixed, grad_swish, grad_head_gain, message_back = head_back(
        grad_low, second, mixed, swish, row_head, queries, gate_pre, message[:, HEAD_V:], marks
    )
    gate_pair, inner, grad_up = after((message_back, gate_pair), gate_pair, inner, grad_up)
    gate = weight_grads([(two_pair, [gate_pair])], ff // 2)
    inner_pair, up_pair = pair(inner), pair(grad_up)
    down = weight_grads([(after(gate.blocks, inner_pair), [down_pair])], 512, True, by_z=True)
    down_blocks = down.blocks
    down.zeroth()
    now = (gate.first(), message_back, down_blocks)
    passing = Passing(after(now, message_back), True)
    now = passing.mine
    swish_pair, low_pair = pair(after(now, grad_swish)), pair(after(now, grad_low))
    up = weight_grads([(two_pair, [after(now, up_pair)])], ff // 2)
    middle = weight_grads([(both, [swish_pair]), (gated_pair, [low_pair])], width)
    now = (passing.near(), gate.second(now), up.blocks, middle.blocks)
    now = passing.distant(now)
    leaving = passing.entering(now)
    now = leaving
    grad_query, grad_key, grad_value, grad_gate_pre, grad_rank = mixer_back(
        queries, keys, values, gate_pre, grad_mixed, states, leaving, first, marks, doc_row, rank
    )
    now = (up.first(now), grad_query)
    up.second(now)
    middle.first(now)
    inside_pairs = [pair(a) for a in after(now, grad_query, grad_key, grad_value, grad_rank, grad_gate_pre)]
    head_terms = grad_head_gain + flip(grad_head_gain, "c")
    head_terms = jnp.pad(head_terms.reshape(devices, -1), ((0, 0), (0, own - head_gain.shape[0]))).reshape(width, 1)
    base = jnp.pad(head_terms.astype(BF16), ((0, 0), (2 * rank + 3, LANES - 2 * rank - 4)))
    inside = weight_grads(
        [(both, inside_pairs[:3])],
        width,
        table=([(both, inside_pairs[3]), (inside_pairs[4], pair(low))], base),
    )
    now = (inside.blocks, middle.arrived, up.through)
    gate.through, up.through = after(inside.blocks, gate.through, up.through)
    gates_part = gate.third(up)
    input_grad = input_back(
        (grad_query, grad_key, grad_value, grad_swish), first, second, after(now, grad_rank), tokens, row_one,
        grad_hidden,
    )
    now = (input_grad, inside.first(now), middle.second(now))
    down.first(now)
    middle_terms = middle.third_terms()
    inside.second(now)
    down.second(inside.through)
    inside_terms = inside.third_terms()
    down_part = down.result()

    chip_half = ff // devices
    down_sum = wide(down_part)
    keep = lax.dynamic_slice_in_dim(down_sum, c * chip_half, chip_half, 0)
    other = flip(lax.dynamic_slice_in_dim(down_sum, (1 - c) * chip_half, chip_half, 0), "c")
    down_sum = jnp.where(c == 0, jnp.concatenate([keep, other], 1), jnp.concatenate([other, keep], 1))
    g_gate, g_up = wide(gates_part[:, :ff]), wide(gates_part[:, ff:])
    g_gain_two = (jnp.sum(wide(w_gate) * g_gate, axis=1) + jnp.sum(wide(w_up) * g_up, axis=1)) / wide(gain_two)
    g_query, g_key, g_value, g_swish, g_output, g_rank_in, g_rank_out, g_bias, g_head, g_gain_one = finish(
        inside_terms, (w_query, w_key, w_value), rank_in.T, gain_one.reshape(1, own), middle_terms, w_swish,
        rank, head_gain.shape[0],
    )
    return (
        output, input_grad, g_gain_one[0], g_query, g_key, g_value, g_swish, g_rank_in.T, g_rank_out, g_bias[0], g_head[0],
        g_output, g_gain_two, g_gate, g_up, down_sum,
    )


def solution(mesh):
    fsdp, seq = mesh.shape["fsdp"], mesh.shape["seq"]
    inner = Mesh(mesh.devices.reshape(fsdp, seq // 4, 2, 2), AXES)
    rows, vector, columns = P(AXES, None), P(AXES), P(None, AXES)
    in_specs = (rows, rows, P("z", None), vector, rows, rows, rows, rows, rows, columns, vector, vector, rows, vector) + (rows,) * 3
    out_specs = (rows, rows, vector) + (rows,) * 5 + (columns, vector, vector, rows, vector) + (rows,) * 3
    return jax.shard_map(shards, mesh=inner, in_specs=in_specs, out_specs=out_specs, check_vma=False)
```
